32 devices in a mesh: groups: 2 (over x), space: 16 (over z, y, core).
Axes of the slice: x: 2, y: 2, z: 4, core: 2. Of those that a mesh axis runs over, the one named last changes fastest.
Arguments:
- eigvecs: bfloat16 [4, 2, 3, 16, 128, 256], P('groups', None, None, 'space'), parts along dimension 0, may hold values from -12 to 12
- links: bfloat16 [4, 3, 2, 3, 3, 16, 128], P('groups', None, None, None, None, 'space'), parts along dimension 0, may hold values from -4 to 4
- directions: int32 [4], P('groups'), parts along dimension 0, may hold values from 0 to 2
- pairs: int32 [128, 2], P(('groups', 'space')), parts along dimension 0, may hold values from 0 to 1
- perambulators: bfloat16 [128, 2, 256, 256], P(('groups', 'space')), parts along dimension 0, may hold values from -0.25 to 0.25
Outputs:
- elementals: float32 [4, 2, 2, 256, 256], P('groups', None, None, 'space'), parts along dimension 0
- pair_matrices: bfloat16 [128, 2, 256, 256], P(('groups', 'space')), parts along dimension 0
The draws below stay inside these ranges and needn't reach their ends.
There are 2 independent parts, one for each index of `groups`. The reference program is written for one: setup_inputs(seed, part) draws one part's arguments, and reference() takes and returns one part's arrays. A program takes and returns all parts, laid end to end along the dimension named above; each array names one. Nothing has to cross between parts.
Inputs may be any that keep to these rules, and one draw needn't show every extreme that they name: `directions`: 0 is x, 1 is y, 2 is z. pairs[p, 0] is the source time slice and pairs[p, 1] the sink time slice of pair p.
All inputs are finite; a program needn't handle non-finite values.
Results may differ from the reference program's by a relative error of at most 0.011.
Values may be sent and summed in bfloat16 or wider, within the bound.
No kernel may reach another device: no remote copies, remote signals or barrier semaphores. Data moves between devices by JAX's collectives and lax.ppermute only.
A program may use at most 64 MiB of HBM per device.

```python
import jax
import jax.numpy as jnp
from jax import lax

NVEC = 256
TSL = 2
LX = 16
LY = 8
NZ = 16
PAIRS = 64


def with_ends(values, key, low, largest):
    index_at = [jax.random.randint(jax.random.fold_in(key, axis), (), 0, length) for axis, length in enumerate(values.shape)]
    widest = values.shape.index(max(values.shape))
    beside = index_at[:widest] + [(index_at[widest] + 1) % values.shape[widest]] + index_at[widest + 1:]
    return values.at[tuple(index_at)].set(low).at[tuple(beside)].set(largest)


def level_of(key, shape, pieces, smallest, largest):
    factor_of = 1.0
    for position, parts in pieces:
        heights = jax.random.uniform(jax.random.fold_in(jax.random.fold_in(key, 6), position), (parts,), jnp.float32, smallest / len(pieces), largest / len(pieces))
        factor_of = factor_of * jnp.repeat(jnp.exp(heights), shape[position] // parts).reshape((-1,) + (1,) * (len(shape) - 1 - position))
    return factor_of


def centred(own_key, shape, width, reach, shards=(), kind=jnp.bfloat16):
    array = jax.random.normal(own_key, shape, jnp.float32) * width
    if len(shards) > 0:
        array = level_of(own_key, shape, shards, -0.22, 0.18) * array
    return jnp.clip(array, min=-reach, max=reach).astype(kind)


def setup_inputs(seed: int = 0, part: int = 0) -> dict:
    arg_keys = jax.random.split(jax.random.key(seed), 6)
    own_keys = jax.random.split(jax.random.fold_in(arg_keys[5], part), 6)
    eigvecs = centred(own_keys[0], (TSL, 2, 3, NZ, LX * LY, NVEC), 2.0, 12.0, ((3, 16),))
    links = centred(own_keys[1], (TSL, 3, 2, 3, 3, NZ, LX * LY), 0.577, 4.0, ((5, 16),))
    directions = jax.random.randint(own_keys[2], (2,), 0, 3).astype(jnp.int32)
    pairs = with_ends(jax.random.randint(own_keys[3], (PAIRS, 2), 0, TSL), jax.random.fold_in(own_keys[3], 1), 0, TSL - 1).astype(jnp.int32)
    perambulators = centred(own_keys[4], (PAIRS, 2, NVEC, NVEC), (2 * NVEC) ** -0.5, 0.25, ((0, 16),))
    return {"eigvecs": eigvecs, "links": links, "directions": directions, "pairs": pairs, "perambulators": perambulators}


smear_weight = 0.12
vector_axes = (3, 4, 2)
link_axes = (4, 5, 3)


def forward_hop(gauge_link, vectors):
    real_parts = []
    imag_parts = []
    for out_color in range(3):
        real_sum = jnp.zeros(vectors.shape[2:], jnp.float32)
        imag_sum = jnp.zeros(vectors.shape[2:], jnp.float32)
        for in_color in range(3):
            link_real = gauge_link[0, out_color, in_color][..., None]
            link_imag = gauge_link[1, out_color, in_color][..., None]
            field_real = vectors[0, in_color].astype(jnp.float32)
            field_imag = vectors[1, in_color].astype(jnp.float32)
            real_sum = real_sum + link_real * field_real - link_imag * field_imag
            imag_sum = imag_sum + link_real * field_imag + link_imag * field_real
        real_parts.append(real_sum)
        imag_parts.append(imag_sum)
    return jnp.stack([jnp.stack(real_parts), jnp.stack(imag_parts)])


def backward_hop(gauge_link, vectors):
    real_parts = []
    imag_parts = []
    for out_color in range(3):
        real_sum = jnp.zeros(vectors.shape[2:], jnp.float32)
        imag_sum = jnp.zeros(vectors.shape[2:], jnp.float32)
        for in_color in range(3):
            link_real = gauge_link[0, in_color, out_color][..., None]
            link_imag = gauge_link[1, in_color, out_color][..., None]
            field_real = vectors[0, in_color].astype(jnp.float32)
            field_imag = vectors[1, in_color].astype(jnp.float32)
            real_sum = real_sum + link_real * field_real + link_imag * field_imag
            imag_sum = imag_sum + link_real * field_imag - link_imag * field_real
        real_parts.append(real_sum)
        imag_parts.append(imag_sum)
    return jnp.stack([jnp.stack(real_parts), jnp.stack(imag_parts)])


def inner_product(left_side, right_side):
    return lax.dot_general(left_side, right_side, (((0,), (0,)), ((), ())), preferred_element_type=jnp.float32)


def plain_dot(left_side, right_side):
    return jnp.dot(left_side, right_side, preferred_element_type=jnp.float32)


def complex_product(left_side, right_side):
    real_part = plain_dot(left_side[0], right_side[0]) - plain_dot(left_side[1], right_side[1])
    imag_part = plain_dot(left_side[0], right_side[1]) + plain_dot(left_side[1], right_side[0])
    return jnp.stack([real_part, imag_part])


def adjoint_product(left_side, right_side):
    real_part = plain_dot(left_side[0], right_side[0].T) + plain_dot(left_side[1], right_side[1].T)
    imag_part = plain_dot(left_side[1], right_side[0].T) - plain_dot(left_side[0], right_side[1].T)
    return jnp.stack([real_part, imag_part])


def slice_terms(eigen_slice, link_slice, directions):
    vectors = eigen_slice.reshape(2, 3, NZ, LX, LY, NVEC)
    gauge_field = link_slice.astype(jnp.float32).reshape(3, 2, 3, 3, NZ, LX, LY)
    ahead_links = [gauge_field[direction] for direction in range(3)]
    behind_links = [jnp.roll(gauge_field[direction], 1, link_axes[direction]) for direction in range(3)]

    def laplace_step(current):
        laplace_sum = -6.0 * current.astype(jnp.float32)
        for direction in range(3):
            ahead_field = jnp.roll(current, -1, vector_axes[direction])
            behind = jnp.roll(current, 1, vector_axes[direction])
            laplace_sum = laplace_sum + forward_hop(ahead_links[direction], ahead_field) + backward_hop(behind_links[direction], behind)
        return (current.astype(jnp.float32) + smear_weight * laplace_sum).astype(jnp.bfloat16)

    def displace_along(direction):
        def displaced(smeared):
            ahead_field = jnp.roll(smeared, -1, vector_axes[direction])
            behind = jnp.roll(smeared, 1, vector_axes[direction])
            return (forward_hop(ahead_links[direction], ahead_field) - backward_hop(behind_links[direction], behind)).astype(jnp.bfloat16)
        return displaced

    branches = [displace_along(direction) for direction in range(3)]
    smeared = laplace_step(laplace_step(vectors))
    site_rows = 3 * NZ * LX * LY
    smeared_rows = smeared.reshape(2, site_rows, NVEC)
    blocks = []
    for copy_index in range(2):
        shifted_rows = lax.switch(directions[copy_index], branches, smeared).reshape(2, site_rows, NVEC)
        real_part = inner_product(smeared_rows[0], shifted_rows[0]) + inner_product(smeared_rows[1], shifted_rows[1])
        imag_part = inner_product(smeared_rows[0], shifted_rows[1]) - inner_product(smeared_rows[1], shifted_rows[0])
        blocks.append(jnp.stack([real_part, imag_part]))
    return jnp.stack(blocks)


def reference(eigvecs, links, directions, pairs, perambulators):
    site_scale = (6.0 * NZ * LX * LY) ** -0.5
    pair_scale = (2.0 * NVEC) ** -0.5

    def per_slice(operands):
        return slice_terms(operands[0], operands[1], directions) * site_scale

    elementals = lax.map(per_slice, (eigvecs, links))
    panels = elementals.astype(jnp.bfloat16)

    def per_pair(operands):
        pair_row = operands[0]
        propagator = operands[1]
        left_side = panels[pair_row[1], 0]
        right_side = panels[pair_row[0], 1]
        first_product = complex_product(left_side, propagator).astype(jnp.bfloat16)
        second_product = (complex_product(first_product, right_side) * pair_scale).astype(jnp.bfloat16)
        return adjoint_product(second_product, propagator).astype(jnp.bfloat16)

    pair_matrices = lax.map(per_pair, (pairs, perambulators))
    return elementals, pair_matrices
```

```python
import functools

import jax
import jax.numpy as jnp
from jax import lax
from jax.experimental import pallas as pl
from jax.experimental.pallas import tpu as pltpu
from jax.sharding import PartitionSpec as P

LX = 16
LY = 8
SITES = LX * LY
COLORS = 3
FIELD = COLORS * SITES
LINK_ROWS = 54
PACKED_LINKS = 32
SMEAR = 0.12
VMEM = 56 * 1024 * 1024

bf16 = jnp.bfloat16
f32 = jnp.float32


def position():
    index = lax.axis_index("space")
    return lax.rem(index, 2), lax.rem(lax.div(index, 2), 2)


def whole_in_vmem():
    return pl.BlockSpec(memory_space=pltpu.VMEM)


def link_row(direction, part, row, column):
    return ((direction * 2 + part) * COLORS + row) * COLORS + column


def split_kernel(vectors, links, keep, send):
    core, _ = position()
    half = vectors.shape[5] // 2
    for t in range(vectors.shape[0]):
        for part in range(2):
            for color in range(COLORS):
                rows = pl.ds(color * SITES, SITES)
                lanes = pl.ds(part * half, half)
                block = vectors[t, part, color, 0]
                low, high = block[:, :half], block[:, half:]
                keep[t, rows, lanes] = jnp.where(core == 0, low, high)
                send[t, rows, lanes] = jnp.where(core == 0, high, low)
        gathered = [
            links[t, d, part, row, column].astype(f32)
            for d in range(3)
            for part in range(2)
            for row in range(COLORS)
            for column in range(COLORS)
        ]
        gathered.append(jnp.zeros((2 * PACKED_LINKS - LINK_ROWS, SITES), f32))
        packed = jnp.concatenate(gathered, axis=0).astype(bf16)
        for out in (keep, send):
            out[t, pl.ds(FIELD, PACKED_LINKS), pl.ds(0, SITES)] = packed[:PACKED_LINKS]
            out[t, pl.ds(FIELD, PACKED_LINKS), pl.ds(SITES, SITES)] = packed[PACKED_LINKS:]


def join_kernel(keep, received, own, other):
    core, chip = position()
    own[core] = keep[chip]
    own[1 - core] = received[chip]
    other[core] = keep[1 - chip]
    other[1 - core] = received[1 - chip]


def shift_y(row, lane):
    return jnp.where(
        lax.rem(lane, LY) == 0,
        pltpu.roll(row, SITES - (LY - 1), 1),
        pltpu.roll(row, 1, 1),
    )


def site_masks():
    row = lax.broadcasted_iota(jnp.int32, (SITES, SITES), 0)
    column = lax.broadcasted_iota(jnp.int32, (SITES, SITES), 1)
    y = lax.rem(row, LY)
    ahead_x = column == lax.rem(row + LY, SITES)
    behind_x = column == lax.rem(row + SITES - LY, SITES)
    ahead_y = column == row - y + lax.rem(y + 1, LY)
    behind_y = column == row - y + lax.rem(y + LY - 1, LY)
    return ahead_x, ahead_y, behind_x, behind_y, column == row


def link_planes(packed):
    return jnp.concatenate([packed[:, :SITES], packed[:, SITES:]], axis=0).astype(f32)


def smear_kernel(own, across, first, second, last, w_out, fields, rims, grown, operator, sems):
    _, chip = position()
    own_at, across_at = 2 + 2 * chip, 4 - 2 * chip
    first_at, second_at = 6 * chip, 6 - 6 * chip
    copies = []
    for k, (ref, at) in enumerate(
        ((own, own_at), (across, across_at), (first, first_at), (second, second_at))
    ):
        copies.append(
            pltpu.make_async_copy(
                ref.at[:, pl.ds(0, FIELD)], fields.at[pl.ds(at, 2)], sems.at[2 * k]
            )
        )
        copies.append(
            pltpu.make_async_copy(
                ref.at[:, pl.ds(FIELD, PACKED_LINKS)], rims.at[pl.ds(at, 2)], sems.at[2 * k + 1]
            )
        )
    copies.append(pltpu.make_async_copy(last.at[pl.ds(0, FIELD)], fields.at[8], sems.at[8]))
    copies.append(
        pltpu.make_async_copy(last.at[pl.ds(FIELD, PACKED_LINKS)], rims.at[8], sems.at[9])
    )
    for copy in copies:
        copy.start()
    for copy in copies:
        copy.wait()

    ahead_x, ahead_y, behind_x, behind_y, same = site_masks()

    def build(z, carry):
        table = link_planes(rims[z])
        below = link_planes(rims[z - 1])
        lane = lax.broadcasted_iota(jnp.int32, table.shape, 1)
        from_x = pltpu.roll(table, LY, 1)
        from_y = shift_y(table, lane)

        def row_of(values, *what):
            k = link_row(*what)
            return values[k : k + 1]

        for part in range(2):
            sign = 1.0 if part == 0 else -1.0
            for i in range(COLORS):
                rows = pl.ds((part * COLORS + i) * SITES, SITES)
                for j in range(COLORS):
                    zero = jnp.zeros((SITES, SITES), f32)
                    plane = jnp.where(ahead_x, row_of(from_x, 0, part, i, j), zero)
                    plane = jnp.where(ahead_y, row_of(from_y, 1, part, i, j), plane)
                    plane = jnp.where(behind_x, sign * row_of(table, 0, part, j, i), plane)
                    plane = jnp.where(behind_y, sign * row_of(table, 1, part, j, i), plane)
                    lower = jnp.where(same, sign * row_of(below, 2, part, j, i), zero)
                    upper = jnp.where(same, row_of(table, 2, part, i, j), zero)
                    for k, block in enumerate((lower, plane, upper)):
                        operator[z - 1, rows, pl.ds((k * COLORS + j) * SITES, SITES)] = (
                            block.astype(bf16)
                        )
        return carry

    lax.fori_loop(1, 8, build, 0)
    half = SITES

    def step(source, z, z_operator):
        window = source[pl.ds(z - 1, 3)].reshape(3 * FIELD, 2 * half)
        product = jnp.dot(operator[z_operator], window, preferred_element_type=f32)
        hops = jnp.concatenate(
            [
                product[:FIELD, :half] - product[FIELD:, half:],
                product[:FIELD, half:] + product[FIELD:, :half],
            ],
            axis=1,
        )
        center = source[z].astype(f32)
        return ((1.0 - 6.0 * SMEAR) * center + SMEAR * hops).astype(bf16)

    def smear_first(z, carry):
        grown[z - 1] = step(fields, z, z - 1)
        return carry

    def smear_second(z, carry):
        w_out[z - 1] = step(grown, z, z)
        return carry

    lax.fori_loop(1, 8, smear_first, 0)
    lax.fori_loop(1, 6, smear_second, 0)


def elemental_kernel(scale, directions, mine, theirs, own, across, out, out_low, w, rims, right, sems):
    core, chip = position()
    half = SITES
    planes = mine.shape[0]
    copies = []
    for k, (ref, side) in enumerate(((mine, core), (theirs, 1 - core))):
        for part in range(2):
            copies.append(
                pltpu.make_async_copy(
                    ref.at[:, :, pl.ds(part * half, half)],
                    w.at[:, part, :, pl.ds(pl.multiple_of(side * half, half), half)],
                    sems.at[2 * k + part],
                )
            )
    copies.append(
        pltpu.make_async_copy(
            own.at[:, pl.ds(FIELD, PACKED_LINKS)], rims.at[pl.ds(2 * chip, 2)], sems.at[4]
        )
    )
    copies.append(
        pltpu.make_async_copy(
            across.at[:, pl.ds(FIELD, PACKED_LINKS)], rims.at[pl.ds(2 - 2 * chip, 2)], sems.at[5]
        )
    )
    for copy in copies:
        copy.start()
    for copy in copies:
        copy.wait()
    direction = directions[core]
    ahead_x, ahead_y, _, _, same = site_masks()
    one = jnp.ones((SITES, SITES), f32)
    zero = jnp.zeros((SITES, SITES), f32)
    is_x, is_y, is_z = direction == 0, direction == 1, direction == 2
    mask_x = jnp.where(ahead_x, one, zero)
    mask_y = jnp.where(ahead_y, one, zero)
    mask_z = jnp.where(same, one, zero)
    mask = jnp.where(is_x, mask_x, jnp.where(is_y, mask_y, mask_z))

    def displace(z, carry):
        table = link_planes(rims[z])
        lane = lax.broadcasted_iota(jnp.int32, table.shape, 1)
        count = 2 * COLORS * COLORS
        along_x = pltpu.roll(table, LY, 1)[:count]
        along_y = shift_y(table, lane)[count : 2 * count]
        along_z = table[2 * count : 3 * count]
        chosen = jnp.where(is_x, along_x, jnp.where(is_y, along_y, along_z))
        operator = jnp.concatenate(
            [
                jnp.concatenate(
                    [
                        (mask * chosen[k : k + 1]).astype(bf16)
                        for k in range((part * COLORS + i) * COLORS, (part * COLORS + i + 1) * COLORS)
                    ],
                    axis=1,
                )
                for part in range(2)
                for i in range(COLORS)
            ],
            axis=0,
        )
        source = z + jnp.where(is_z, 1, 0)
        real = jnp.dot(operator, w[source, 0], preferred_element_type=f32)
        imag = jnp.dot(operator, w[source, 1], preferred_element_type=f32)
        hop_real = real[:FIELD] - imag[FIELD:]
        hop_imag = real[FIELD:] + imag[:FIELD]
        total = (hop_real + hop_imag).astype(bf16)
        rest = (hop_imag - hop_real).astype(bf16)
        vectors = 2 * half
        right[z, 0, :, pl.ds(0, vectors)] = total
        right[z, 0, :, pl.ds(vectors, vectors)] = rest
        right[z, 1, :, pl.ds(0, vectors)] = rest
        right[z, 1, :, pl.ds(vectors, vectors)] = -total
        return carry

    lax.fori_loop(0, planes - 1, displace, 0)
    vectors = 2 * half
    depth = (planes - 1) * 2 * FIELD
    product = lax.dot_general(
        w[pl.ds(0, planes - 1)].reshape(depth, vectors),
        right[...].reshape(depth, 2 * vectors),
        (((0,), (0,)), ((), ())),
        preferred_element_type=f32,
    )
    packed = (product[:, :vectors] + product[:, vectors:].T) * scale
    out[...] = packed
    out_low[...] = packed.astype(bf16)


def pair_kernel(pair_scale, pairs, s00, s10, s01, s11, perambulators, elementals, out, parts, left, right):
    core, chip = position()
    index = lax.axis_index("space")
    size = s00.shape[0]
    rows = elementals.shape[3]
    own_rows = pl.ds(pl.multiple_of(index * rows, 8), rows)
    for ref, t, k in (
        (s00, chip, core),
        (s10, 1 - chip, core),
        (s01, chip, 1 - core),
        (s11, 1 - chip, 1 - core),
    ):
        packed = ref[...].astype(f32)
        turned = packed.T
        parts[t, k, 0] = 0.5 * (packed - turned)
        parts[t, k, 1] = 0.5 * (packed + turned)
    for t in range(2):
        for k in range(2):
            for part in range(2):
                elementals[t, k, part] = parts[t, k, part, own_rows]
        real, imag = parts[t, 0, 0].astype(bf16), parts[t, 0, 1].astype(bf16)
        left[t, :size, :size] = real
        left[t, :size, size:] = -imag
        left[t, size:, :size] = imag
        left[t, size:, size:] = real
        real, imag = parts[t, 1, 0].astype(bf16), parts[t, 1, 1].astype(bf16)
        right[t, :size, :size] = real
        right[t, :size, size:] = imag
        right[t, size:, :size] = -imag
        right[t, size:, size:] = real

    def contract(p, carry):
        source, sink = pairs[p, 0], pairs[p, 1]
        propagator = perambulators[p].reshape(2 * size, size)
        first = jnp.dot(left[sink], propagator, preferred_element_type=f32).astype(bf16)
        wide = jnp.concatenate([first[:size], first[size:]], axis=1)
        second = (
            jnp.dot(wide, right[source], preferred_element_type=f32) * pair_scale
        ).astype(bf16)
        real, imag = second[:, :size], second[:, size:]
        both = jnp.concatenate(
            [second, jnp.concatenate([imag, -real], axis=1)], axis=0
        )
        turned = jnp.concatenate([propagator[:size], propagator[size:]], axis=1)
        third = lax.dot_general(
            both, turned, (((1,), (1,)), ((), ())), preferred_element_type=f32
        ).astype(bf16)
        out[p] = third.reshape(2, size, size)
        return carry

    lax.fori_loop(0, perambulators.shape[0], contract, 0)


def params():
    return pltpu.CompilerParams(vmem_limit_bytes=VMEM)


def body(eigvecs, links, directions, pairs, perambulators):
    slices = eigvecs.shape[0]
    vector_count = eigvecs.shape[5]
    n = lax.axis_size("space")
    blocks = n // 4
    vmem = whole_in_vmem()
    anywhere = pl.BlockSpec(memory_space=pl.ANY)
    smem = pl.BlockSpec(memory_space=pltpu.SMEM)
    rows = FIELD + PACKED_LINKS

    def swap(value, bit):
        return lax.ppermute(value, "space", [(i, i ^ bit) for i in range(n)])

    package = jax.ShapeDtypeStruct((slices, rows, vector_count), bf16)
    keep, send = pl.pallas_call(
        split_kernel,
        out_shape=(package, package),
        in_specs=[vmem, vmem],
        out_specs=(vmem, vmem),
        compiler_params=params(),
    )(eigvecs, links)
    received = swap(send, 1)
    own, other = pl.pallas_call(
        join_kernel,
        out_shape=(package, package),
        in_specs=[vmem, vmem],
        out_specs=(vmem, vmem),
        compiler_params=params(),
    )(keep, received)

    crossing, straight, down = [], [], []
    for q in range(blocks):
        above, below = (q + 1) % blocks, (q + blocks - 1) % blocks
        for core in range(2):
            a, b = 4 * q + core, 4 * q + 2 + core
            crossing += [(b, 4 * above + core), (a, 4 * below + 2 + core)]
            straight += [(b, 4 * above + 2 + core), (a, 4 * below + core)]
            down += [(a, 4 * below + core), (b, 4 * below + 2 + core)]
    across = swap(other, 2)
    second = lax.ppermute(own, "space", straight)
    first = lax.ppermute(other, "space", crossing)
    _, chip = position()
    third_plane = jnp.where(chip == 0, across[0], own[0])
    last = lax.ppermute(third_plane, "space", down)

    w_shape = jax.ShapeDtypeStruct((5, FIELD, vector_count), bf16)
    mine = pl.pallas_call(
        smear_kernel,
        out_shape=w_shape,
        in_specs=[anywhere] * 5,
        out_specs=vmem,
        scratch_shapes=[
            pltpu.VMEM((9, FIELD, vector_count), bf16),
            pltpu.VMEM((9, PACKED_LINKS, 2 * SITES), bf16),
            pltpu.VMEM((7, FIELD, vector_count), bf16),
            pltpu.VMEM((7, 2 * FIELD, 3 * FIELD), bf16),
            pltpu.SemaphoreType.DMA((10,)),
        ],
        compiler_params=params(),
    )(own, across, first, second, last)
    theirs = swap(mine, 1)
    site_scale = (6.0 * n * SITES) ** (-0.5)
    square = (vector_count, vector_count)
    partial, partial_low = pl.pallas_call(
        functools.partial(elemental_kernel, site_scale),
        out_shape=(jax.ShapeDtypeStruct(square, f32), jax.ShapeDtypeStruct(square, bf16)),
        in_specs=[smem] + [anywhere] * 4,
        out_specs=(vmem, vmem),
        scratch_shapes=[
            pltpu.VMEM((5, 2, FIELD, vector_count), bf16),
            pltpu.VMEM((4, PACKED_LINKS, 2 * SITES), bf16),
            pltpu.VMEM((4, 2, FIELD, 2 * vector_count), bf16),
            pltpu.SemaphoreType.DMA((6,)),
        ],
        compiler_params=params(),
    )(directions, mine, theirs, own, across)

    bit = 4
    while bit < n:
        partial = partial + swap(partial_low, bit).astype(f32)
        partial_low = partial.astype(bf16)
        bit *= 2
    other_slice = swap(partial_low, 2)
    other_copy = swap(partial_low, 1)
    other_both = swap(other_slice, 1)

    pair_scale = (2.0 * vector_count) ** (-0.5)
    owned_rows = vector_count // n
    big = 2 * vector_count
    return pl.pallas_call(
        functools.partial(pair_kernel, pair_scale),
        out_shape=(
            jax.ShapeDtypeStruct((slices, 2, 2, owned_rows, vector_count), f32),
            jax.ShapeDtypeStruct(perambulators.shape, bf16),
        ),
        in_specs=[smem] + [vmem] * 5,
        out_specs=(vmem, vmem),
        scratch_shapes=[
            pltpu.VMEM((slices, 2, 2, vector_count, vector_count), f32),
            pltpu.VMEM((slices, big, big), bf16),
            pltpu.VMEM((slices, big, big), bf16),
        ],
        compiler_params=params(),
    )(pairs, partial_low, other_slice, other_copy, other_both, perambulators)


def solution(mesh):
    placed = (
        P("groups", None, None, "space", None, None),
        P("groups", None, None, None, None, "space", None),
        P("groups"),
        P(("groups", "space"), None),
        P(("groups", "space"), None, None, None),
    )
    return jax.shard_map(
        body,
        mesh=mesh,
        in_specs=placed,
        out_specs=(
            P("groups", None, None, "space", None),
            P(("groups", "space"), None, None, None),
        ),
        check_vma=False,
    )
```

```python
import functools

import jax
import jax.numpy as jnp
from jax import lax
from jax.experimental import pallas as pl
from jax.experimental.pallas import tpu as pltpu
from jax.sharding import PartitionSpec as P

LX = 16
LY = 8
SITES = LX * LY
COLORS = 3
FIELD = COLORS * SITES
LINK_ROWS = 54
PACKED_LINKS = 32
SMEAR = 0.12

bf16 = jnp.bfloat16
f32 = jnp.float32


def position():
    index = lax.axis_index("space")
    return lax.rem(index, 2), lax.rem(lax.div(index, 2), 2)


def whole_in_vmem():
    return pl.BlockSpec(memory_space=pltpu.VMEM)


def link_row(direction, part, row, column):
    return ((direction * COLORS + row) * COLORS + column) * 2 + part


def split_kernel(vectors, links, own, other, send, packed, sems):
    core, chip = position()
    half = vectors.shape[5] // 2
    copies = []
    for t in range(2):
        for part in range(2):
            for color in range(COLORS):
                rows = pl.ds(color * SITES, SITES)
                lanes = pl.ds(part * half, half)
                near = pl.ds(pl.multiple_of(core * half, half), half)
                far = pl.ds(pl.multiple_of((1 - core) * half, half), half)
                block = vectors.at[chip + t * (1 - 2 * chip), part, color, 0]
                kept = (own, other)[t]
                for source, target in (
                    (block.at[:, near], kept.at[core, rows, lanes]),
                    (block.at[:, far], send.at[t, rows, lanes]),
                ):
                    copies.append(pltpu.make_async_copy(source, target, sems.at[len(copies)]))
                    copies[-1].start()
    for t in range(2):
        table = links.at[chip + t * (1 - 2 * chip)]
        gathered = [
            table[d, row, column, 0].astype(f32)
            for d in range(3)
            for row in range(COLORS)
            for column in range(COLORS)
        ]
        gathered.append(jnp.zeros((2 * PACKED_LINKS - LINK_ROWS, SITES), f32))
        rows = jnp.concatenate(gathered, axis=0).astype(bf16)
        packed[t, :, pl.ds(0, SITES)] = rows[:PACKED_LINKS]
        packed[t, :, pl.ds(SITES, SITES)] = rows[PACKED_LINKS:]
        for target in ((own, other)[t].at[core], send.at[t]):
            copies.append(
                pltpu.make_async_copy(
                    packed.at[t], target.at[pl.ds(FIELD, PACKED_LINKS)], sems.at[len(copies)]
                )
            )
            copies[-1].start()
    for copy in copies:
        copy.wait()


def join_kernel(received, own_in, other_in, own, other, edge, sems):
    core, chip = position()
    copies = [
        pltpu.make_async_copy(received.at[t], kept.at[1 - core], sems.at[t])
        for t, kept in enumerate((own, other))
    ]
    for copy in copies:
        copy.start()
    for copy in copies:
        copy.wait()
    copy = pltpu.make_async_copy(own.at[1 - chip], edge, sems.at[2])
    copy.start()
    copy.wait()


def shift_y(row, lane):
    return jnp.where(
        lax.rem(lane, LY) == 0,
        pltpu.roll(row, SITES - (LY - 1), 1),
        pltpu.roll(row, 1, 1),
    )


def site_masks():
    row = lax.broadcasted_iota(jnp.int32, (SITES, SITES), 0)
    column = lax.broadcasted_iota(jnp.int32, (SITES, SITES), 1)
    y = lax.rem(row, LY)
    ahead_x = column == lax.rem(row + LY, SITES)
    behind_x = column == lax.rem(row + SITES - LY, SITES)
    ahead_y = column == row - y + lax.rem(y + 1, LY)
    behind_y = column == row - y + lax.rem(y + LY - 1, LY)
    return ahead_x, ahead_y, behind_x, behind_y, column == row


def link_planes(packed):
    return jnp.concatenate([packed[:, :SITES], packed[:, SITES:]], axis=0).astype(f32)


def smear_kernel(own, across, first, second, last, w_out, rims_out, fields, rims, grown, operator, sems):
    _, chip = position()
    own_at, across_at = 3 + chip, 5 - 3 * chip
    first_at, second_at, last_at = 1 + 5 * chip, 7 - 7 * chip, 8 * chip
    copies = []
    for k, (ref, at) in enumerate(
        ((own, own_at), (across, across_at), (first, first_at), (second, second_at))
    ):
        copies.append(
            pltpu.make_async_copy(
                ref.at[:, pl.ds(0, FIELD)], fields.at[pl.ds(at, 2)], sems.at[2 * k]
            )
        )
        copies.append(
            pltpu.make_async_copy(
                ref.at[:, pl.ds(FIELD, PACKED_LINKS)], rims.at[pl.ds(at, 2)], sems.at[2 * k + 1]
            )
        )
    copies.append(pltpu.make_async_copy(last.at[pl.ds(0, FIELD)], fields.at[last_at], sems.at[8]))
    copies.append(
        pltpu.make_async_copy(last.at[pl.ds(FIELD, PACKED_LINKS)], rims.at[last_at], sems.at[9])
    )
    for copy in copies:
        copy.start()
    for copy in copies:
        copy.wait()

    rims_out[...] = rims[2:6]
    ahead_x, ahead_y, behind_x, behind_y, same = site_masks()

    def build(z, carry):
        table = link_planes(rims[z])
        below = link_planes(rims[z - 1])
        lane = lax.broadcasted_iota(jnp.int32, table.shape, 1)
        from_x = pltpu.roll(table, LY, 1)
        from_y = shift_y(table, lane)

        def row_of(values, *what):
            k = link_row(*what)
            return values[k : k + 1]

        for part in range(2):
            sign = 1.0 if part == 0 else -1.0
            for i in range(COLORS):
                rows = pl.ds((part * COLORS + i) * SITES, SITES)
                for j in range(COLORS):
                    zero = jnp.zeros((SITES, SITES), f32)
                    plane = jnp.where(ahead_x, row_of(from_x, 0, part, i, j), zero)
                    plane = jnp.where(ahead_y, row_of(from_y, 1, part, i, j), plane)
                    plane = jnp.where(behind_x, sign * row_of(table, 0, part, j, i), plane)
                    plane = jnp.where(behind_y, sign * row_of(table, 1, part, j, i), plane)
                    lower = jnp.where(same, sign * row_of(below, 2, part, j, i), zero)
                    upper = jnp.where(same, row_of(table, 2, part, i, j), zero)
                    for k, block in enumerate((lower, plane, upper)):
                        operator[z - 1, rows, pl.ds((k * COLORS + j) * SITES, SITES)] = (
                            block.astype(bf16)
                        )
        return carry

    lax.fori_loop(1, 8, build, 0)
    half = SITES

    def step(source, z, z_operator):
        window = source[pl.ds(z - 1, 3)].reshape(3 * FIELD, 2 * half)
        product = jnp.dot(operator[z_operator], window, preferred_element_type=f32)
        hops = jnp.concatenate(
            [
                product[:FIELD, :half] - product[FIELD:, half:],
                product[:FIELD, half:] + product[FIELD:, :half],
            ],
            axis=1,
        )
        center = source[z].astype(f32)
        return ((1.0 - 6.0 * SMEAR) * center + SMEAR * hops).astype(bf16)

    def smear_first(z, carry):
        grown[z - 1] = step(fields, z, z - 1)
        return carry

    def smear_second(z, carry):
        w_out[z - 1] = step(grown, z, z)
        return carry

    lax.fori_loop(1, 8, smear_first, 0)
    lax.fori_loop(1, 6, smear_second, 0)


def elemental_kernel(scale, directions, mine, theirs, rims, out, out_low, w, right, sems):
    core, _ = position()
    half = SITES
    planes = mine.shape[0]
    copies = []
    for k, (ref, side) in enumerate(((mine, core), (theirs, 1 - core))):
        for part in range(2):
            copies.append(
                pltpu.make_async_copy(
                    ref.at[:, :, pl.ds(part * half, half)],
                    w.at[:, part, :, pl.ds(pl.multiple_of(side * half, half), half)],
                    sems.at[2 * k + part],
                )
            )
    for copy in copies:
        copy.start()
    for copy in copies:
        copy.wait()
    direction = directions[core]
    ahead_x, ahead_y, _, _, same = site_masks()
    one = jnp.ones((SITES, SITES), f32)
    zero = jnp.zeros((SITES, SITES), f32)
    is_x, is_y, is_z = direction == 0, direction == 1, direction == 2
    mask_x = jnp.where(ahead_x, one, zero)
    mask_y = jnp.where(ahead_y, one, zero)
    mask_z = jnp.where(same, one, zero)
    mask = jnp.where(is_x, mask_x, jnp.where(is_y, mask_y, mask_z))

    def displace(z, carry):
        table = link_planes(rims[z])
        lane = lax.broadcasted_iota(jnp.int32, table.shape, 1)
        count = 2 * COLORS * COLORS
        along_x = pltpu.roll(table, LY, 1)[:count]
        along_y = shift_y(table, lane)[count : 2 * count]
        along_z = table[2 * count : 3 * count]
        chosen = jnp.where(is_x, along_x, jnp.where(is_y, along_y, along_z))
        operator = jnp.concatenate(
            [
                jnp.concatenate(
                    [
                        (mask * chosen[k : k + 1]).astype(bf16)
                        for k in range(2 * COLORS * i + part, 2 * COLORS * (i + 1), 2)
                    ],
                    axis=1,
                )
                for part in range(2)
                for i in range(COLORS)
            ],
            axis=0,
        )
        source = z + jnp.where(is_z, 1, 0)
        real = jnp.dot(operator, w[source, 0], preferred_element_type=f32)
        imag = jnp.dot(operator, w[source, 1], preferred_element_type=f32)
        hop_real = real[:FIELD] - imag[FIELD:]
        hop_imag = real[FIELD:] + imag[:FIELD]
        total = (hop_real + hop_imag).astype(bf16)
        rest = (hop_imag - hop_real).astype(bf16)
        vectors = 2 * half
        right[z, 0, :, pl.ds(0, vectors)] = total
        right[z, 0, :, pl.ds(vectors, vectors)] = rest
        right[z, 1, :, pl.ds(0, vectors)] = rest
        right[z, 1, :, pl.ds(vectors, vectors)] = -total
        return carry

    lax.fori_loop(0, planes - 1, displace, 0)
    vectors = 2 * half
    depth = (planes - 1) * 2 * FIELD
    product = lax.dot_general(
        w[pl.ds(0, planes - 1)].reshape(depth, vectors),
        right[...].reshape(depth, 2 * vectors),
        (((0,), (0,)), ((), ())),
        preferred_element_type=f32,
    )
    packed = (product[:, :vectors] + product[:, vectors:].T) * scale
    out[...] = packed
    out_low[...] = packed.astype(bf16)


def pair_kernel(pair_scale, pairs, s00, s10, s01, s11, perambulators, elementals, out, parts, left, right):
    core, chip = position()
    index = lax.axis_index("space")
    size = s00.shape[0]
    rows = elementals.shape[3]
    own_rows = pl.ds(pl.multiple_of(index * rows, 8), rows)
    for ref, t, k in (
        (s00, chip, core),
        (s10, 1 - chip, core),
        (s01, chip, 1 - core),
        (s11, 1 - chip, 1 - core),
    ):
        packed = ref[...].astype(f32)
        turned = packed.T
        parts[t, k, 0] = 0.5 * (packed - turned)
        parts[t, k, 1] = 0.5 * (packed + turned)
    for t in range(2):
        for k in range(2):
            for part in range(2):
                elementals[t, k, part] = parts[t, k, part, own_rows]
        real, imag = parts[t, 0, 0].astype(bf16), parts[t, 0, 1].astype(bf16)
        left[t, :size, :size] = real
        left[t, :size, size:] = -imag
        left[t, size:, :size] = imag
        left[t, size:, size:] = real
        real, imag = parts[t, 1, 0].astype(bf16), parts[t, 1, 1].astype(bf16)
        right[t, :size, :size] = real
        right[t, :size, size:] = imag
        right[t, size:, :size] = -imag
        right[t, size:, size:] = real

    def contract(p, carry):
        source, sink = pairs[0, p], pairs[1, p]
        propagator = perambulators[p].reshape(2 * size, size)
        first = jnp.dot(left[sink], propagator, preferred_element_type=f32).astype(bf16)
        wide = jnp.concatenate([first[:size], first[size:]], axis=1)
        second = (
            jnp.dot(wide, right[source], preferred_element_type=f32) * pair_scale
        ).astype(bf16)
        real, imag = second[:, :size], second[:, size:]
        both = jnp.concatenate(
            [second, jnp.concatenate([imag, -real], axis=1)], axis=0
        )
        turned = jnp.concatenate([propagator[:size], propagator[size:]], axis=1)
        third = lax.dot_general(
            both, turned, (((1,), (1,)), ((), ())), preferred_element_type=f32
        ).astype(bf16)
        out[p] = third.reshape(2, size, size)
        return carry

    lax.fori_loop(0, perambulators.shape[0], contract, 0)


def params(megabytes):
    return pltpu.CompilerParams(vmem_limit_bytes=megabytes * 1024 * 1024)


def body(eigvecs, links, directions, pairs, perambulators):
    slices = eigvecs.shape[0]
    vector_count = eigvecs.shape[5]
    n = lax.axis_size("space")
    blocks = n // 4
    vmem = whole_in_vmem()
    anywhere = pl.BlockSpec(memory_space=pl.ANY)
    smem = pl.BlockSpec(memory_space=pltpu.SMEM)
    rows = FIELD + PACKED_LINKS

    def swap(value, bit):
        return lax.ppermute(value, "space", [(i, i ^ bit) for i in range(n)])

    package = jax.ShapeDtypeStruct((2, rows, vector_count), bf16)
    own, other, send = pl.pallas_call(
        split_kernel,
        out_shape=(package, package, package),
        in_specs=[anywhere, vmem],
        out_specs=(anywhere, anywhere, anywhere),
        scratch_shapes=[
            pltpu.VMEM((2, PACKED_LINKS, 2 * SITES), bf16),
            pltpu.SemaphoreType.DMA((28,)),
        ],
        compiler_params=params(8),
    )(eigvecs, jnp.transpose(links, (0, 1, 3, 4, 5, 2, 6)))
    received = swap(send, 1)
    own, other, edge = pl.pallas_call(
        join_kernel,
        out_shape=(package, package, jax.ShapeDtypeStruct((rows, vector_count), bf16)),
        in_specs=[anywhere] * 3,
        out_specs=(anywhere, anywhere, anywhere),
        scratch_shapes=[pltpu.SemaphoreType.DMA((3,))],
        input_output_aliases={1: 0, 2: 1},
        compiler_params=params(8),
    )(received, own, other)

    crossing, straight, outer = [], [], []
    for q in range(blocks):
        above, below = (q + 1) % blocks, (q + blocks - 1) % blocks
        for core in range(2):
            a, b = 4 * q + core, 4 * q + 2 + core
            crossing += [(b, 4 * above + core), (a, 4 * below + 2 + core)]
            straight += [(b, 4 * above + 2 + core), (a, 4 * below + core)]
            outer += [(a, 4 * above + core), (b, 4 * below + 2 + core)]
    across = swap(other, 2)
    second = lax.ppermute(own, "space", straight)
    first = lax.ppermute(other, "space", crossing)
    last = lax.ppermute(edge, "space", outer)

    w_shape = jax.ShapeDtypeStruct((5, FIELD, vector_count), bf16)
    rims_shape = jax.ShapeDtypeStruct((4, PACKED_LINKS, 2 * SITES), bf16)
    mine, rims = pl.pallas_call(
        smear_kernel,
        out_shape=(w_shape, rims_shape),
        in_specs=[anywhere] * 5,
        out_specs=(vmem, vmem),
        scratch_shapes=[
            pltpu.VMEM((9, FIELD, vector_count), bf16),
            pltpu.VMEM((9, PACKED_LINKS, 2 * SITES), bf16),
            pltpu.VMEM((7, FIELD, vector_count), bf16),
            pltpu.VMEM((7, 2 * FIELD, 3 * FIELD), bf16),
            pltpu.SemaphoreType.DMA((10,)),
        ],
        compiler_params=params(24),
    )(own, across, first, second, last)
    theirs = swap(mine, 1)
    site_scale = (6.0 * n * SITES) ** (-0.5)
    square = (vector_count, vector_count)
    partial, partial_low = pl.pallas_call(
        functools.partial(elemental_kernel, site_scale),
        out_shape=(jax.ShapeDtypeStruct(square, f32), jax.ShapeDtypeStruct(square, bf16)),
        in_specs=[smem, anywhere, anywhere, vmem],
        out_specs=(vmem, vmem),
        scratch_shapes=[
            pltpu.VMEM((5, 2, FIELD, vector_count), bf16),
            pltpu.VMEM((4, 2, FIELD, 2 * vector_count), bf16),
            pltpu.SemaphoreType.DMA((4,)),
        ],
        compiler_params=params(16),
    )(directions, mine, theirs, rims)

    bit = 4
    while bit < n:
        partial = partial + swap(partial_low, bit).astype(f32)
        partial_low = partial.astype(bf16)
        bit *= 2
    other_slice = swap(partial_low, 2)
    other_copy = swap(partial_low, 1)
    other_both = swap(other_slice, 1)

    pair_scale = (2.0 * vector_count) ** (-0.5)
    owned_rows = vector_count // n
    big = 2 * vector_count
    return pl.pallas_call(
        functools.partial(pair_kernel, pair_scale),
        out_shape=(
            jax.ShapeDtypeStruct((slices, 2, 2, owned_rows, vector_count), f32),
            jax.ShapeDtypeStruct(perambulators.shape, bf16),
        ),
        in_specs=[smem] + [vmem] * 5,
        out_specs=(vmem, vmem),
        scratch_shapes=[
            pltpu.VMEM((slices, 2, 2, vector_count, vector_count), f32),
            pltpu.VMEM((slices, big, big), bf16),
            pltpu.VMEM((slices, big, big), bf16),
        ],
        compiler_params=params(16),
    )(pairs.T, partial_low, other_slice, other_copy, other_both, perambulators)


def solution(mesh):
    placed = (
        P("groups", None, None, "space", None, None),
        P("groups", None, None, None, None, "space", None),
        P("groups"),
        P(("groups", "space"), None),
        P(("groups", "space"), None, None, None),
    )
    return jax.shard_map(
        body,
        mesh=mesh,
        in_specs=placed,
        out_specs=(
            P("groups", None, None, "space", None),
            P(("groups", "space"), None, None, None),
        ),
        check_vma=False,
    )
```

```python
import functools

import jax
import jax.numpy as jnp
from jax import lax
from jax.experimental import pallas as pl
from jax.experimental.pallas import tpu as pltpu
from jax.sharding import PartitionSpec as P

LX = 16
LY = 8
SITES = LX * LY
COLORS = 3
FIELD = COLORS * SITES
LINK_ROWS = 54
PACKED_LINKS = 32
SMEAR = 0.12

bf16 = jnp.bfloat16
f32 = jnp.float32


def position():
    index = lax.axis_index("space")
    return lax.rem(index, 2), lax.rem(lax.div(index, 2), 2)


def whole_in_vmem():
    return pl.BlockSpec(memory_space=pltpu.VMEM)


def link_row(direction, part, row, column):
    return ((direction * COLORS + row) * COLORS + column) * 2 + part


def split_kernel(vectors, links, own, other, send, packed, sems):
    core, chip = position()
    half = vectors.shape[5] // 2
    copies = []
    for t in range(2):
        for part in range(2):
            for color in range(COLORS):
                rows = pl.ds(color * SITES, SITES)
                lanes = pl.ds(part * half, half)
                near = pl.ds(pl.multiple_of(core * half, half), half)
                far = pl.ds(pl.multiple_of((1 - core) * half, half), half)
                block = vectors.at[chip + t * (1 - 2 * chip), part, color, 0]
                kept = (own, other)[t]
                for source, target in (
                    (block.at[:, near], kept.at[core, rows, lanes]),
                    (block.at[:, far], send.at[t, rows, lanes]),
                ):
                    copies.append(pltpu.make_async_copy(source, target, sems.at[len(copies)]))
                    copies[-1].start()
    for t in range(2):
        table = links.at[chip + t * (1 - 2 * chip)]
        gathered = [
            table[d, row, column, 0].astype(f32)
            for d in range(3)
            for row in range(COLORS)
            for column in range(COLORS)
        ]
        gathered.append(jnp.zeros((2 * PACKED_LINKS - LINK_ROWS, SITES), f32))
        rows = jnp.concatenate(gathered, axis=0).astype(bf16)
        packed[t, :, pl.ds(0, SITES)] = rows[:PACKED_LINKS]
        packed[t, :, pl.ds(SITES, SITES)] = rows[PACKED_LINKS:]
        for target in ((own, other)[t].at[core], send.at[t]):
            copies.append(
                pltpu.make_async_copy(
                    packed.at[t], target.at[pl.ds(FIELD, PACKED_LINKS)], sems.at[len(copies)]
                )
            )
            copies[-1].start()
    for copy in copies:
        copy.wait()


def join_kernel(received, own_in, other_in, own, other, edge, sems):
    core, chip = position()
    copies = [
        pltpu.make_async_copy(received.at[t], kept.at[1 - core], sems.at[t])
        for t, kept in enumerate((own, other))
    ]
    for copy in copies:
        copy.start()
    for copy in copies:
        copy.wait()
    copy = pltpu.make_async_copy(own.at[1 - chip], edge, sems.at[2])
    copy.start()
    copy.wait()


def shift_y(row, lane):
    return jnp.where(
        lax.rem(lane, LY) == 0,
        pltpu.roll(row, SITES - (LY - 1), 1),
        pltpu.roll(row, 1, 1),
    )


def site_masks():
    row = lax.broadcasted_iota(jnp.int32, (SITES, SITES), 0)
    column = lax.broadcasted_iota(jnp.int32, (SITES, SITES), 1)
    y = lax.rem(row, LY)
    ahead_x = column == lax.rem(row + LY, SITES)
    behind_x = column == lax.rem(row + SITES - LY, SITES)
    ahead_y = column == row - y + lax.rem(y + 1, LY)
    behind_y = column == row - y + lax.rem(y + LY - 1, LY)
    return ahead_x, ahead_y, behind_x, behind_y, column == row


def link_planes(packed):
    return jnp.concatenate([packed[:, :SITES], packed[:, SITES:]], axis=0).astype(f32)


def smear_kernel(own, across, first, second, last, w_out, rims_out, fields, rims, grown, operator, sems):
    _, chip = position()
    own_at, across_at = 3 + chip, 5 - 3 * chip
    first_at, second_at, last_at = 1 + 5 * chip, 7 - 7 * chip, 8 * chip
    copies = []
    for k, (ref, at) in enumerate(
        ((own, own_at), (across, across_at), (first, first_at), (second, second_at))
    ):
        copies.append(
            pltpu.make_async_copy(
                ref.at[:, pl.ds(0, FIELD)], fields.at[pl.ds(at, 2)], sems.at[2 * k]
            )
        )
        copies.append(
            pltpu.make_async_copy(
                ref.at[:, pl.ds(FIELD, PACKED_LINKS)], rims.at[pl.ds(at, 2)], sems.at[2 * k + 1]
            )
        )
    copies.append(pltpu.make_async_copy(last.at[pl.ds(0, FIELD)], fields.at[last_at], sems.at[8]))
    copies.append(
        pltpu.make_async_copy(last.at[pl.ds(FIELD, PACKED_LINKS)], rims.at[last_at], sems.at[9])
    )
    for copy in copies:
        copy.start()
    for copy in copies:
        copy.wait()

    rims_out[...] = rims[2:6]
    ahead_x, ahead_y, behind_x, behind_y, same = site_masks()

    def build(z):
        table = link_planes(rims[z])
        below = link_planes(rims[z - 1])
        lane = lax.broadcasted_iota(jnp.int32, table.shape, 1)
        from_x = pltpu.roll(table, LY, 1)
        from_y = shift_y(table, lane)

        def row_of(values, *what):
            k = link_row(*what)
            return values[k : k + 1]

        for part in range(2):
            sign = 1.0 if part == 0 else -1.0
            for i in range(COLORS):
                rows = pl.ds((part * COLORS + i) * SITES, SITES)
                for j in range(COLORS):
                    zero = jnp.zeros((SITES, SITES), f32)
                    plane = jnp.where(ahead_x, row_of(from_x, 0, part, i, j), zero)
                    plane = jnp.where(ahead_y, row_of(from_y, 1, part, i, j), plane)
                    plane = jnp.where(behind_x, sign * row_of(table, 0, part, j, i), plane)
                    plane = jnp.where(behind_y, sign * row_of(table, 1, part, j, i), plane)
                    lower = jnp.where(same, sign * row_of(below, 2, part, j, i), zero)
                    upper = jnp.where(same, row_of(table, 2, part, i, j), zero)
                    for k, block in enumerate((lower, plane, upper)):
                        operator[z - 1, rows, pl.ds((k * COLORS + j) * SITES, SITES)] = (
                            block.astype(bf16)
                        )

    for z in range(1, 8):
        build(z)
    half = SITES

    def step(source, z, z_operator):
        window = source[pl.ds(z - 1, 3)].reshape(3 * FIELD, 2 * half)
        product = jnp.dot(operator[z_operator], window, preferred_element_type=f32)
        hops = jnp.concatenate(
            [
                product[:FIELD, :half] - product[FIELD:, half:],
                product[:FIELD, half:] + product[FIELD:, :half],
            ],
            axis=1,
        )
        center = source[z].astype(f32)
        return ((1.0 - 6.0 * SMEAR) * center + SMEAR * hops).astype(bf16)

    for z in range(1, 8):
        grown[z - 1] = step(fields, z, z - 1)
    for z in range(1, 6):
        w_out[z - 1] = step(grown, z, z)


def elemental_kernel(scale, directions, mine, theirs, rims, out, out_low, w, right, sems):
    core, _ = position()
    half = SITES
    planes = mine.shape[0]
    copies = []
    for k, (ref, side) in enumerate(((mine, core), (theirs, 1 - core))):
        for part in range(2):
            copies.append(
                pltpu.make_async_copy(
                    ref.at[:, :, pl.ds(part * half, half)],
                    w.at[:, part, :, pl.ds(pl.multiple_of(side * half, half), half)],
                    sems.at[2 * k + part],
                )
            )
    for copy in copies:
        copy.start()
    for copy in copies:
        copy.wait()
    direction = directions[core]
    ahead_x, ahead_y, _, _, same = site_masks()
    one = jnp.ones((SITES, SITES), f32)
    zero = jnp.zeros((SITES, SITES), f32)
    is_x, is_y, is_z = direction == 0, direction == 1, direction == 2
    mask_x = jnp.where(ahead_x, one, zero)
    mask_y = jnp.where(ahead_y, one, zero)
    mask_z = jnp.where(same, one, zero)
    mask = jnp.where(is_x, mask_x, jnp.where(is_y, mask_y, mask_z))

    for z in range(planes - 1):
        table = link_planes(rims[z])
        lane = lax.broadcasted_iota(jnp.int32, table.shape, 1)
        count = 2 * COLORS * COLORS
        along_x = pltpu.roll(table, LY, 1)[:count]
        along_y = shift_y(table, lane)[count : 2 * count]
        along_z = table[2 * count : 3 * count]
        chosen = jnp.where(is_x, along_x, jnp.where(is_y, along_y, along_z))
        operator = jnp.concatenate(
            [
                jnp.concatenate(
                    [
                        (mask * chosen[k : k + 1]).astype(bf16)
                        for k in range(2 * COLORS * i + part, 2 * COLORS * (i + 1), 2)
                    ],
                    axis=1,
                )
                for part in range(2)
                for i in range(COLORS)
            ],
            axis=0,
        )
        source = z + jnp.where(is_z, 1, 0)
        real = jnp.dot(operator, w[source, 0], preferred_element_type=f32)
        imag = jnp.dot(operator, w[source, 1], preferred_element_type=f32)
        hop_real = real[:FIELD] - imag[FIELD:]
        hop_imag = real[FIELD:] + imag[:FIELD]
        total = (hop_real + hop_imag).astype(bf16)
        rest = (hop_imag - hop_real).astype(bf16)
        vectors = 2 * half
        right[z, 0, :, pl.ds(0, vectors)] = total
        right[z, 0, :, pl.ds(vectors, vectors)] = rest
        right[z, 1, :, pl.ds(0, vectors)] = rest
        right[z, 1, :, pl.ds(vectors, vectors)] = -total
    vectors = 2 * half
    depth = (planes - 1) * 2 * FIELD
    product = lax.dot_general(
        w[pl.ds(0, planes - 1)].reshape(depth, vectors),
        right[...].reshape(depth, 2 * vectors),
        (((0,), (0,)), ((), ())),
        preferred_element_type=f32,
    )
    packed = (product[:, :vectors] + product[:, vectors:].T) * scale
    out[...] = packed
    out_low[...] = packed.astype(bf16)


def pair_kernel(pair_scale, pairs, s00, s10, s01, s11, perambulators, elementals, out, parts, left, right):
    core, chip = position()
    index = lax.axis_index("space")
    size = s00.shape[0]
    rows = elementals.shape[3]
    own_rows = pl.ds(pl.multiple_of(index * rows, 8), rows)
    for ref, t, k in (
        (s00, chip, core),
        (s10, 1 - chip, core),
        (s01, chip, 1 - core),
        (s11, 1 - chip, 1 - core),
    ):
        packed = ref[...].astype(f32)
        turned = packed.T
        parts[t, k, 0] = 0.5 * (packed - turned)
        parts[t, k, 1] = 0.5 * (packed + turned)
    for t in range(2):
        for k in range(2):
            for part in range(2):
                elementals[t, k, part] = parts[t, k, part, own_rows]
        real, imag = parts[t, 0, 0].astype(bf16), parts[t, 0, 1].astype(bf16)
        left[t, :size, :size] = real
        left[t, :size, size:] = -imag
        left[t, size:, :size] = imag
        left[t, size:, size:] = real
        real, imag = parts[t, 1, 0].astype(bf16), parts[t, 1, 1].astype(bf16)
        right[t, :size, :size] = real
        right[t, :size, size:] = imag
        right[t, size:, :size] = -imag
        right[t, size:, size:] = real

    for p in range(perambulators.shape[0]):
        source, sink = pairs[0, p], pairs[1, p]
        propagator = perambulators[p].reshape(2 * size, size)
        first = jnp.dot(left[sink], propagator, preferred_element_type=f32).astype(bf16)
        wide = jnp.concatenate([first[:size], first[size:]], axis=1)
        second = (
            jnp.dot(wide, right[source], preferred_element_type=f32) * pair_scale
        ).astype(bf16)
        real, imag = second[:, :size], second[:, size:]
        both = jnp.concatenate(
            [second, jnp.concatenate([imag, -real], axis=1)], axis=0
        )
        turned = jnp.concatenate([propagator[:size], propagator[size:]], axis=1)
        third = lax.dot_general(
            both, turned, (((1,), (1,)), ((), ())), preferred_element_type=f32
        ).astype(bf16)
        out[p] = third.reshape(2, size, size)


def params(megabytes):
    return pltpu.CompilerParams(vmem_limit_bytes=megabytes * 1024 * 1024)


def body(eigvecs, links, directions, pairs, perambulators):
    slices = eigvecs.shape[0]
    vector_count = eigvecs.shape[5]
    n = lax.axis_size("space")
    blocks = n // 4
    vmem = whole_in_vmem()
    anywhere = pl.BlockSpec(memory_space=pl.ANY)
    smem = pl.BlockSpec(memory_space=pltpu.SMEM)
    rows = FIELD + PACKED_LINKS

    def swap(value, bit):
        return lax.ppermute(value, "space", [(i, i ^ bit) for i in range(n)])

    package = jax.ShapeDtypeStruct((2, rows, vector_count), bf16)
    own, other, send = pl.pallas_call(
        split_kernel,
        out_shape=(package, package, package),
        in_specs=[anywhere, vmem],
        out_specs=(anywhere, anywhere, anywhere),
        scratch_shapes=[
            pltpu.VMEM((2, PACKED_LINKS, 2 * SITES), bf16),
            pltpu.SemaphoreType.DMA((28,)),
        ],
        compiler_params=params(8),
    )(eigvecs, jnp.transpose(links, (0, 1, 3, 4, 5, 2, 6)))
    received = swap(send, 1)
    own, other, edge = pl.pallas_call(
        join_kernel,
        out_shape=(package, package, jax.ShapeDtypeStruct((rows, vector_count), bf16)),
        in_specs=[anywhere] * 3,
        out_specs=(anywhere, anywhere, anywhere),
        scratch_shapes=[pltpu.SemaphoreType.DMA((3,))],
        input_output_aliases={1: 0, 2: 1},
        compiler_params=params(8),
    )(received, own, other)

    crossing, straight, outer = [], [], []
    for q in range(blocks):
        above, below = (q + 1) % blocks, (q + blocks - 1) % blocks
        for core in range(2):
            a, b = 4 * q + core, 4 * q + 2 + core
            crossing += [(b, 4 * above + core), (a, 4 * below + 2 + core)]
            straight += [(b, 4 * above + 2 + core), (a, 4 * below + core)]
            outer += [(a, 4 * above + core), (b, 4 * below + 2 + core)]
    across = swap(other, 2)
    second = lax.ppermute(own, "space", straight)
    first = lax.ppermute(other, "space", crossing)
    last = lax.ppermute(edge, "space", outer)

    w_shape = jax.ShapeDtypeStruct((5, FIELD, vector_count), bf16)
    rims_shape = jax.ShapeDtypeStruct((4, PACKED_LINKS, 2 * SITES), bf16)
    mine, rims = pl.pallas_call(
        smear_kernel,
        out_shape=(w_shape, rims_shape),
        in_specs=[anywhere] * 5,
        out_specs=(vmem, vmem),
        scratch_shapes=[
            pltpu.VMEM((9, FIELD, vector_count), bf16),
            pltpu.VMEM((9, PACKED_LINKS, 2 * SITES), bf16),
            pltpu.VMEM((7, FIELD, vector_count), bf16),
            pltpu.VMEM((7, 2 * FIELD, 3 * FIELD), bf16),
            pltpu.SemaphoreType.DMA((10,)),
        ],
        compiler_params=params(24),
    )(own, across, first, second, last)
    theirs = swap(mine, 1)
    site_scale = (6.0 * n * SITES) ** (-0.5)
    square = (vector_count, vector_count)
    partial, partial_low = pl.pallas_call(
        functools.partial(elemental_kernel, site_scale),
        out_shape=(jax.ShapeDtypeStruct(square, f32), jax.ShapeDtypeStruct(square, bf16)),
        in_specs=[smem, anywhere, anywhere, vmem],
        out_specs=(vmem, vmem),
        scratch_shapes=[
            pltpu.VMEM((5, 2, FIELD, vector_count), bf16),
            pltpu.VMEM((4, 2, FIELD, 2 * vector_count), bf16),
            pltpu.SemaphoreType.DMA((4,)),
        ],
        compiler_params=params(16),
    )(directions, mine, theirs, rims)

    bit = 4
    while bit < n:
        partial = partial + swap(partial_low, bit).astype(f32)
        partial_low = partial.astype(bf16)
        bit *= 2
    other_slice = swap(partial_low, 2)
    other_copy = swap(partial_low, 1)
    other_both = swap(other_slice, 1)

    pair_scale = (2.0 * vector_count) ** (-0.5)
    owned_rows = vector_count // n
    big = 2 * vector_count
    return pl.pallas_call(
        functools.partial(pair_kernel, pair_scale),
        out_shape=(
            jax.ShapeDtypeStruct((slices, 2, 2, owned_rows, vector_count), f32),
            jax.ShapeDtypeStruct(perambulators.shape, bf16),
        ),
        in_specs=[smem] + [vmem] * 5,
        out_specs=(vmem, vmem),
        scratch_shapes=[
            pltpu.VMEM((slices, 2, 2, vector_count, vector_count), f32),
            pltpu.VMEM((slices, big, big), bf16),
            pltpu.VMEM((slices, big, big), bf16),
        ],
        compiler_params=params(16),
    )(pairs.T, partial_low, other_slice, other_copy, other_both, perambulators)


def solution(mesh):
    placed = (
        P("groups", None, None, "space", None, None),
        P("groups", None, None, None, None, "space", None),
        P("groups"),
        P(("groups", "space"), None),
        P(("groups", "space"), None, None, None),
    )
    return jax.shard_map(
        body,
        mesh=mesh,
        in_specs=placed,
        out_specs=(
            P("groups", None, None, "space", None),
            P(("groups", "space"), None, None, None),
        ),
        check_vma=False,
    )
```

```python
import functools

import jax
import jax.numpy as jnp
from jax import lax
from jax.experimental import pallas as pl
from jax.experimental.pallas import tpu as pltpu
from jax.sharding import PartitionSpec as P

LX = 16
LY = 8
SITES = LX * LY
COLORS = 3
FIELD = COLORS * SITES
LINK_ROWS = 54
PACKED_LINKS = 32
SMEAR = 0.12

bf16 = jnp.bfloat16
f32 = jnp.float32


def position():
    index = lax.axis_index("space")
    return lax.rem(index, 2), lax.rem(lax.div(index, 2), 2)


def whole_in_vmem():
    return pl.BlockSpec(memory_space=pltpu.VMEM)


def link_row(direction, part, row, column):
    return ((direction * COLORS + row) * COLORS + column) * 2 + part


def slot_of(core, chip, t):
    return core + (1 - 2 * core) * ((1 - chip) if t == 0 else chip)


def split_kernel(vectors, links, own, other, send, packed, sems):
    core, chip = position()
    half = vectors.shape[5] // 2
    copies = []
    for t in range(2):
        for part in range(2):
            for color in range(COLORS):
                rows = pl.ds(color * SITES, SITES)
                lanes = pl.ds(part * half, half)
                near = pl.ds(pl.multiple_of(core * half, half), half)
                far = pl.ds(pl.multiple_of((1 - core) * half, half), half)
                block = vectors.at[chip + t * (1 - 2 * chip), part, color, 0]
                kept = (own, other)[t]
                for source, target in (
                    (block.at[:, near], kept.at[slot_of(core, chip, t), rows, lanes]),
                    (block.at[:, far], send.at[t, rows, lanes]),
                ):
                    copies.append(pltpu.make_async_copy(source, target, sems.at[len(copies)]))
                    copies[-1].start()
    for t in range(2):
        table = links.at[chip + t * (1 - 2 * chip)]
        gathered = [
            table[d, row, column, 0].astype(f32)
            for d in range(3)
            for row in range(COLORS)
            for column in range(COLORS)
        ]
        gathered.append(jnp.zeros((2 * PACKED_LINKS - LINK_ROWS, SITES), f32))
        rows = jnp.concatenate(gathered, axis=0).astype(bf16)
        packed[t, :, pl.ds(0, SITES)] = rows[:PACKED_LINKS]
        packed[t, :, pl.ds(SITES, SITES)] = rows[PACKED_LINKS:]
        for target in ((own, other)[t].at[slot_of(core, chip, t)], send.at[t]):
            copies.append(
                pltpu.make_async_copy(
                    packed.at[t], target.at[pl.ds(FIELD, PACKED_LINKS)], sems.at[len(copies)]
                )
            )
            copies[-1].start()
    for copy in copies:
        copy.wait()


def join_kernel(received, own_in, other_in, own, other, edge, sems):
    core, chip = position()
    copies = [
        pltpu.make_async_copy(received.at[t], kept.at[1 - slot_of(core, chip, t)], sems.at[t])
        for t, kept in enumerate((own, other))
    ]
    for copy in copies:
        copy.start()
    for copy in copies:
        copy.wait()
    copy = pltpu.make_async_copy(own.at[0], edge, sems.at[2])
    copy.start()
    copy.wait()


def shift_y(row, lane):
    return jnp.where(
        lax.rem(lane, LY) == 0,
        pltpu.roll(row, SITES - (LY - 1), 1),
        pltpu.roll(row, 1, 1),
    )


def site_masks():
    row = lax.broadcasted_iota(jnp.int32, (SITES, SITES), 0)
    column = lax.broadcasted_iota(jnp.int32, (SITES, SITES), 1)
    y = lax.rem(row, LY)
    ahead_x = column == lax.rem(row + LY, SITES)
    behind_x = column == lax.rem(row + SITES - LY, SITES)
    ahead_y = column == row - y + lax.rem(y + 1, LY)
    behind_y = column == row - y + lax.rem(y + LY - 1, LY)
    return ahead_x, ahead_y, behind_x, behind_y, column == row


def link_planes(packed):
    return jnp.concatenate([packed[:, :SITES], packed[:, SITES:]], axis=0).astype(f32)


def fetch(copies, sems):
    started = [
        pltpu.make_async_copy(source, target, sems.at[k])
        for k, (source, target) in enumerate(copies)
    ]
    for copy in started:
        copy.start()
    for copy in started:
        copy.wait()


def field_of(package):
    return package.at[:, pl.ds(0, FIELD)]


def links_of(package):
    return package.at[:, pl.ds(FIELD, PACKED_LINKS)]


def build(operator, rims, at):
    _, chip = position()
    ascending = chip == 1
    ahead_x, ahead_y, behind_x, behind_y, same = site_masks()
    table = link_planes(rims[at])
    below = link_planes(jnp.where(ascending, rims[at - 1], rims[at + 1]))
    lane = lax.broadcasted_iota(jnp.int32, table.shape, 1)
    from_x = pltpu.roll(table, LY, 1)
    from_y = shift_y(table, lane)

    def row_of(values, *what):
        k = link_row(*what)
        return values[k : k + 1]

    for part in range(2):
        sign = 1.0 if part == 0 else -1.0
        for i in range(COLORS):
            rows = pl.ds((part * COLORS + i) * SITES, SITES)
            for j in range(COLORS):
                zero = jnp.zeros((SITES, SITES), f32)
                plane = jnp.where(ahead_x, row_of(from_x, 0, part, i, j), zero)
                plane = jnp.where(ahead_y, row_of(from_y, 1, part, i, j), plane)
                plane = jnp.where(behind_x, sign * row_of(table, 0, part, j, i), plane)
                plane = jnp.where(behind_y, sign * row_of(table, 1, part, j, i), plane)
                lower = sign * row_of(below, 2, part, j, i)
                upper = row_of(table, 2, part, i, j)
                before = jnp.where(same, jnp.where(ascending, lower, upper), zero)
                after = jnp.where(same, jnp.where(ascending, upper, lower), zero)
                for k, block in enumerate((before, plane, after)):
                    operator[rows, pl.ds((k * COLORS + j) * SITES, SITES)] = block.astype(bf16)


def smeared(operator, source, at):
    half = SITES
    window = source[pl.ds(at - 1, 3)].reshape(3 * FIELD, 2 * half)
    product = jnp.dot(operator[...], window, preferred_element_type=f32)
    hops = jnp.concatenate(
        [
            product[:FIELD, :half] - product[FIELD:, half:],
            product[:FIELD, half:] + product[FIELD:, :half],
        ],
        axis=1,
    )
    center = source[at].astype(f32)
    return ((1.0 - 6.0 * SMEAR) * center + SMEAR * hops).astype(bf16)


def smear_inner(second, across, own, w_out, u_out, fields, rims, grown, operators, sems):
    copies = []
    for k, package in enumerate((second, across, own)):
        copies.append((field_of(package), fields.at[pl.ds(2 * k, 2)]))
        copies.append((links_of(package), rims.at[pl.ds(2 * k, 2)]))
    fetch(copies, sems)
    for r in range(1, 5):
        build(operators.at[r - 1], rims, r)
        grown[r - 1] = smeared(operators.at[r - 1], fields, r)
    for r in range(2, 4):
        w_out[r - 2] = smeared(operators.at[r - 1], grown, r - 1)
    u_out[...] = grown[2:4]


def smear_middle(across, own, first, u_in, w_out, u_out, fields, rims, grown, operators, sems):
    fetch(
        [
            (field_of(own), fields.at[pl.ds(0, 2)]),
            (field_of(first), fields.at[pl.ds(2, 2)]),
            (across.at[1, pl.ds(FIELD, PACKED_LINKS)], rims.at[0]),
            (links_of(own), rims.at[pl.ds(1, 2)]),
            (links_of(first), rims.at[pl.ds(3, 2)]),
            (u_in, grown.at[pl.ds(0, 2)]),
        ],
        sems,
    )
    for r in (5, 6, 4):
        build(operators.at[r - 4], rims, r - 3)
        if r > 4:
            grown[r - 3] = smeared(operators.at[r - 4], fields, r - 4)
    for r in (4, 5):
        w_out[r - 4] = smeared(operators.at[r - 4], grown, r - 3)
    u_out[...] = grown[2:4]


def smear_outer(own, first, last, u_in, w_out, fields, rims, grown, operators, sems):
    fetch(
        [
            (field_of(first), fields.at[pl.ds(0, 2)]),
            (last.at[pl.ds(0, FIELD)], fields.at[2]),
            (own.at[1, pl.ds(FIELD, PACKED_LINKS)], rims.at[0]),
            (links_of(first), rims.at[pl.ds(1, 2)]),
            (last.at[pl.ds(FIELD, PACKED_LINKS)], rims.at[3]),
            (u_in, grown.at[pl.ds(0, 2)]),
        ],
        sems,
    )
    build(operators.at[1], rims, 2)
    grown[2] = smeared(operators.at[1], fields, 1)
    build(operators.at[0], rims, 1)
    w_out[0] = smeared(operators.at[0], grown, 1)


def elemental_kernel(scale, directions, *refs):
    mine, theirs, (across, own, first) = refs[:3], refs[3:6], refs[6:9]
    out, out_low, w, rims, right, sems = refs[9:]
    core, chip = position()
    half = SITES
    copies = [
        (links_of(across), rims.at[pl.ds(0, 2)]),
        (links_of(own), rims.at[pl.ds(2, 2)]),
        (first.at[0, pl.ds(FIELD, PACKED_LINKS)], rims.at[4]),
    ]
    for group, side in ((mine, core), (theirs, 1 - core)):
        at = 0
        for ref in group:
            count = ref.shape[0]
            for part in range(2):
                copies.append(
                    (
                        ref.at[:, :, pl.ds(part * half, half)],
                        w.at[
                            pl.ds(at, count),
                            part,
                            :,
                            pl.ds(pl.multiple_of(side * half, half), half),
                        ],
                    )
                )
            at += count
    fetch(copies, sems)
    direction = directions[core]
    ahead_x, ahead_y, _, _, same = site_masks()
    one = jnp.ones((SITES, SITES), f32)
    zero = jnp.zeros((SITES, SITES), f32)
    is_x, is_y, is_z = direction == 0, direction == 1, direction == 2
    mask_x = jnp.where(ahead_x, one, zero)
    mask_y = jnp.where(ahead_y, one, zero)
    mask_z = jnp.where(same, one, zero)
    mask = jnp.where(is_x, mask_x, jnp.where(is_y, mask_y, mask_z))
    start = jnp.where(is_z, 1 - chip, 0)
    ahead = jnp.where(is_z, chip, 0)
    steps = w.shape[0] - 1

    for z in range(steps):
        table = link_planes(rims[z + start])
        lane = lax.broadcasted_iota(jnp.int32, table.shape, 1)
        count = 2 * COLORS * COLORS
        along_x = pltpu.roll(table, LY, 1)[:count]
        along_y = shift_y(table, lane)[count : 2 * count]
        along_z = table[2 * count : 3 * count]
        chosen = jnp.where(is_x, along_x, jnp.where(is_y, along_y, along_z))
        operator = jnp.concatenate(
            [
                jnp.concatenate(
                    [
                        (mask * chosen[k : k + 1]).astype(bf16)
                        for k in range(2 * COLORS * i + part, 2 * COLORS * (i + 1), 2)
                    ],
                    axis=1,
                )
                for part in range(2)
                for i in range(COLORS)
            ],
            axis=0,
        )
        source = z + ahead
        real = jnp.dot(operator, w[source, 0], preferred_element_type=f32)
        imag = jnp.dot(operator, w[source, 1], preferred_element_type=f32)
        hop_real = real[:FIELD] - imag[FIELD:]
        hop_imag = real[FIELD:] + imag[:FIELD]
        total = (hop_real + hop_imag).astype(bf16)
        rest = (hop_imag - hop_real).astype(bf16)
        vectors = 2 * half
        right[z, 0, :, pl.ds(0, vectors)] = total
        right[z, 0, :, pl.ds(vectors, vectors)] = rest
        right[z, 1, :, pl.ds(0, vectors)] = rest
        right[z, 1, :, pl.ds(vectors, vectors)] = -total
    vectors = 2 * half
    depth = steps * 2 * FIELD
    product = lax.dot_general(
        w[pl.ds(start, steps)].reshape(depth, vectors),
        right[...].reshape(depth, 2 * vectors),
        (((0,), (0,)), ((), ())),
        preferred_element_type=f32,
    )
    packed = (product[:, :vectors] + product[:, vectors:].T) * scale
    out[...] = packed
    out_low[...] = packed.astype(bf16)


def pair_kernel(pair_scale, pairs, s00, s10, s01, s11, perambulators, elementals, out, parts, left, right):
    core, chip = position()
    index = lax.axis_index("space")
    size = s00.shape[0]
    rows = elementals.shape[3]
    own_rows = pl.ds(pl.multiple_of(index * rows, 8), rows)
    for ref, t, k in (
        (s00, chip, core),
        (s10, 1 - chip, core),
        (s01, chip, 1 - core),
        (s11, 1 - chip, 1 - core),
    ):
        packed = ref[...].astype(f32)
        turned = packed.T
        parts[t, k, 0] = 0.5 * (packed - turned)
        parts[t, k, 1] = 0.5 * (packed + turned)
    for t in range(2):
        for k in range(2):
            for part in range(2):
                elementals[t, k, part] = parts[t, k, part, own_rows]
        real, imag = parts[t, 0, 0].astype(bf16), parts[t, 0, 1].astype(bf16)
        left[t, :size, :size] = real
        left[t, :size, size:] = -imag
        left[t, size:, :size] = imag
        left[t, size:, size:] = real
        real, imag = parts[t, 1, 0].astype(bf16), parts[t, 1, 1].astype(bf16)
        right[t, :size, :size] = real
        right[t, :size, size:] = imag
        right[t, size:, :size] = -imag
        right[t, size:, size:] = real

    for p in range(perambulators.shape[0]):
        source, sink = pairs[0, p], pairs[1, p]
        propagator = perambulators[p].reshape(2 * size, size)
        first = jnp.dot(left[sink], propagator, preferred_element_type=f32).astype(bf16)
        wide = jnp.concatenate([first[:size], first[size:]], axis=1)
        second = (
            jnp.dot(wide, right[source], preferred_element_type=f32) * pair_scale
        ).astype(bf16)
        real, imag = second[:, :size], second[:, size:]
        both = jnp.concatenate(
            [second, jnp.concatenate([imag, -real], axis=1)], axis=0
        )
        turned = jnp.concatenate([propagator[:size], propagator[size:]], axis=1)
        third = lax.dot_general(
            both, turned, (((1,), (1,)), ((), ())), preferred_element_type=f32
        ).astype(bf16)
        out[p] = third.reshape(2, size, size)


def params(megabytes):
    return pltpu.CompilerParams(vmem_limit_bytes=megabytes * 1024 * 1024)


def body(eigvecs, links, directions, pairs, perambulators):
    slices = eigvecs.shape[0]
    vector_count = eigvecs.shape[5]
    n = lax.axis_size("space")
    blocks = n // 4
    vmem = whole_in_vmem()
    anywhere = pl.BlockSpec(memory_space=pl.ANY)
    smem = pl.BlockSpec(memory_space=pltpu.SMEM)
    rows = FIELD + PACKED_LINKS

    def swap(value, bit):
        return lax.ppermute(value, "space", [(i, i ^ bit) for i in range(n)])

    package = jax.ShapeDtypeStruct((2, rows, vector_count), bf16)
    own, other, send = pl.pallas_call(
        split_kernel,
        out_shape=(package, package, package),
        in_specs=[anywhere, vmem],
        out_specs=(anywhere, anywhere, anywhere),
        scratch_shapes=[
            pltpu.VMEM((2, PACKED_LINKS, 2 * SITES), bf16),
            pltpu.SemaphoreType.DMA((28,)),
        ],
        compiler_params=params(8),
    )(eigvecs, jnp.transpose(links, (0, 1, 3, 4, 5, 2, 6)))
    received = swap(send, 1)
    own, other, edge = pl.pallas_call(
        join_kernel,
        out_shape=(package, package, jax.ShapeDtypeStruct((rows, vector_count), bf16)),
        in_specs=[anywhere] * 3,
        out_specs=(anywhere, anywhere, anywhere),
        scratch_shapes=[pltpu.SemaphoreType.DMA((3,))],
        input_output_aliases={1: 0, 2: 1},
        compiler_params=params(8),
    )(received, own, other)

    crossing, straight, outer = [], [], []
    for q in range(blocks):
        above, below = (q + 1) % blocks, (q + blocks - 1) % blocks
        for core in range(2):
            a, b = 4 * q + core, 4 * q + 2 + core
            crossing += [(b, 4 * above + core), (a, 4 * below + 2 + core)]
            straight += [(b, 4 * above + 2 + core), (a, 4 * below + core)]
            outer += [(a, 4 * above + core), (b, 4 * below + 2 + core)]
    across = swap(other, 2)
    second = lax.ppermute(own, "space", straight)
    first = lax.ppermute(other, "space", crossing)
    last = lax.ppermute(edge, "space", outer)

    def smear(kernel, operands, ranks, link_planes_held, grown_held, operators_held, outputs):
        def shape(count):
            return jax.ShapeDtypeStruct((count, FIELD, vector_count), bf16)

        products = 2 * FIELD * 3 * FIELD * vector_count * (operators_held + outputs[0])
        return pl.pallas_call(
            kernel,
            out_shape=tuple(shape(count) for count in outputs),
            in_specs=[anywhere] * len(operands),
            out_specs=(vmem,) * len(outputs),
            scratch_shapes=[
                pltpu.VMEM((ranks, FIELD, vector_count), bf16),
                pltpu.VMEM((link_planes_held, PACKED_LINKS, 2 * SITES), bf16),
                pltpu.VMEM((grown_held, FIELD, vector_count), bf16),
                pltpu.VMEM((operators_held, 2 * FIELD, 3 * FIELD), bf16),
                pltpu.SemaphoreType.DMA((6,)),
            ],
            compiler_params=params(20),
            cost_estimate=pl.CostEstimate(
                flops=4 * products, bytes_accessed=4 * 1024 * 1024, transcendentals=0
            ),
        )(*operands)

    w_inner, u_inner = smear(smear_inner, (second, across, own), 6, 6, 4, 4, (2, 2))
    w_middle, u_middle = smear(smear_middle, (across, own, first, u_inner), 4, 5, 4, 3, (2, 2))
    (w_outer,) = smear(smear_outer, (own, first, last, u_middle), 3, 4, 3, 2, (1,))
    mine = (w_inner, w_middle, w_outer)
    theirs = tuple(swap(part, 1) for part in mine)
    site_scale = (6.0 * n * SITES) ** (-0.5)
    square = (vector_count, vector_count)
    partial, partial_low = pl.pallas_call(
        functools.partial(elemental_kernel, site_scale),
        out_shape=(jax.ShapeDtypeStruct(square, f32), jax.ShapeDtypeStruct(square, bf16)),
        in_specs=[smem] + [anywhere] * 9,
        out_specs=(vmem, vmem),
        scratch_shapes=[
            pltpu.VMEM((5, 2, FIELD, vector_count), bf16),
            pltpu.VMEM((5, PACKED_LINKS, 2 * SITES), bf16),
            pltpu.VMEM((4, 2, FIELD, 2 * vector_count), bf16),
            pltpu.SemaphoreType.DMA((15,)),
        ],
        compiler_params=params(16),
    )(directions, *mine, *theirs, across, own, first)

    bit = 4
    while bit < n:
        partial = partial + swap(partial_low, bit).astype(f32)
        partial_low = partial.astype(bf16)
        bit *= 2
    other_slice = swap(partial_low, 2)
    other_copy = swap(partial_low, 1)
    other_both = swap(other_slice, 1)

    pair_scale = (2.0 * vector_count) ** (-0.5)
    owned_rows = vector_count // n
    big = 2 * vector_count
    return pl.pallas_call(
        functools.partial(pair_kernel, pair_scale),
        out_shape=(
            jax.ShapeDtypeStruct((slices, 2, 2, owned_rows, vector_count), f32),
            jax.ShapeDtypeStruct(perambulators.shape, bf16),
        ),
        in_specs=[smem] + [vmem] * 5,
        out_specs=(vmem, vmem),
        scratch_shapes=[
            pltpu.VMEM((slices, 2, 2, vector_count, vector_count), f32),
            pltpu.VMEM((slices, big, big), bf16),
            pltpu.VMEM((slices, big, big), bf16),
        ],
        compiler_params=params(16),
    )(pairs.T, partial_low, other_slice, other_copy, other_both, perambulators)


def solution(mesh):
    placed = (
        P("groups", None, None, "space", None, None),
        P("groups", None, None, None, None, "space", None),
        P("groups"),
        P(("groups", "space"), None),
        P(("groups", "space"), None, None, None),
    )
    return jax.shard_map(
        body,
        mesh=mesh,
        in_specs=placed,
        out_specs=(
            P("groups", None, None, "space", None),
            P(("groups", "space"), None, None, None),
        ),
        check_vma=False,
    )
```

```python
import functools

import jax
import jax.numpy as jnp
from jax import lax
from jax.experimental import pallas as pl
from jax.experimental.pallas import tpu as pltpu
from jax.sharding import PartitionSpec as P

LX = 16
LY = 8
SITES = LX * LY
COLORS = 3
FIELD = COLORS * SITES
LINK_ROWS = 54
PACKED_LINKS = 32
SMEAR = 0.12

bf16 = jnp.bfloat16
f32 = jnp.float32


def position():
    index = lax.axis_index("space")
    return lax.rem(index, 2), lax.rem(lax.div(index, 2), 2)


def whole_in_vmem():
    return pl.BlockSpec(memory_space=pltpu.VMEM)


def link_row(direction, part, row, column):
    return ((direction * COLORS + row) * COLORS + column) * 2 + part


def slot_of(core, chip, t):
    return core + (1 - 2 * core) * ((1 - chip) if t == 0 else chip)


def split_kernel(vectors, links_in, own, other, send, links, packed, sems):
    core, chip = position()
    half = vectors.shape[5] // 2
    arriving = pltpu.make_async_copy(links_in, links, sems.at[28])
    arriving.start()
    copies = []
    for t in range(2):
        for part in range(2):
            for color in range(COLORS):
                rows = pl.ds(color * SITES, SITES)
                lanes = pl.ds(part * half, half)
                near = pl.ds(pl.multiple_of(core * half, half), half)
                far = pl.ds(pl.multiple_of((1 - core) * half, half), half)
                block = vectors.at[chip + t * (1 - 2 * chip), part, color, 0]
                kept = (own, other)[t]
                for source, target in (
                    (block.at[:, near], kept.at[slot_of(core, chip, t), rows, lanes]),
                    (block.at[:, far], send.at[t, rows, lanes]),
                ):
                    copies.append(pltpu.make_async_copy(source, target, sems.at[len(copies)]))
                    copies[-1].start()
    arriving.wait()
    for t in range(2):
        table = links.at[chip + t * (1 - 2 * chip)]
        gathered = [
            table[d, row, column, 0].astype(f32)
            for d in range(3)
            for row in range(COLORS)
            for column in range(COLORS)
        ]
        gathered.append(jnp.zeros((2 * PACKED_LINKS - LINK_ROWS, SITES), f32))
        rows = jnp.concatenate(gathered, axis=0).astype(bf16)
        packed[t, :, pl.ds(0, SITES)] = rows[:PACKED_LINKS]
        packed[t, :, pl.ds(SITES, SITES)] = rows[PACKED_LINKS:]
        for target in ((own, other)[t].at[slot_of(core, chip, t)], send.at[t]):
            copies.append(
                pltpu.make_async_copy(
                    packed.at[t], target.at[pl.ds(FIELD, PACKED_LINKS)], sems.at[len(copies)]
                )
            )
            copies[-1].start()
    for copy in copies:
        copy.wait()


def join_kernel(received, own_in, other_in, own, other, edge, sems):
    core, chip = position()
    copies = [
        pltpu.make_async_copy(received.at[t], kept.at[1 - slot_of(core, chip, t)], sems.at[t])
        for t, kept in enumerate((own, other))
    ]
    for copy in copies:
        copy.start()
    here = slot_of(core, chip, 0) == 0
    kept_edge = pltpu.make_async_copy(own_in.at[0], edge, sems.at[2])
    received_edge = pltpu.make_async_copy(received.at[0], edge, sems.at[2])
    pl.when(here)(kept_edge.start)
    pl.when(jnp.logical_not(here))(received_edge.start)
    for copy in copies:
        copy.wait()
    kept_edge.wait()


def shift_y(row, lane):
    return jnp.where(
        lax.rem(lane, LY) == 0,
        pltpu.roll(row, SITES - (LY - 1), 1),
        pltpu.roll(row, 1, 1),
    )


def site_masks():
    row = lax.broadcasted_iota(jnp.int32, (SITES, SITES), 0)
    column = lax.broadcasted_iota(jnp.int32, (SITES, SITES), 1)
    y = lax.rem(row, LY)
    ahead_x = column == lax.rem(row + LY, SITES)
    behind_x = column == lax.rem(row + SITES - LY, SITES)
    ahead_y = column == row - y + lax.rem(y + 1, LY)
    behind_y = column == row - y + lax.rem(y + LY - 1, LY)
    return ahead_x, ahead_y, behind_x, behind_y, column == row


def link_planes(packed):
    return jnp.concatenate([packed[:, :SITES], packed[:, SITES:]], axis=0).astype(f32)


def fetch(copies, sems):
    started = [
        pltpu.make_async_copy(source, target, sems.at[k])
        for k, (source, target) in enumerate(copies)
    ]
    for copy in started:
        copy.start()
    for copy in started:
        copy.wait()


def field_of(package):
    return package.at[:, pl.ds(0, FIELD)]


def links_of(package):
    return package.at[:, pl.ds(FIELD, PACKED_LINKS)]


def build(operator, rims, at):
    _, chip = position()
    ascending = chip == 1
    ahead_x, ahead_y, behind_x, behind_y, same = site_masks()
    table = link_planes(rims[at])
    below = link_planes(jnp.where(ascending, rims[at - 1], rims[at + 1]))
    lane = lax.broadcasted_iota(jnp.int32, table.shape, 1)
    from_x = pltpu.roll(table, LY, 1)
    from_y = shift_y(table, lane)

    def row_of(values, *what):
        k = link_row(*what)
        return values[k : k + 1]

    for part in range(2):
        sign = 1.0 if part == 0 else -1.0
        for i in range(COLORS):
            rows = pl.ds((part * COLORS + i) * SITES, SITES)
            for j in range(COLORS):
                zero = jnp.zeros((SITES, SITES), f32)
                plane = jnp.where(ahead_x, row_of(from_x, 0, part, i, j), zero)
                plane = jnp.where(ahead_y, row_of(from_y, 1, part, i, j), plane)
                plane = jnp.where(behind_x, sign * row_of(table, 0, part, j, i), plane)
                plane = jnp.where(behind_y, sign * row_of(table, 1, part, j, i), plane)
                lower = sign * row_of(below, 2, part, j, i)
                upper = row_of(table, 2, part, i, j)
                before = jnp.where(same, jnp.where(ascending, lower, upper), zero)
                after = jnp.where(same, jnp.where(ascending, upper, lower), zero)
                for k, block in enumerate((before, plane, after)):
                    operator[rows, pl.ds((k * COLORS + j) * SITES, SITES)] = block.astype(bf16)


def smeared(operator, source, at):
    half = SITES
    window = source[pl.ds(at - 1, 3)].reshape(3 * FIELD, 2 * half)
    product = jnp.dot(operator[...], window, preferred_element_type=f32)
    hops = jnp.concatenate(
        [
            product[:FIELD, :half] - product[FIELD:, half:],
            product[:FIELD, half:] + product[FIELD:, :half],
        ],
        axis=1,
    )
    center = source[at].astype(f32)
    return ((1.0 - 6.0 * SMEAR) * center + SMEAR * hops).astype(bf16)


def smear_inner(second, across, own, w_out, u_out, fields, rims, grown, operators, sems):
    copies = []
    for k, package in enumerate((second, across, own)):
        copies.append((field_of(package), fields.at[pl.ds(2 * k, 2)]))
        copies.append((links_of(package), rims.at[pl.ds(2 * k, 2)]))
    fetch(copies, sems)
    for r in range(1, 5):
        build(operators.at[r - 1], rims, r)
        grown[r - 1] = smeared(operators.at[r - 1], fields, r)
    for r in range(2, 4):
        w_out[r - 2] = smeared(operators.at[r - 1], grown, r - 1)
    u_out[...] = grown[2:4]


def smear_middle(across, own, first, u_in, w_out, u_out, fields, rims, grown, operators, sems):
    fetch(
        [
            (field_of(own), fields.at[pl.ds(0, 2)]),
            (field_of(first), fields.at[pl.ds(2, 2)]),
            (across.at[1, pl.ds(FIELD, PACKED_LINKS)], rims.at[0]),
            (links_of(own), rims.at[pl.ds(1, 2)]),
            (links_of(first), rims.at[pl.ds(3, 2)]),
            (u_in, grown.at[pl.ds(0, 2)]),
        ],
        sems,
    )
    for r in (5, 6, 4):
        build(operators.at[r - 4], rims, r - 3)
        if r > 4:
            grown[r - 3] = smeared(operators.at[r - 4], fields, r - 4)
    for r in (4, 5):
        w_out[r - 4] = smeared(operators.at[r - 4], grown, r - 3)
    u_out[...] = grown[2:4]


def smear_outer(own, first, last, u_in, w_out, fields, rims, grown, operators, sems):
    fetch(
        [
            (field_of(first), fields.at[pl.ds(0, 2)]),
            (last.at[pl.ds(0, FIELD)], fields.at[2]),
            (own.at[1, pl.ds(FIELD, PACKED_LINKS)], rims.at[0]),
            (links_of(first), rims.at[pl.ds(1, 2)]),
            (last.at[pl.ds(FIELD, PACKED_LINKS)], rims.at[3]),
            (u_in, grown.at[pl.ds(0, 2)]),
        ],
        sems,
    )
    build(operators.at[1], rims, 2)
    grown[2] = smeared(operators.at[1], fields, 1)
    build(operators.at[0], rims, 1)
    w_out[0] = smeared(operators.at[0], grown, 1)


def elemental_kernel(scale, vector_pieces, link_pieces, directions, *refs):
    groups = max(piece[0] for piece in vector_pieces) + 1
    packages = max(piece[0] for piece in link_pieces) + 1
    mine, theirs, refs = refs[:groups], refs[groups : 2 * groups], refs[2 * groups :]
    packages, refs = refs[:packages], refs[packages:]
    *sums, w, rims, right, sems = refs
    core, chip = position()
    half = SITES
    copies = []
    at = 0
    for k, first, count in link_pieces:
        copies.append((links_of(packages[k].at[pl.ds(first, count)]), rims.at[pl.ds(at, count)]))
        at += count
    for group, side in ((mine, core), (theirs, 1 - core)):
        lanes = pl.ds(pl.multiple_of(side * half, half), half)
        at = 0
        for k, first, count in vector_pieces:
            for part in range(2):
                copies.append(
                    (
                        group[k].at[pl.ds(first, count), :, pl.ds(part * half, half)],
                        w.at[pl.ds(at, count), part, :, lanes],
                    )
                )
            at += count
    fetch(copies, sems)
    direction = directions[core]
    ahead_x, ahead_y, _, _, same = site_masks()
    one = jnp.ones((SITES, SITES), f32)
    zero = jnp.zeros((SITES, SITES), f32)
    is_x, is_y, is_z = direction == 0, direction == 1, direction == 2
    mask_x = jnp.where(ahead_x, one, zero)
    mask_y = jnp.where(ahead_y, one, zero)
    mask_z = jnp.where(same, one, zero)
    mask = jnp.where(is_x, mask_x, jnp.where(is_y, mask_y, mask_z))
    start = jnp.where(is_z, 1 - chip, 0)
    ahead = jnp.where(is_z, chip, 0)
    steps = w.shape[0] - 1

    for z in range(steps):
        table = link_planes(rims[z + start])
        lane = lax.broadcasted_iota(jnp.int32, table.shape, 1)
        count = 2 * COLORS * COLORS
        along_x = pltpu.roll(table, LY, 1)[:count]
        along_y = shift_y(table, lane)[count : 2 * count]
        along_z = table[2 * count : 3 * count]
        chosen = jnp.where(is_x, along_x, jnp.where(is_y, along_y, along_z))
        operator = jnp.concatenate(
            [
                jnp.concatenate(
                    [
                        (mask * chosen[k : k + 1]).astype(bf16)
                        for k in range(2 * COLORS * i + part, 2 * COLORS * (i + 1), 2)
                    ],
                    axis=1,
                )
                for part in range(2)
                for i in range(COLORS)
            ],
            axis=0,
        )
        source = z + ahead
        real = jnp.dot(operator, w[source, 0], preferred_element_type=f32)
        imag = jnp.dot(operator, w[source, 1], preferred_element_type=f32)
        hop_real = real[:FIELD] - imag[FIELD:]
        hop_imag = real[FIELD:] + imag[:FIELD]
        total = (hop_real + hop_imag).astype(bf16)
        rest = (hop_imag - hop_real).astype(bf16)
        vectors = 2 * half
        right[z, 0, :, pl.ds(0, vectors)] = total
        right[z, 0, :, pl.ds(vectors, vectors)] = rest
        right[z, 1, :, pl.ds(0, vectors)] = rest
        right[z, 1, :, pl.ds(vectors, vectors)] = -total
    vectors = 2 * half
    depth = steps * 2 * FIELD
    product = lax.dot_general(
        w[pl.ds(start, steps)].reshape(depth, vectors),
        right[...].reshape(depth, 2 * vectors),
        (((0,), (0,)), ((), ())),
        preferred_element_type=f32,
    )
    if scale is None:
        sums[-1][...] = product if len(sums) == 1 else product + sums[0][...]
        return
    before, out, out_low = sums
    product = product + before[...]
    packed = (product[:, :vectors] + product[:, vectors:].T) * scale
    out[...] = packed
    out_low[...] = packed.astype(bf16)


def pair_kernel(pair_scale, pairs, s00, s10, s01, s11, perambulators, elementals, out, parts, left, right):
    core, chip = position()
    index = lax.axis_index("space")
    size = s00.shape[0]
    rows = elementals.shape[3]
    own_rows = pl.ds(pl.multiple_of(index * rows, 8), rows)
    for ref, t, k in (
        (s00, chip, core),
        (s10, 1 - chip, core),
        (s01, chip, 1 - core),
        (s11, 1 - chip, 1 - core),
    ):
        packed = ref[...].astype(f32)
        turned = packed.T
        parts[t, k, 0] = 0.5 * (packed - turned)
        parts[t, k, 1] = 0.5 * (packed + turned)
    for t in range(2):
        for k in range(2):
            for part in range(2):
                elementals[t, k, part] = parts[t, k, part, own_rows]
        real, imag = parts[t, 0, 0].astype(bf16), parts[t, 0, 1].astype(bf16)
        left[t, :size, :size] = real
        left[t, :size, size:] = -imag
        left[t, size:, :size] = imag
        left[t, size:, size:] = real
        real, imag = parts[t, 1, 0].astype(bf16), parts[t, 1, 1].astype(bf16)
        right[t, :size, :size] = real
        right[t, :size, size:] = imag
        right[t, size:, :size] = -imag
        right[t, size:, size:] = real

    for p in range(perambulators.shape[0]):
        source, sink = pairs[0, p], pairs[1, p]
        propagator = perambulators[p].reshape(2 * size, size)
        first = jnp.dot(left[sink], propagator, preferred_element_type=f32).astype(bf16)
        wide = jnp.concatenate([first[:size], first[size:]], axis=1)
        second = (
            jnp.dot(wide, right[source], preferred_element_type=f32) * pair_scale
        ).astype(bf16)
        real, imag = second[:, :size], second[:, size:]
        both = jnp.concatenate(
            [second, jnp.concatenate([imag, -real], axis=1)], axis=0
        )
        turned = jnp.concatenate([propagator[:size], propagator[size:]], axis=1)
        third = lax.dot_general(
            both, turned, (((1,), (1,)), ((), ())), preferred_element_type=f32
        ).astype(bf16)
        out[p] = third.reshape(2, size, size)


def params(megabytes):
    return pltpu.CompilerParams(vmem_limit_bytes=megabytes * 1024 * 1024)


def body(eigvecs, links, directions, pairs, perambulators):
    slices = eigvecs.shape[0]
    vector_count = eigvecs.shape[5]
    n = lax.axis_size("space")
    blocks = n // 4
    vmem = whole_in_vmem()
    anywhere = pl.BlockSpec(memory_space=pl.ANY)
    hbm = pl.BlockSpec(memory_space=pltpu.HBM)
    smem = pl.BlockSpec(memory_space=pltpu.SMEM)
    table = jnp.transpose(links, (0, 1, 3, 4, 5, 2, 6))
    rows = FIELD + PACKED_LINKS

    def swap(value, bit):
        return lax.ppermute(value, "space", [(i, i ^ bit) for i in range(n)])

    package = jax.ShapeDtypeStruct((2, rows, vector_count), bf16)
    own, other, send = pl.pallas_call(
        split_kernel,
        out_shape=(package, package, package),
        in_specs=[hbm, hbm],
        out_specs=(anywhere, anywhere, anywhere),
        scratch_shapes=[
            pltpu.VMEM(table.shape, bf16),
            pltpu.VMEM((2, PACKED_LINKS, 2 * SITES), bf16),
            pltpu.SemaphoreType.DMA((29,)),
        ],
        compiler_params=params(8),
    )(eigvecs, table)
    received = swap(send, 1)
    own, other, edge = pl.pallas_call(
        join_kernel,
        out_shape=(package, package, jax.ShapeDtypeStruct((rows, vector_count), bf16)),
        in_specs=[anywhere] * 3,
        out_specs=(anywhere, anywhere, anywhere),
        scratch_shapes=[pltpu.SemaphoreType.DMA((3,))],
        input_output_aliases={1: 0, 2: 1},
        compiler_params=params(8),
    )(received, own, other)

    crossing, straight, outer = [], [], []
    for q in range(blocks):
        above, below = (q + 1) % blocks, (q + blocks - 1) % blocks
        for core in range(2):
            a, b = 4 * q + core, 4 * q + 2 + core
            crossing += [(b, 4 * above + core), (a, 4 * below + 2 + core)]
            straight += [(b, 4 * above + 2 + core), (a, 4 * below + core)]
            outer += [(a, 4 * above + core), (b, 4 * below + 2 + core)]
    across = swap(other, 2)
    second = lax.ppermute(own, "space", straight)
    first = lax.ppermute(other, "space", crossing)
    last = lax.ppermute(edge, "space", outer)

    def smear(kernel, operands, ranks, link_planes_held, grown_held, operators_held, outputs):
        def shape(count):
            return jax.ShapeDtypeStruct((count, FIELD, vector_count), bf16)

        products = 2 * FIELD * 3 * FIELD * vector_count * (operators_held + outputs[0])
        return pl.pallas_call(
            kernel,
            out_shape=tuple(shape(count) for count in outputs),
            in_specs=[anywhere] * len(operands),
            out_specs=(vmem,) * len(outputs),
            scratch_shapes=[
                pltpu.VMEM((ranks, FIELD, vector_count), bf16),
                pltpu.VMEM((link_planes_held, PACKED_LINKS, 2 * SITES), bf16),
                pltpu.VMEM((grown_held, FIELD, vector_count), bf16),
                pltpu.VMEM((operators_held, 2 * FIELD, 3 * FIELD), bf16),
                pltpu.SemaphoreType.DMA((6,)),
            ],
            compiler_params=params(20),
            cost_estimate=pl.CostEstimate(
                flops=1024, bytes_accessed=1024, transcendentals=0
            ),
        )(*operands)

    site_scale = (6.0 * n * SITES) ** (-0.5)
    square = (vector_count, vector_count)
    running = jax.ShapeDtypeStruct((vector_count, 2 * vector_count), f32)

    def elemental(scale, groups, vector_pieces, packages, link_pieces, sums):
        ranks = sum(piece[2] for piece in vector_pieces)
        outputs = (running,)
        if scale is not None:
            outputs = (jax.ShapeDtypeStruct(square, f32), jax.ShapeDtypeStruct(square, bf16))
        operands = [part[0] for part in groups] + [part[1] for part in groups] + list(packages)
        products = (ranks - 1) * 4 * FIELD * vector_count * (FIELD + 2 * vector_count)
        return pl.pallas_call(
            functools.partial(elemental_kernel, scale, vector_pieces, link_pieces),
            out_shape=outputs,
            in_specs=[smem] + [anywhere] * len(operands) + [vmem] * len(sums),
            out_specs=(vmem,) * len(outputs),
            scratch_shapes=[
                pltpu.VMEM((ranks, 2, FIELD, vector_count), bf16),
                pltpu.VMEM((ranks, PACKED_LINKS, 2 * SITES), bf16),
                pltpu.VMEM((ranks - 1, 2, FIELD, 2 * vector_count), bf16),
                pltpu.SemaphoreType.DMA((4 * len(vector_pieces) + len(link_pieces),)),
            ],
            compiler_params=params(16),
            cost_estimate=pl.CostEstimate(
                flops=1024, bytes_accessed=1024, transcendentals=0
            ),
        )(directions, *operands, *sums)

    def with_partner(part):
        return part, swap(part, 1)

    w_inner, u_inner = smear(smear_inner, (second, across, own), 6, 6, 4, 4, (2, 2))
    inner = with_partner(w_inner)
    (sum_inner,) = elemental(None, (inner,), ((0, 0, 2),), (across,), ((0, 0, 2),), ())
    u_inner, sum_inner = lax.optimization_barrier((u_inner, sum_inner))
    w_middle, u_middle = smear(smear_middle, (across, own, first, u_inner), 4, 5, 4, 3, (2, 2))
    middle = with_partner(w_middle)
    (w_outer,) = smear(smear_outer, (own, first, last, u_middle), 3, 4, 3, 2, (1,))
    outer_part = with_partner(w_outer)
    partial, partial_low = elemental(
        site_scale,
        (inner, middle, outer_part),
        ((0, 1, 1), (1, 0, 2), (2, 0, 1)),
        (across, own, first),
        ((0, 1, 1), (1, 0, 2), (2, 0, 1)),
        (sum_inner,),
    )

    bit = n // 2
    while bit >= 4:
        partner = bit if bit == 4 else bit + bit // 2
        partial = partial + swap(partial_low, partner).astype(f32)
        partial_low = partial.astype(bf16)
        bit //= 2
    other_slice = swap(partial_low, 2)
    other_copy = swap(partial_low, 1)
    other_both = swap(other_slice, 1)

    pair_scale = (2.0 * vector_count) ** (-0.5)
    owned_rows = vector_count // n
    big = 2 * vector_count
    return pl.pallas_call(
        functools.partial(pair_kernel, pair_scale),
        out_shape=(
            jax.ShapeDtypeStruct((slices, 2, 2, owned_rows, vector_count), f32),
            jax.ShapeDtypeStruct(perambulators.shape, bf16),
        ),
        in_specs=[smem] + [vmem] * 5,
        out_specs=(vmem, vmem),
        scratch_shapes=[
            pltpu.VMEM((slices, 2, 2, vector_count, vector_count), f32),
            pltpu.VMEM((slices, big, big), bf16),
            pltpu.VMEM((slices, big, big), bf16),
        ],
        compiler_params=params(16),
    )(pairs.T, partial_low, other_slice, other_copy, other_both, perambulators)


def solution(mesh):
    placed = (
        P("groups", None, None, "space", None, None),
        P("groups", None, None, None, None, "space", None),
        P("groups"),
        P(("groups", "space"), None),
        P(("groups", "space"), None, None, None),
    )
    return jax.shard_map(
        body,
        mesh=mesh,
        in_specs=placed,
        out_specs=(
            P("groups", None, None, "space", None),
            P(("groups", "space"), None, None, None),
        ),
        check_vma=False,
    )
```

```python
import functools

import jax
import jax.numpy as jnp
from jax import lax
from jax.experimental import pallas as pl
from jax.experimental.pallas import tpu as pltpu
from jax.sharding import PartitionSpec as P

LX = 16
LY = 8
SITES = LX * LY
COLORS = 3
FIELD = COLORS * SITES
LINK_ROWS = 54
PACKED_LINKS = 32
SMEAR = 0.12

bf16 = jnp.bfloat16
f32 = jnp.float32


def position():
    index = lax.axis_index("space")
    return lax.rem(index, 2), lax.rem(lax.div(index, 2), 2)


def whole_in_vmem():
    return pl.BlockSpec(memory_space=pltpu.VMEM)


def link_row(direction, part, row, column):
    return ((direction * COLORS + row) * COLORS + column) * 2 + part


def slot_of(core, chip, t):
    return core + (1 - 2 * core) * ((1 - chip) if t == 0 else chip)


def split_kernel(vectors, links_in, own, other, send, links, packed, sems):
    core, chip = position()
    half = vectors.shape[5] // 2
    arriving = pltpu.make_async_copy(links_in, links, sems.at[28])
    arriving.start()
    copies = []
    for t in range(2):
        for part in range(2):
            for color in range(COLORS):
                rows = pl.ds(color * SITES, SITES)
                lanes = pl.ds(part * half, half)
                near = pl.ds(pl.multiple_of(core * half, half), half)
                far = pl.ds(pl.multiple_of((1 - core) * half, half), half)
                block = vectors.at[chip + t * (1 - 2 * chip), part, color, 0]
                kept = (own, other)[t]
                for source, target in (
                    (block.at[:, near], kept.at[slot_of(core, chip, t), rows, lanes]),
                    (block.at[:, far], send.at[t, rows, lanes]),
                ):
                    copies.append(pltpu.make_async_copy(source, target, sems.at[len(copies)]))
                    copies[-1].start()
    arriving.wait()
    for t in range(2):
        table = links.at[chip + t * (1 - 2 * chip)]
        gathered = [
            table[d, row, column, 0].astype(f32)
            for d in range(3)
            for row in range(COLORS)
            for column in range(COLORS)
        ]
        gathered.append(jnp.zeros((2 * PACKED_LINKS - LINK_ROWS, SITES), f32))
        rows = jnp.concatenate(gathered, axis=0).astype(bf16)
        packed[t, :, pl.ds(0, SITES)] = rows[:PACKED_LINKS]
        packed[t, :, pl.ds(SITES, SITES)] = rows[PACKED_LINKS:]
        for target in ((own, other)[t].at[slot_of(core, chip, t)], send.at[t]):
            copies.append(
                pltpu.make_async_copy(
                    packed.at[t], target.at[pl.ds(FIELD, PACKED_LINKS)], sems.at[len(copies)]
                )
            )
            copies[-1].start()
    for copy in copies:
        copy.wait()


def join_kernel(received, own_in, other_in, own, other, edge, sems):
    core, chip = position()
    copies = [
        pltpu.make_async_copy(received.at[t], kept.at[1 - slot_of(core, chip, t)], sems.at[t])
        for t, kept in enumerate((own, other))
    ]
    for copy in copies:
        copy.start()
    here = slot_of(core, chip, 0) == 0
    kept_edge = pltpu.make_async_copy(own_in.at[0], edge, sems.at[2])
    received_edge = pltpu.make_async_copy(received.at[0], edge, sems.at[2])
    pl.when(here)(kept_edge.start)
    pl.when(jnp.logical_not(here))(received_edge.start)
    for copy in copies:
        copy.wait()
    kept_edge.wait()


def shift_y(row, lane):
    return jnp.where(
        lax.rem(lane, LY) == 0,
        pltpu.roll(row, SITES - (LY - 1), 1),
        pltpu.roll(row, 1, 1),
    )


def site_masks():
    row = lax.broadcasted_iota(jnp.int32, (SITES, SITES), 0)
    column = lax.broadcasted_iota(jnp.int32, (SITES, SITES), 1)
    y = lax.rem(row, LY)
    ahead_x = column == lax.rem(row + LY, SITES)
    behind_x = column == lax.rem(row + SITES - LY, SITES)
    ahead_y = column == row - y + lax.rem(y + 1, LY)
    behind_y = column == row - y + lax.rem(y + LY - 1, LY)
    return ahead_x, ahead_y, behind_x, behind_y, column == row


def link_planes(packed):
    return jnp.concatenate([packed[:, :SITES], packed[:, SITES:]], axis=0).astype(f32)


def fetch(copies, sems):
    started = [
        pltpu.make_async_copy(source, target, sems.at[k])
        for k, (source, target) in enumerate(copies)
    ]
    for copy in started:
        copy.start()
    for copy in started:
        copy.wait()


def field_of(package):
    return package.at[:, pl.ds(0, FIELD)]


def links_of(package):
    return package.at[:, pl.ds(FIELD, PACKED_LINKS)]


BEFORE, WITHIN, AFTER = range(3)


def build(operator, rims, at, pieces=(BEFORE, WITHIN, AFTER)):
    _, chip = position()
    ascending = chip == 1
    ahead_x, ahead_y, behind_x, behind_y, same = site_masks()
    table = link_planes(rims[at])
    if AFTER not in pieces:
        below = link_planes(rims[at - 1])
    elif BEFORE not in pieces:
        below = link_planes(rims[at + 1])
    else:
        below = link_planes(jnp.where(ascending, rims[at - 1], rims[at + 1]))
    lane = lax.broadcasted_iota(jnp.int32, table.shape, 1)
    from_x = pltpu.roll(table, LY, 1)
    from_y = shift_y(table, lane)

    def row_of(values, *what):
        k = link_row(*what)
        return values[k : k + 1]

    for part in range(2):
        sign = 1.0 if part == 0 else -1.0
        for i in range(COLORS):
            rows = pl.ds((part * COLORS + i) * SITES, SITES)
            for j in range(COLORS):
                zero = jnp.zeros((SITES, SITES), f32)
                lower = sign * row_of(below, 2, part, j, i)
                upper = row_of(table, 2, part, i, j)
                for k, piece in enumerate(pieces):
                    if piece == BEFORE:
                        block = jnp.where(same, jnp.where(ascending, lower, upper), zero)
                    elif piece == AFTER:
                        block = jnp.where(same, jnp.where(ascending, upper, lower), zero)
                    else:
                        block = jnp.where(ahead_x, row_of(from_x, 0, part, i, j), zero)
                        block = jnp.where(ahead_y, row_of(from_y, 1, part, i, j), block)
                        block = jnp.where(behind_x, sign * row_of(table, 0, part, j, i), block)
                        block = jnp.where(behind_y, sign * row_of(table, 1, part, j, i), block)
                    operator[rows, pl.ds((k * COLORS + j) * SITES, SITES)] = block.astype(bf16)


def weighted_hops(operator, planes):
    half = SITES
    window = planes.reshape(-1, 2 * half)
    product = jnp.dot(operator, window, preferred_element_type=f32)
    hops = jnp.concatenate(
        [
            product[:FIELD, :half] - product[FIELD:, half:],
            product[:FIELD, half:] + product[FIELD:, :half],
        ],
        axis=1,
    )
    return SMEAR * hops


def smeared(operator, source, at):
    center = (1.0 - 6.0 * SMEAR) * source[at].astype(f32)
    return (center + weighted_hops(operator[...], source[pl.ds(at - 1, 3)])).astype(bf16)


def smeared_short(operator, source, at):
    center = (1.0 - 6.0 * SMEAR) * source[at].astype(f32)
    columns = operator[:, pl.ds(0, 2 * FIELD)]
    return center + weighted_hops(columns, source[pl.ds(at - 1, 2)])


def smear_inner(second, across, own, w_out, u_out, fields, rims, grown, operators, sems):
    copies = []
    for k, package in enumerate((second, across, own)):
        copies.append((field_of(package), fields.at[pl.ds(2 * k, 2)]))
        copies.append((links_of(package), rims.at[pl.ds(2 * k, 2)]))
    fetch(copies, sems)
    for r in range(1, 5):
        build(operators.at[r - 1], rims, r)
        grown[r - 1] = smeared(operators.at[r - 1], fields, r)
    for r in range(2, 4):
        w_out[r - 2] = smeared(operators.at[r - 1], grown, r - 1)
    u_out[...] = grown[2:4]


def smear_middle(
    across, own, first, u_in, w_out, first_short, second_short, after_out, fields, rims, grown, operators, sems
):
    fetch(
        [
            (field_of(own), fields.at[pl.ds(0, 2)]),
            (field_of(first), fields.at[pl.ds(2, 2)]),
            (across.at[1, pl.ds(FIELD, PACKED_LINKS)], rims.at[0]),
            (links_of(own), rims.at[pl.ds(1, 2)]),
            (links_of(first), rims.at[pl.ds(3, 2)]),
            (u_in, grown.at[pl.ds(0, 2)]),
        ],
        sems,
    )
    for r in (5, 6, 4):
        build(operators.at[r - 4], rims, r - 3)
        if r > 4:
            grown[r - 3] = smeared(operators.at[r - 4], fields, r - 4)
    build(operators.at[3], rims, 4, (BEFORE, WITHIN))
    for r in (4, 5):
        w_out[r - 4] = smeared(operators.at[r - 4], grown, r - 3)
    first_short[...] = smeared_short(operators.at[3], fields, 3)
    second_short[...] = smeared_short(operators.at[2], grown, 3)
    after_out[...] = operators[2, :, pl.ds(2 * FIELD, FIELD)]


def smear_outer(first, last, first_short, second_short, after, w_out, rims, operator):
    rims[0] = first[1, pl.ds(FIELD, PACKED_LINKS)]
    rims[1] = last[pl.ds(FIELD, PACKED_LINKS)]
    build(operator, rims, 0, (AFTER,))
    outer = last[pl.ds(0, FIELD)]
    grown = (first_short[...] + weighted_hops(operator[...], outer)).astype(bf16)
    w_out[0] = (second_short[...] + weighted_hops(after[...], grown)).astype(bf16)


def elemental_kernel(scale, vector_pieces, link_pieces, directions, *refs):
    groups = max(piece[0] for piece in vector_pieces) + 1
    packages = max(piece[0] for piece in link_pieces) + 1
    mine, theirs, refs = refs[:groups], refs[groups : 2 * groups], refs[2 * groups :]
    packages, refs = refs[:packages], refs[packages:]
    *sums, w, rims, right = refs
    core, chip = position()
    half = SITES
    at = 0
    for k, first, count in link_pieces:
        rims[pl.ds(at, count)] = packages[k][pl.ds(first, count), pl.ds(FIELD, PACKED_LINKS)]
        at += count
    for group, side in ((mine, core), (theirs, 1 - core)):
        lanes = pl.ds(pl.multiple_of(side * half, half), half)
        at = 0
        for k, first, count in vector_pieces:
            for part in range(2):
                w[pl.ds(at, count), part, :, lanes] = group[k][
                    pl.ds(first, count), :, pl.ds(part * half, half)
                ]
            at += count
    direction = directions[core]
    ahead_x, ahead_y, _, _, same = site_masks()
    one = jnp.ones((SITES, SITES), f32)
    zero = jnp.zeros((SITES, SITES), f32)
    is_x, is_y, is_z = direction == 0, direction == 1, direction == 2
    mask_x = jnp.where(ahead_x, one, zero)
    mask_y = jnp.where(ahead_y, one, zero)
    mask_z = jnp.where(same, one, zero)
    mask = jnp.where(is_x, mask_x, jnp.where(is_y, mask_y, mask_z))
    start = jnp.where(is_z, 1 - chip, 0)
    ahead = jnp.where(is_z, chip, 0)
    steps = w.shape[0] - 1

    for z in range(steps):
        table = link_planes(rims[z + start])
        lane = lax.broadcasted_iota(jnp.int32, table.shape, 1)
        count = 2 * COLORS * COLORS
        along_x = pltpu.roll(table, LY, 1)[:count]
        along_y = shift_y(table, lane)[count : 2 * count]
        along_z = table[2 * count : 3 * count]
        chosen = jnp.where(is_x, along_x, jnp.where(is_y, along_y, along_z))
        operator = jnp.concatenate(
            [
                jnp.concatenate(
                    [
                        (mask * chosen[k : k + 1]).astype(bf16)
                        for k in range(2 * COLORS * i + part, 2 * COLORS * (i + 1), 2)
                    ],
                    axis=1,
                )
                for part in range(2)
                for i in range(COLORS)
            ],
            axis=0,
        )
        source = z + ahead
        real = jnp.dot(operator, w[source, 0], preferred_element_type=f32)
        imag = jnp.dot(operator, w[source, 1], preferred_element_type=f32)
        hop_real = real[:FIELD] - imag[FIELD:]
        hop_imag = real[FIELD:] + imag[:FIELD]
        total = (hop_real + hop_imag).astype(bf16)
        rest = (hop_imag - hop_real).astype(bf16)
        vectors = 2 * half
        right[z, 0, :, pl.ds(0, vectors)] = total
        right[z, 0, :, pl.ds(vectors, vectors)] = rest
        right[z, 1, :, pl.ds(0, vectors)] = rest
        right[z, 1, :, pl.ds(vectors, vectors)] = -total
    vectors = 2 * half
    depth = steps * 2 * FIELD
    product = lax.dot_general(
        w[pl.ds(start, steps)].reshape(depth, vectors),
        right[...].reshape(depth, 2 * vectors),
        (((0,), (0,)), ((), ())),
        preferred_element_type=f32,
    )
    if scale is None:
        sums[-1][...] = product if len(sums) == 1 else product + sums[0][...]
        return
    before, out, out_low = sums
    product = product + before[...]
    packed = (product[:, :vectors] + product[:, vectors:].T) * scale
    out[...] = packed
    out_low[...] = packed.astype(bf16)


def pair_kernel(pair_scale, pairs, s00, s10, s01, s11, perambulators, elementals, out, parts, left, right):
    core, chip = position()
    index = lax.axis_index("space")
    size = s00.shape[0]
    rows = elementals.shape[3]
    own_rows = pl.ds(pl.multiple_of(index * rows, 8), rows)
    for ref, t, k in (
        (s00, chip, core),
        (s10, 1 - chip, core),
        (s01, chip, 1 - core),
        (s11, 1 - chip, 1 - core),
    ):
        packed = ref[...].astype(f32)
        turned = packed.T
        parts[t, k, 0] = 0.5 * (packed - turned)
        parts[t, k, 1] = 0.5 * (packed + turned)
    for t in range(2):
        for k in range(2):
            for part in range(2):
                elementals[t, k, part] = parts[t, k, part, own_rows]
        real, imag = parts[t, 0, 0].astype(bf16), parts[t, 0, 1].astype(bf16)
        left[t, :size, :size] = real
        left[t, :size, size:] = -imag
        left[t, size:, :size] = imag
        left[t, size:, size:] = real
        real, imag = parts[t, 1, 0].astype(bf16), parts[t, 1, 1].astype(bf16)
        right[t, :size, :size] = real
        right[t, :size, size:] = imag
        right[t, size:, :size] = -imag
        right[t, size:, size:] = real

    for p in range(perambulators.shape[0]):
        source, sink = pairs[0, p], pairs[1, p]
        propagator = perambulators[p].reshape(2 * size, size)
        first = jnp.dot(left[sink], propagator, preferred_element_type=f32).astype(bf16)
        wide = jnp.concatenate([first[:size], first[size:]], axis=1)
        second = (
            jnp.dot(wide, right[source], preferred_element_type=f32) * pair_scale
        ).astype(bf16)
        real, imag = second[:, :size], second[:, size:]
        both = jnp.concatenate(
            [second, jnp.concatenate([imag, -real], axis=1)], axis=0
        )
        turned = jnp.concatenate([propagator[:size], propagator[size:]], axis=1)
        third = lax.dot_general(
            both, turned, (((1,), (1,)), ((), ())), preferred_element_type=f32
        ).astype(bf16)
        out[p] = third.reshape(2, size, size)


def params(megabytes):
    return pltpu.CompilerParams(vmem_limit_bytes=megabytes * 1024 * 1024)


def body(eigvecs, links, directions, pairs, perambulators):
    slices = eigvecs.shape[0]
    vector_count = eigvecs.shape[5]
    n = lax.axis_size("space")
    blocks = n // 4
    vmem = whole_in_vmem()
    anywhere = pl.BlockSpec(memory_space=pl.ANY)
    hbm = pl.BlockSpec(memory_space=pltpu.HBM)
    smem = pl.BlockSpec(memory_space=pltpu.SMEM)
    table = jnp.transpose(links, (0, 1, 3, 4, 5, 2, 6))
    rows = FIELD + PACKED_LINKS

    def swap(value, bit):
        return lax.ppermute(value, "space", [(i, i ^ bit) for i in range(n)])

    package = jax.ShapeDtypeStruct((2, rows, vector_count), bf16)
    own, other, send = pl.pallas_call(
        split_kernel,
        out_shape=(package, package, package),
        in_specs=[hbm, hbm],
        out_specs=(anywhere, anywhere, anywhere),
        scratch_shapes=[
            pltpu.VMEM(table.shape, bf16),
            pltpu.VMEM((2, PACKED_LINKS, 2 * SITES), bf16),
            pltpu.SemaphoreType.DMA((29,)),
        ],
        compiler_params=params(8),
    )(eigvecs, table)
    received = swap(send, 1)
    own, other, edge = pl.pallas_call(
        join_kernel,
        out_shape=(package, package, jax.ShapeDtypeStruct((rows, vector_count), bf16)),
        in_specs=[anywhere] * 3,
        out_specs=(anywhere, anywhere, anywhere),
        scratch_shapes=[pltpu.SemaphoreType.DMA((3,))],
        input_output_aliases={1: 0, 2: 1},
        compiler_params=params(8),
    )(received, own, other)

    crossing, straight, outer = [], [], []
    for q in range(blocks):
        above, below = (q + 1) % blocks, (q + blocks - 1) % blocks
        for core in range(2):
            a, b = 4 * q + core, 4 * q + 2 + core
            crossing += [(b, 4 * above + core), (a, 4 * below + 2 + core)]
            straight += [(b, 4 * above + 2 + core), (a, 4 * below + core)]
            outer += [(a, 4 * above + core), (b, 4 * below + 2 + core)]
    across = swap(other, 2)
    second = lax.ppermute(own, "space", straight)
    first = lax.ppermute(other, "space", crossing)
    last = lax.ppermute(edge, "space", outer)

    small = pl.CostEstimate(flops=1024, bytes_accessed=1024, transcendentals=0)

    def smear(kernel, operands, ranks, link_planes_held, grown_held, operators_held, outputs, more=()):
        def shape(count):
            return jax.ShapeDtypeStruct((count, FIELD, vector_count), bf16)

        return pl.pallas_call(
            kernel,
            out_shape=tuple(shape(count) for count in outputs) + more,
            in_specs=[anywhere] * len(operands),
            out_specs=(vmem,) * (len(outputs) + len(more)),
            scratch_shapes=[
                pltpu.VMEM((ranks, FIELD, vector_count), bf16),
                pltpu.VMEM((link_planes_held, PACKED_LINKS, 2 * SITES), bf16),
                pltpu.VMEM((grown_held, FIELD, vector_count), bf16),
                pltpu.VMEM((operators_held, 2 * FIELD, 3 * FIELD), bf16),
                pltpu.SemaphoreType.DMA((6,)),
            ],
            compiler_params=params(20),
            cost_estimate=small,
        )(*operands)

    site_scale = (6.0 * n * SITES) ** (-0.5)
    square = (vector_count, vector_count)
    running = jax.ShapeDtypeStruct((vector_count, 2 * vector_count), f32)

    def elemental(scale, groups, vector_pieces, packages, link_pieces, sums):
        ranks = sum(piece[2] for piece in vector_pieces)
        outputs = (running,)
        if scale is not None:
            outputs = (jax.ShapeDtypeStruct(square, f32), jax.ShapeDtypeStruct(square, bf16))
        operands = [part[0] for part in groups] + [part[1] for part in groups] + list(packages)
        return pl.pallas_call(
            functools.partial(elemental_kernel, scale, vector_pieces, link_pieces),
            out_shape=outputs,
            in_specs=[smem] + [vmem] * (len(operands) + len(sums)),
            out_specs=(vmem,) * len(outputs),
            scratch_shapes=[
                pltpu.VMEM((ranks, 2, FIELD, vector_count), bf16),
                pltpu.VMEM((ranks, PACKED_LINKS, 2 * SITES), bf16),
                pltpu.VMEM((ranks - 1, 2, FIELD, 2 * vector_count), bf16),
            ],
            compiler_params=params(16),
            cost_estimate=small,
        )(directions, *operands, *sums)

    def with_partner(part):
        return part, swap(part, 1)

    w_inner, u_inner = smear(smear_inner, (second, across, own), 6, 6, 4, 4, (2, 2))
    inner = with_partner(w_inner)
    (sum_inner,) = elemental(None, (inner,), ((0, 0, 2),), (across,), ((0, 0, 2),), ())
    u_inner, sum_inner = lax.optimization_barrier((u_inner, sum_inner))
    short = jax.ShapeDtypeStruct((FIELD, vector_count), f32)
    after_shape = jax.ShapeDtypeStruct((2 * FIELD, FIELD), bf16)
    w_middle, first_short, second_short, after = smear(
        smear_middle, (across, own, first, u_inner), 4, 5, 4, 4, (2,), (short, short, after_shape)
    )
    middle = with_partner(w_middle)
    w_outer = pl.pallas_call(
        smear_outer,
        out_shape=jax.ShapeDtypeStruct((1, FIELD, vector_count), bf16),
        in_specs=[vmem] * 5,
        out_specs=vmem,
        scratch_shapes=[
            pltpu.VMEM((2, PACKED_LINKS, 2 * SITES), bf16),
            pltpu.VMEM((2 * FIELD, FIELD), bf16),
        ],
        compiler_params=params(8),
        cost_estimate=small,
    )(first, last, first_short, second_short, after)
    outer_part = with_partner(w_outer)
    (sum_middle,) = elemental(
        None, (inner, middle), ((0, 1, 1), (1, 0, 2)), (across, own), ((0, 1, 1), (1, 0, 2)), (sum_inner,)
    )
    partial, partial_low = elemental(
        site_scale, (middle, outer_part), ((0, 1, 1), (1, 0, 1)), (own, first), ((0, 1, 1), (1, 0, 1)), (sum_middle,)
    )

    bit = n // 2
    while bit >= 4:
        partner = bit if bit == 4 else bit + bit // 2
        partial = partial + swap(partial_low, partner).astype(f32)
        partial_low = partial.astype(bf16)
        bit //= 2
    other_slice = swap(partial_low, 2)
    other_copy = swap(partial_low, 1)
    other_both = swap(other_slice, 1)

    pair_scale = (2.0 * vector_count) ** (-0.5)
    owned_rows = vector_count // n
    big = 2 * vector_count
    return pl.pallas_call(
        functools.partial(pair_kernel, pair_scale),
        out_shape=(
            jax.ShapeDtypeStruct((slices, 2, 2, owned_rows, vector_count), f32),
            jax.ShapeDtypeStruct(perambulators.shape, bf16),
        ),
        in_specs=[smem] + [vmem] * 5,
        out_specs=(vmem, vmem),
        scratch_shapes=[
            pltpu.VMEM((slices, 2, 2, vector_count, vector_count), f32),
            pltpu.VMEM((slices, big, big), bf16),
            pltpu.VMEM((slices, big, big), bf16),
        ],
        compiler_params=params(16),
    )(pairs.T, partial_low, other_slice, other_copy, other_both, perambulators)


def solution(mesh):
    placed = (
        P("groups", None, None, "space", None, None),
        P("groups", None, None, None, None, "space", None),
        P("groups"),
        P(("groups", "space"), None),
        P(("groups", "space"), None, None, None),
    )
    return jax.shard_map(
        body,
        mesh=mesh,
        in_specs=placed,
        out_specs=(
            P("groups", None, None, "space", None),
            P(("groups", "space"), None, None, None),
        ),
        check_vma=False,
    )
```

```python
import functools

import jax
import jax.numpy as jnp
from jax import lax
from jax.experimental import pallas as pl
from jax.experimental.pallas import tpu as pltpu
from jax.sharding import PartitionSpec as P

LX = 16
LY = 8
SITES = LX * LY
COLORS = 3
FIELD = COLORS * SITES
LINK_ROWS = 54
PACKED_LINKS = 32
SMEAR = 0.12

bf16 = jnp.bfloat16
f32 = jnp.float32


def position():
    index = lax.axis_index("space")
    return lax.rem(index, 2), lax.rem(lax.div(index, 2), 2)


def whole_in_vmem():
    return pl.BlockSpec(memory_space=pltpu.VMEM)


def link_row(direction, part, row, column):
    return ((direction * COLORS + row) * COLORS + column) * 2 + part


def slot_of(core, chip, t):
    return core + (1 - 2 * core) * ((1 - chip) if t == 0 else chip)


def split_kernel(vectors, links_in, own, other, send, links, packed, sems):
    core, chip = position()
    half = vectors.shape[5] // 2
    arriving = pltpu.make_async_copy(links_in, links, sems.at[28])
    arriving.start()
    copies = []
    for t in range(2):
        for part in range(2):
            for color in range(COLORS):
                rows = pl.ds(color * SITES, SITES)
                lanes = pl.ds(part * half, half)
                near = pl.ds(pl.multiple_of(core * half, half), half)
                far = pl.ds(pl.multiple_of((1 - core) * half, half), half)
                block = vectors.at[chip + t * (1 - 2 * chip), part, color, 0]
                kept = (own, other)[t]
                for source, target in (
                    (block.at[:, near], kept.at[slot_of(core, chip, t), rows, lanes]),
                    (block.at[:, far], send.at[t, rows, lanes]),
                ):
                    copies.append(pltpu.make_async_copy(source, target, sems.at[len(copies)]))
                    copies[-1].start()
    arriving.wait()
    for t in range(2):
        table = links.at[chip + t * (1 - 2 * chip)]
        gathered = [
            table[d, row, column, 0].astype(f32)
            for d in range(3)
            for row in range(COLORS)
            for column in range(COLORS)
        ]
        gathered.append(jnp.zeros((2 * PACKED_LINKS - LINK_ROWS, SITES), f32))
        rows = jnp.concatenate(gathered, axis=0).astype(bf16)
        packed[t, :, pl.ds(0, SITES)] = rows[:PACKED_LINKS]
        packed[t, :, pl.ds(SITES, SITES)] = rows[PACKED_LINKS:]
        for target in ((own, other)[t].at[slot_of(core, chip, t)], send.at[t]):
            copies.append(
                pltpu.make_async_copy(
                    packed.at[t], target.at[pl.ds(FIELD, PACKED_LINKS)], sems.at[len(copies)]
                )
            )
            copies[-1].start()
    for copy in copies:
        copy.wait()


def join_kernel(received, own_in, other_in, own, other, edge, sems):
    core, chip = position()
    copies = [
        pltpu.make_async_copy(received.at[t], kept.at[1 - slot_of(core, chip, t)], sems.at[t])
        for t, kept in enumerate((own, other))
    ]
    for copy in copies:
        copy.start()
    here = slot_of(core, chip, 0) == 0
    kept_edge = pltpu.make_async_copy(own_in.at[0], edge, sems.at[2])
    received_edge = pltpu.make_async_copy(received.at[0], edge, sems.at[2])
    pl.when(here)(kept_edge.start)
    pl.when(jnp.logical_not(here))(received_edge.start)
    for copy in copies:
        copy.wait()
    kept_edge.wait()


def shift_y(row, lane):
    return jnp.where(
        lax.rem(lane, LY) == 0,
        pltpu.roll(row, SITES - (LY - 1), 1),
        pltpu.roll(row, 1, 1),
    )


def site_masks():
    row = lax.broadcasted_iota(jnp.int32, (SITES, SITES), 0)
    column = lax.broadcasted_iota(jnp.int32, (SITES, SITES), 1)
    y = lax.rem(row, LY)
    ahead_x = column == lax.rem(row + LY, SITES)
    behind_x = column == lax.rem(row + SITES - LY, SITES)
    ahead_y = column == row - y + lax.rem(y + 1, LY)
    behind_y = column == row - y + lax.rem(y + LY - 1, LY)
    return ahead_x, ahead_y, behind_x, behind_y, column == row


def link_planes(packed):
    return jnp.concatenate([packed[:, :SITES], packed[:, SITES:]], axis=0).astype(f32)


def fetch(copies, sems):
    started = [
        pltpu.make_async_copy(source, target, sems.at[k])
        for k, (source, target) in enumerate(copies)
    ]
    for copy in started:
        copy.start()
    for copy in started:
        copy.wait()


def field_of(package):
    return package.at[:, pl.ds(0, FIELD)]


def links_of(package):
    return package.at[:, pl.ds(FIELD, PACKED_LINKS)]


BEFORE, WITHIN, AFTER = range(3)


def build(operator, rims, at, pieces=(BEFORE, WITHIN, AFTER)):
    _, chip = position()
    ascending = chip == 1
    ahead_x, ahead_y, behind_x, behind_y, same = site_masks()
    table = link_planes(rims[at])
    if AFTER not in pieces:
        below = link_planes(rims[at - 1])
    elif BEFORE not in pieces:
        below = link_planes(rims[at + 1])
    else:
        below = link_planes(jnp.where(ascending, rims[at - 1], rims[at + 1]))
    lane = lax.broadcasted_iota(jnp.int32, table.shape, 1)
    from_x = pltpu.roll(table, LY, 1)
    from_y = shift_y(table, lane)

    def row_of(values, *what):
        k = link_row(*what)
        return values[k : k + 1]

    for part in range(2):
        sign = 1.0 if part == 0 else -1.0
        for i in range(COLORS):
            rows = pl.ds((part * COLORS + i) * SITES, SITES)
            for j in range(COLORS):
                zero = jnp.zeros((SITES, SITES), f32)
                lower = sign * row_of(below, 2, part, j, i)
                upper = row_of(table, 2, part, i, j)
                for k, piece in enumerate(pieces):
                    if piece == BEFORE:
                        block = jnp.where(same, jnp.where(ascending, lower, upper), zero)
                    elif piece == AFTER:
                        block = jnp.where(same, jnp.where(ascending, upper, lower), zero)
                    else:
                        block = jnp.where(ahead_x, row_of(from_x, 0, part, i, j), zero)
                        block = jnp.where(ahead_y, row_of(from_y, 1, part, i, j), block)
                        block = jnp.where(behind_x, sign * row_of(table, 0, part, j, i), block)
                        block = jnp.where(behind_y, sign * row_of(table, 1, part, j, i), block)
                    operator[rows, pl.ds((k * COLORS + j) * SITES, SITES)] = block.astype(bf16)


def weighted_hops(operator, planes):
    half = SITES
    window = planes.reshape(-1, 2 * half)
    product = jnp.dot(operator, window, preferred_element_type=f32)
    hops = jnp.concatenate(
        [
            product[:FIELD, :half] - product[FIELD:, half:],
            product[:FIELD, half:] + product[FIELD:, :half],
        ],
        axis=1,
    )
    return SMEAR * hops


def smeared(operator, source, at):
    center = (1.0 - 6.0 * SMEAR) * source[at].astype(f32)
    return (center + weighted_hops(operator[...], source[pl.ds(at - 1, 3)])).astype(bf16)


def smeared_short(operator, planes):
    center = (1.0 - 6.0 * SMEAR) * planes[1].astype(f32)
    return center + weighted_hops(operator, planes)


def smear_inner(second, across, own, w_out, u_out, operator_out, fields, rims, grown, operators, sems):
    copies = []
    for k, package in enumerate((second, across, own)):
        copies.append((field_of(package), fields.at[pl.ds(2 * k, 2)]))
        copies.append((links_of(package), rims.at[pl.ds(2 * k, 2)]))
    fetch(copies, sems)
    for r in range(1, 5):
        operator = operators.at[r - 1] if r < 4 else operator_out
        build(operator, rims, r)
        grown[r - 1] = smeared(operator, fields, r)
    for r in range(2, 4):
        w_out[r - 2] = smeared(operators.at[r - 1], grown, r - 1)
    u_out[...] = grown[2:4]


def smear_prepare(own, u_in, operator, first_short, second_short, within_out, rims):
    for k in range(2):
        rims[k] = own[k, pl.ds(FIELD, PACKED_LINKS)]
    build(within_out, rims, 1, (BEFORE, WITHIN))
    first_short[...] = smeared_short(within_out[...], own[:, pl.ds(0, FIELD)])
    second_short[...] = smeared_short(operator[:, pl.ds(0, 2 * FIELD)], u_in[...])


def smear_middle(
    own, first, u_in, operator_in, short_in, second_in, within_in, w_out, first_short, second_short, after_out, fields, rims, grown, operator, within, after
):
    fields[0] = own[1, pl.ds(0, FIELD)]
    rims[0] = own[1, pl.ds(FIELD, PACKED_LINKS)]
    for k in range(2):
        fields[1 + k] = first[k, pl.ds(0, FIELD)]
        rims[1 + k] = first[k, pl.ds(FIELD, PACKED_LINKS)]
    grown[0] = u_in[1]
    build(after, rims, 0, (AFTER,))
    grown[1] = (short_in[...] + weighted_hops(after[...], fields[1])).astype(bf16)
    build(operator, rims, 1)
    grown[2] = smeared(operator, fields, 1)
    w_out[0] = (second_in[...] + weighted_hops(operator_in[:, pl.ds(2 * FIELD, FIELD)], grown[1])).astype(bf16)
    short = smeared_short(within_in[...], grown[pl.ds(0, 2)])
    w_out[1] = (short + weighted_hops(after[...], grown[2])).astype(bf16)
    build(within, rims, 2, (BEFORE, WITHIN))
    first_short[...] = smeared_short(within[...], fields[pl.ds(1, 2)])
    second_short[...] = smeared_short(operator[:, pl.ds(0, 2 * FIELD)], grown[pl.ds(1, 2)])
    after_out[...] = operator[:, pl.ds(2 * FIELD, FIELD)]


def smear_outer(first, last, first_short, second_short, after, w_out, rims, operator):
    rims[0] = first[1, pl.ds(FIELD, PACKED_LINKS)]
    rims[1] = last[pl.ds(FIELD, PACKED_LINKS)]
    build(operator, rims, 0, (AFTER,))
    outer = last[pl.ds(0, FIELD)]
    grown = (first_short[...] + weighted_hops(operator[...], outer)).astype(bf16)
    w_out[0] = (second_short[...] + weighted_hops(after[...], grown)).astype(bf16)


def elemental_kernel(scale, vector_pieces, link_pieces, directions, *refs):
    groups = max(piece[0] for piece in vector_pieces) + 1
    packages = max(piece[0] for piece in link_pieces) + 1
    mine, theirs, refs = refs[:groups], refs[groups : 2 * groups], refs[2 * groups :]
    packages, refs = refs[:packages], refs[packages:]
    *sums, w, rims, right = refs
    core, chip = position()
    half = SITES
    at = 0
    for k, first, count in link_pieces:
        rims[pl.ds(at, count)] = packages[k][pl.ds(first, count), pl.ds(FIELD, PACKED_LINKS)]
        at += count
    for group, side in ((mine, core), (theirs, 1 - core)):
        lanes = pl.ds(pl.multiple_of(side * half, half), half)
        at = 0
        for k, first, count in vector_pieces:
            for part in range(2):
                w[pl.ds(at, count), part, :, lanes] = group[k][
                    pl.ds(first, count), :, pl.ds(part * half, half)
                ]
            at += count
    direction = directions[core]
    ahead_x, ahead_y, _, _, same = site_masks()
    one = jnp.ones((SITES, SITES), f32)
    zero = jnp.zeros((SITES, SITES), f32)
    is_x, is_y, is_z = direction == 0, direction == 1, direction == 2
    mask_x = jnp.where(ahead_x, one, zero)
    mask_y = jnp.where(ahead_y, one, zero)
    mask_z = jnp.where(same, one, zero)
    mask = jnp.where(is_x, mask_x, jnp.where(is_y, mask_y, mask_z))
    start = jnp.where(is_z, 1 - chip, 0)
    ahead = jnp.where(is_z, chip, 0)
    steps = w.shape[0] - 1

    for z in range(steps):
        table = link_planes(rims[z + start])
        lane = lax.broadcasted_iota(jnp.int32, table.shape, 1)
        count = 2 * COLORS * COLORS
        along_x = pltpu.roll(table, LY, 1)[:count]
        along_y = shift_y(table, lane)[count : 2 * count]
        along_z = table[2 * count : 3 * count]
        chosen = jnp.where(is_x, along_x, jnp.where(is_y, along_y, along_z))
        operator = jnp.concatenate(
            [
                jnp.concatenate(
                    [
                        (mask * chosen[k : k + 1]).astype(bf16)
                        for k in range(2 * COLORS * i + part, 2 * COLORS * (i + 1), 2)
                    ],
                    axis=1,
                )
                for part in range(2)
                for i in range(COLORS)
            ],
            axis=0,
        )
        source = z + ahead
        real = jnp.dot(operator, w[source, 0], preferred_element_type=f32)
        imag = jnp.dot(operator, w[source, 1], preferred_element_type=f32)
        hop_real = real[:FIELD] - imag[FIELD:]
        hop_imag = real[FIELD:] + imag[:FIELD]
        total = (hop_real + hop_imag).astype(bf16)
        rest = (hop_imag - hop_real).astype(bf16)
        vectors = 2 * half
        right[z, 0, :, pl.ds(0, vectors)] = total
        right[z, 0, :, pl.ds(vectors, vectors)] = rest
        right[z, 1, :, pl.ds(0, vectors)] = rest
        right[z, 1, :, pl.ds(vectors, vectors)] = -total
    vectors = 2 * half
    depth = steps * 2 * FIELD
    product = lax.dot_general(
        w[pl.ds(start, steps)].reshape(depth, vectors),
        right[...].reshape(depth, 2 * vectors),
        (((0,), (0,)), ((), ())),
        preferred_element_type=f32,
    )
    if scale is None:
        sums[-1][...] = product if len(sums) == 1 else product + sums[0][...]
        return
    before, out, out_low = sums
    product = product + before[...]
    packed = (product[:, :vectors] + product[:, vectors:].T) * scale
    out[...] = packed
    out_low[...] = packed.astype(bf16)


def pair_kernel(pair_scale, pairs, s00, s10, s01, s11, perambulators, elementals, out, parts, left, right):
    core, chip = position()
    index = lax.axis_index("space")
    size = s00.shape[0]
    rows = elementals.shape[3]
    own_rows = pl.ds(pl.multiple_of(index * rows, 8), rows)
    for ref, t, k in (
        (s00, chip, core),
        (s10, 1 - chip, core),
        (s01, chip, 1 - core),
        (s11, 1 - chip, 1 - core),
    ):
        packed = ref[...].astype(f32)
        turned = packed.T
        parts[t, k, 0] = 0.5 * (packed - turned)
        parts[t, k, 1] = 0.5 * (packed + turned)
    for t in range(2):
        for k in range(2):
            for part in range(2):
                elementals[t, k, part] = parts[t, k, part, own_rows]
        real, imag = parts[t, 0, 0].astype(bf16), parts[t, 0, 1].astype(bf16)
        left[t, :size, :size] = real
        left[t, :size, size:] = -imag
        left[t, size:, :size] = imag
        left[t, size:, size:] = real
        real, imag = parts[t, 1, 0].astype(bf16), parts[t, 1, 1].astype(bf16)
        right[t, :size, :size] = real
        right[t, :size, size:] = imag
        right[t, size:, :size] = -imag
        right[t, size:, size:] = real

    for p in range(perambulators.shape[0]):
        source, sink = pairs[0, p], pairs[1, p]
        propagator = perambulators[p].reshape(2 * size, size)
        first = jnp.dot(left[sink], propagator, preferred_element_type=f32).astype(bf16)
        wide = jnp.concatenate([first[:size], first[size:]], axis=1)
        second = (
            jnp.dot(wide, right[source], preferred_element_type=f32) * pair_scale
        ).astype(bf16)
        real, imag = second[:, :size], second[:, size:]
        both = jnp.concatenate(
            [second, jnp.concatenate([imag, -real], axis=1)], axis=0
        )
        turned = jnp.concatenate([propagator[:size], propagator[size:]], axis=1)
        third = lax.dot_general(
            both, turned, (((1,), (1,)), ((), ())), preferred_element_type=f32
        ).astype(bf16)
        out[p] = third.reshape(2, size, size)


def params(megabytes):
    return pltpu.CompilerParams(vmem_limit_bytes=megabytes * 1024 * 1024)


def body(eigvecs, links, directions, pairs, perambulators):
    slices = eigvecs.shape[0]
    vector_count = eigvecs.shape[5]
    n = lax.axis_size("space")
    blocks = n // 4
    vmem = whole_in_vmem()
    anywhere = pl.BlockSpec(memory_space=pl.ANY)
    hbm = pl.BlockSpec(memory_space=pltpu.HBM)
    smem = pl.BlockSpec(memory_space=pltpu.SMEM)
    table = jnp.transpose(links, (0, 1, 3, 4, 5, 2, 6))
    rows = FIELD + PACKED_LINKS

    def swap(value, bit):
        return lax.ppermute(value, "space", [(i, i ^ bit) for i in range(n)])

    package = jax.ShapeDtypeStruct((2, rows, vector_count), bf16)
    own, other, send = pl.pallas_call(
        split_kernel,
        out_shape=(package, package, package),
        in_specs=[hbm, hbm],
        out_specs=(anywhere, anywhere, anywhere),
        scratch_shapes=[
            pltpu.VMEM(table.shape, bf16),
            pltpu.VMEM((2, PACKED_LINKS, 2 * SITES), bf16),
            pltpu.SemaphoreType.DMA((29,)),
        ],
        compiler_params=params(8),
    )(eigvecs, table)
    received = swap(send, 1)
    own, other, edge = pl.pallas_call(
        join_kernel,
        out_shape=(package, package, jax.ShapeDtypeStruct((rows, vector_count), bf16)),
        in_specs=[anywhere] * 3,
        out_specs=(anywhere, anywhere, anywhere),
        scratch_shapes=[pltpu.SemaphoreType.DMA((3,))],
        input_output_aliases={1: 0, 2: 1},
        compiler_params=params(8),
    )(received, own, other)

    crossing, straight, outer = [], [], []
    for q in range(blocks):
        above, below = (q + 1) % blocks, (q + blocks - 1) % blocks
        for core in range(2):
            a, b = 4 * q + core, 4 * q + 2 + core
            crossing += [(b, 4 * above + core), (a, 4 * below + 2 + core)]
            straight += [(b, 4 * above + 2 + core), (a, 4 * below + core)]
            outer += [(a, 4 * above + core), (b, 4 * below + 2 + core)]
    across = swap(other, 2)
    second = lax.ppermute(own, "space", straight)
    first = lax.ppermute(other, "space", crossing)
    last = lax.ppermute(edge, "space", outer)

    small = pl.CostEstimate(flops=1024, bytes_accessed=1024, transcendentals=0)

    def field(count):
        return jax.ShapeDtypeStruct((count, FIELD, vector_count), bf16)

    def scratch(*shape):
        return pltpu.VMEM(shape, bf16)

    small = pl.CostEstimate(flops=1024, bytes_accessed=1024, transcendentals=0)
    site_scale = (6.0 * n * SITES) ** (-0.5)
    square = (vector_count, vector_count)
    running = jax.ShapeDtypeStruct((vector_count, 2 * vector_count), f32)

    def elemental(scale, groups, vector_pieces, packages, link_pieces, sums):
        ranks = sum(piece[2] for piece in vector_pieces)
        outputs = (running,)
        if scale is not None:
            outputs = (jax.ShapeDtypeStruct(square, f32), jax.ShapeDtypeStruct(square, bf16))
        operands = [part[0] for part in groups] + [part[1] for part in groups] + list(packages)
        return pl.pallas_call(
            functools.partial(elemental_kernel, scale, vector_pieces, link_pieces),
            out_shape=outputs,
            in_specs=[smem] + [vmem] * (len(operands) + len(sums)),
            out_specs=(vmem,) * len(outputs),
            scratch_shapes=[
                pltpu.VMEM((ranks, 2, FIELD, vector_count), bf16),
                pltpu.VMEM((ranks, PACKED_LINKS, 2 * SITES), bf16),
                pltpu.VMEM((ranks - 1, 2, FIELD, 2 * vector_count), bf16),
            ],
            compiler_params=params(16),
            cost_estimate=small,
        )(directions, *operands, *sums)

    def with_partner(part):
        return part, swap(part, 1)

    short = jax.ShapeDtypeStruct((FIELD, vector_count), f32)
    after_shape = jax.ShapeDtypeStruct((2 * FIELD, FIELD), bf16)
    within_shape = jax.ShapeDtypeStruct((2 * FIELD, 2 * FIELD), bf16)
    w_inner, u_inner, operator = pl.pallas_call(
        smear_inner,
        out_shape=(field(2), field(2), jax.ShapeDtypeStruct((2 * FIELD, 3 * FIELD), bf16)),
        in_specs=[anywhere] * 3,
        out_specs=(vmem,) * 3,
        scratch_shapes=[
            scratch(6, FIELD, vector_count),
            scratch(6, PACKED_LINKS, 2 * SITES),
            scratch(4, FIELD, vector_count),
            scratch(3, 2 * FIELD, 3 * FIELD),
            pltpu.SemaphoreType.DMA((6,)),
        ],
        compiler_params=params(24),
        cost_estimate=small,
    )(second, across, own)
    inner = with_partner(w_inner)
    prepared = pl.pallas_call(
        smear_prepare,
        out_shape=(short, short, within_shape),
        in_specs=[vmem] * 3,
        out_specs=(vmem,) * 3,
        scratch_shapes=[scratch(2, PACKED_LINKS, 2 * SITES)],
        compiler_params=params(12),
        cost_estimate=small,
    )(own, u_inner, operator)
    (sum_inner,) = elemental(None, (inner,), ((0, 0, 2),), (across,), ((0, 0, 2),), ())
    prepared, sum_inner = lax.optimization_barrier((prepared, sum_inner))
    w_middle, first_short, second_short, after = pl.pallas_call(
        smear_middle,
        out_shape=(field(2), short, short, after_shape),
        in_specs=[vmem] * 7,
        out_specs=(vmem,) * 4,
        scratch_shapes=[
            scratch(3, FIELD, vector_count),
            scratch(3, PACKED_LINKS, 2 * SITES),
            scratch(3, FIELD, vector_count),
            scratch(2 * FIELD, 3 * FIELD),
            scratch(2 * FIELD, 2 * FIELD),
            scratch(2 * FIELD, FIELD),
        ],
        compiler_params=params(20),
        cost_estimate=small,
    )(own, first, u_inner, operator, *prepared)
    middle = with_partner(w_middle)
    w_outer = pl.pallas_call(
        smear_outer,
        out_shape=jax.ShapeDtypeStruct((1, FIELD, vector_count), bf16),
        in_specs=[vmem] * 5,
        out_specs=vmem,
        scratch_shapes=[
            pltpu.VMEM((2, PACKED_LINKS, 2 * SITES), bf16),
            pltpu.VMEM((2 * FIELD, FIELD), bf16),
        ],
        compiler_params=params(8),
        cost_estimate=small,
    )(first, last, first_short, second_short, after)
    outer_part = with_partner(w_outer)
    (sum_middle,) = elemental(
        None, (inner, middle), ((0, 1, 1), (1, 0, 2)), (across, own), ((0, 1, 1), (1, 0, 2)), (sum_inner,)
    )
    partial, partial_low = elemental(
        site_scale, (middle, outer_part), ((0, 1, 1), (1, 0, 1)), (own, first), ((0, 1, 1), (1, 0, 1)), (sum_middle,)
    )

    bit = n // 2
    while bit >= 4:
        partner = bit if bit == 4 else bit + bit // 2
        partial = partial + swap(partial_low, partner).astype(f32)
        partial_low = partial.astype(bf16)
        bit //= 2
    other_slice = swap(partial_low, 2)
    other_copy = swap(partial_low, 1)
    other_both = swap(other_slice, 1)

    pair_scale = (2.0 * vector_count) ** (-0.5)
    owned_rows = vector_count // n
    big = 2 * vector_count
    return pl.pallas_call(
        functools.partial(pair_kernel, pair_scale),
        out_shape=(
            jax.ShapeDtypeStruct((slices, 2, 2, owned_rows, vector_count), f32),
            jax.ShapeDtypeStruct(perambulators.shape, bf16),
        ),
        in_specs=[smem] + [vmem] * 5,
        out_specs=(vmem, vmem),
        scratch_shapes=[
            pltpu.VMEM((slices, 2, 2, vector_count, vector_count), f32),
            pltpu.VMEM((slices, big, big), bf16),
            pltpu.VMEM((slices, big, big), bf16),
        ],
        compiler_params=params(16),
    )(pairs.T, partial_low, other_slice, other_copy, other_both, perambulators)


def solution(mesh):
    placed = (
        P("groups", None, None, "space", None, None),
        P("groups", None, None, None, None, "space", None),
        P("groups"),
        P(("groups", "space"), None),
        P(("groups", "space"), None, None, None),
    )
    return jax.shard_map(
        body,
        mesh=mesh,
        in_specs=placed,
        out_specs=(
            P("groups", None, None, "space", None),
            P(("groups", "space"), None, None, None),
        ),
        check_vma=False,
    )
```

```python
import functools

import jax
import jax.numpy as jnp
from jax import lax
from jax.experimental import pallas as pl
from jax.experimental.pallas import tpu as pltpu
from jax.sharding import PartitionSpec as P

LX = 16
LY = 8
SITES = LX * LY
COLORS = 3
FIELD = COLORS * SITES
LINK_ROWS = 54
PACKED_LINKS = 32
SMEAR = 0.12

bf16 = jnp.bfloat16
f32 = jnp.float32


def position():
    index = lax.axis_index("space")
    return lax.rem(index, 2), lax.rem(lax.div(index, 2), 2)


def whole_in_vmem():
    return pl.BlockSpec(memory_space=pltpu.VMEM)


def link_row(direction, part, row, column):
    return ((direction * COLORS + row) * COLORS + column) * 2 + part


def slot_of(core, chip, t):
    return core + (1 - 2 * core) * ((1 - chip) if t == 0 else chip)


def split_kernel(vectors, links_in, own, other, send, links, packed, sems):
    core, chip = position()
    half = vectors.shape[5] // 2
    arriving = pltpu.make_async_copy(links_in, links, sems.at[28])
    arriving.start()
    copies = []
    for t in range(2):
        for part in range(2):
            for color in range(COLORS):
                rows = pl.ds(color * SITES, SITES)
                lanes = pl.ds(part * half, half)
                near = pl.ds(pl.multiple_of(core * half, half), half)
                far = pl.ds(pl.multiple_of((1 - core) * half, half), half)
                block = vectors.at[chip + t * (1 - 2 * chip), part, color, 0]
                kept = (own, other)[t]
                for source, target in (
                    (block.at[:, near], kept.at[slot_of(core, chip, t), rows, lanes]),
                    (block.at[:, far], send.at[t, rows, lanes]),
                ):
                    copies.append(pltpu.make_async_copy(source, target, sems.at[len(copies)]))
                    copies[-1].start()
    arriving.wait()
    for t in range(2):
        table = links.at[chip + t * (1 - 2 * chip)]
        gathered = [
            table[d, row, column, 0].astype(f32)
            for d in range(3)
            for row in range(COLORS)
            for column in range(COLORS)
        ]
        gathered.append(jnp.zeros((2 * PACKED_LINKS - LINK_ROWS, SITES), f32))
        rows = jnp.concatenate(gathered, axis=0).astype(bf16)
        packed[t, :, pl.ds(0, SITES)] = rows[:PACKED_LINKS]
        packed[t, :, pl.ds(SITES, SITES)] = rows[PACKED_LINKS:]
        for target in ((own, other)[t].at[slot_of(core, chip, t)], send.at[t]):
            copies.append(
                pltpu.make_async_copy(
                    packed.at[t], target.at[pl.ds(FIELD, PACKED_LINKS)], sems.at[len(copies)]
                )
            )
            copies[-1].start()
    for copy in copies:
        copy.wait()


def join_kernel(received, own_in, other_in, own, other, edge, sems):
    core, chip = position()
    copies = [
        pltpu.make_async_copy(received.at[t], kept.at[1 - slot_of(core, chip, t)], sems.at[t])
        for t, kept in enumerate((own, other))
    ]
    for copy in copies:
        copy.start()
    here = slot_of(core, chip, 0) == 0
    kept_edge = pltpu.make_async_copy(own_in.at[0], edge, sems.at[2])
    received_edge = pltpu.make_async_copy(received.at[0], edge, sems.at[2])
    pl.when(here)(kept_edge.start)
    pl.when(jnp.logical_not(here))(received_edge.start)
    for copy in copies:
        copy.wait()
    kept_edge.wait()


def shift_y(row, lane):
    return jnp.where(
        lax.rem(lane, LY) == 0,
        pltpu.roll(row, SITES - (LY - 1), 1),
        pltpu.roll(row, 1, 1),
    )


def site_masks():
    row = lax.broadcasted_iota(jnp.int32, (SITES, SITES), 0)
    column = lax.broadcasted_iota(jnp.int32, (SITES, SITES), 1)
    y = lax.rem(row, LY)
    ahead_x = column == lax.rem(row + LY, SITES)
    behind_x = column == lax.rem(row + SITES - LY, SITES)
    ahead_y = column == row - y + lax.rem(y + 1, LY)
    behind_y = column == row - y + lax.rem(y + LY - 1, LY)
    return ahead_x, ahead_y, behind_x, behind_y, column == row


def link_planes(packed):
    return jnp.concatenate([packed[:, :SITES], packed[:, SITES:]], axis=0).astype(f32)


def fetch(copies, sems):
    started = [
        pltpu.make_async_copy(source, target, sems.at[k])
        for k, (source, target) in enumerate(copies)
    ]
    for copy in started:
        copy.start()
    for copy in started:
        copy.wait()


def field_of(package):
    return package.at[:, pl.ds(0, FIELD)]


def links_of(package):
    return package.at[:, pl.ds(FIELD, PACKED_LINKS)]


BEFORE, WITHIN, AFTER = range(3)


def build(operator, rims, at, pieces=(BEFORE, WITHIN, AFTER)):
    _, chip = position()
    ascending = chip == 1
    ahead_x, ahead_y, behind_x, behind_y, same = site_masks()
    table = link_planes(rims[at])
    if AFTER not in pieces:
        below = link_planes(rims[at - 1])
    elif BEFORE not in pieces:
        below = link_planes(rims[at + 1])
    else:
        below = link_planes(jnp.where(ascending, rims[at - 1], rims[at + 1]))
    lane = lax.broadcasted_iota(jnp.int32, table.shape, 1)
    from_x = pltpu.roll(table, LY, 1)
    from_y = shift_y(table, lane)

    def row_of(values, *what):
        k = link_row(*what)
        return values[k : k + 1]

    for part in range(2):
        sign = 1.0 if part == 0 else -1.0
        for i in range(COLORS):
            rows = pl.ds((part * COLORS + i) * SITES, SITES)
            for j in range(COLORS):
                zero = jnp.zeros((SITES, SITES), f32)
                lower = sign * row_of(below, 2, part, j, i)
                upper = row_of(table, 2, part, i, j)
                for k, piece in enumerate(pieces):
                    if piece == BEFORE:
                        block = jnp.where(same, jnp.where(ascending, lower, upper), zero)
                    elif piece == AFTER:
                        block = jnp.where(same, jnp.where(ascending, upper, lower), zero)
                    else:
                        block = jnp.where(ahead_x, row_of(from_x, 0, part, i, j), zero)
                        block = jnp.where(ahead_y, row_of(from_y, 1, part, i, j), block)
                        block = jnp.where(behind_x, sign * row_of(table, 0, part, j, i), block)
                        block = jnp.where(behind_y, sign * row_of(table, 1, part, j, i), block)
                    operator[rows, pl.ds((k * COLORS + j) * SITES, SITES)] = block.astype(bf16)


def weighted_hops(operator, planes):
    half = SITES
    window = planes.reshape(-1, 2 * half)
    product = jnp.dot(operator, window, preferred_element_type=f32)
    hops = jnp.concatenate(
        [
            product[:FIELD, :half] - product[FIELD:, half:],
            product[:FIELD, half:] + product[FIELD:, :half],
        ],
        axis=1,
    )
    return SMEAR * hops


def smeared(operator, source, at):
    center = (1.0 - 6.0 * SMEAR) * source[at].astype(f32)
    return (center + weighted_hops(operator[...], source[pl.ds(at - 1, 3)])).astype(bf16)


def smeared_short(operator, planes):
    center = (1.0 - 6.0 * SMEAR) * planes[1].astype(f32)
    return center + weighted_hops(operator, planes)


def smear_inner(second, across, own, w_out, u_out, operator_out, fields, rims, grown, operators, sems):
    copies = []
    for k, package in enumerate((second, across, own)):
        copies.append((field_of(package), fields.at[pl.ds(2 * k, 2)]))
        copies.append((links_of(package), rims.at[pl.ds(2 * k, 2)]))
    fetch(copies, sems)
    for r in range(1, 5):
        operator = operators.at[r - 1] if r < 4 else operator_out
        build(operator, rims, r)
        grown[r - 1] = smeared(operator, fields, r)
    for r in range(2, 4):
        w_out[r - 2] = smeared(operators.at[r - 1], grown, r - 1)
    u_out[...] = grown[2:4]


def smear_prepare(own, u_in, operator, first_short, second_short, within_out, rims):
    for k in range(2):
        rims[k] = own[k, pl.ds(FIELD, PACKED_LINKS)]
    build(within_out, rims, 1, (BEFORE, WITHIN))
    first_short[...] = smeared_short(within_out[...], own[:, pl.ds(0, FIELD)])
    second_short[...] = smeared_short(operator[:, pl.ds(0, 2 * FIELD)], u_in[...])


def smear_middle(
    own, first, u_in, operator_in, short_in, second_in, within_in, w_out, first_short, second_short, after_out, fields, rims, grown, operator, within, after
):
    fields[0] = own[1, pl.ds(0, FIELD)]
    rims[0] = own[1, pl.ds(FIELD, PACKED_LINKS)]
    for k in range(2):
        fields[1 + k] = first[k, pl.ds(0, FIELD)]
        rims[1 + k] = first[k, pl.ds(FIELD, PACKED_LINKS)]
    grown[0] = u_in[1]
    build(after, rims, 0, (AFTER,))
    grown[1] = (short_in[...] + weighted_hops(after[...], fields[1])).astype(bf16)
    build(operator, rims, 1)
    grown[2] = smeared(operator, fields, 1)
    w_out[0] = (second_in[...] + weighted_hops(operator_in[:, pl.ds(2 * FIELD, FIELD)], grown[1])).astype(bf16)
    short = smeared_short(within_in[...], grown[pl.ds(0, 2)])
    w_out[1] = (short + weighted_hops(after[...], grown[2])).astype(bf16)
    build(within, rims, 2, (BEFORE, WITHIN))
    first_short[...] = smeared_short(within[...], fields[pl.ds(1, 2)])
    second_short[...] = smeared_short(operator[:, pl.ds(0, 2 * FIELD)], grown[pl.ds(1, 2)])
    after_out[...] = operator[:, pl.ds(2 * FIELD, FIELD)]


def smear_outer(first, last, first_short, second_short, after, w_out, rims, operator):
    rims[0] = first[1, pl.ds(FIELD, PACKED_LINKS)]
    rims[1] = last[pl.ds(FIELD, PACKED_LINKS)]
    build(operator, rims, 0, (AFTER,))
    outer = last[pl.ds(0, FIELD)]
    grown = (first_short[...] + weighted_hops(operator[...], outer)).astype(bf16)
    w_out[0] = (second_short[...] + weighted_hops(after[...], grown)).astype(bf16)


def elemental_kernel(scale, vector_pieces, link_pieces, directions, *refs):
    groups = max(piece[0] for piece in vector_pieces) + 1
    packages = max(piece[0] for piece in link_pieces) + 1
    mine, theirs, refs = refs[:groups], refs[groups : 2 * groups], refs[2 * groups :]
    packages, refs = refs[:packages], refs[packages:]
    *sums, w, rims, right = refs
    core, chip = position()
    half = SITES
    at = 0
    for k, first, count in link_pieces:
        rims[pl.ds(at, count)] = packages[k][pl.ds(first, count), pl.ds(FIELD, PACKED_LINKS)]
        at += count
    for group, side in ((mine, core), (theirs, 1 - core)):
        lanes = pl.ds(pl.multiple_of(side * half, half), half)
        at = 0
        for k, first, count in vector_pieces:
            for part in range(2):
                w[pl.ds(at, count), part, :, lanes] = group[k][
                    pl.ds(first, count), :, pl.ds(part * half, half)
                ]
            at += count
    direction = directions[core]
    ahead_x, ahead_y, _, _, same = site_masks()
    one = jnp.ones((SITES, SITES), f32)
    zero = jnp.zeros((SITES, SITES), f32)
    is_x, is_y, is_z = direction == 0, direction == 1, direction == 2
    mask_x = jnp.where(ahead_x, one, zero)
    mask_y = jnp.where(ahead_y, one, zero)
    mask_z = jnp.where(same, one, zero)
    mask = jnp.where(is_x, mask_x, jnp.where(is_y, mask_y, mask_z))
    start = jnp.where(is_z, 1 - chip, 0)
    ahead = jnp.where(is_z, chip, 0)
    steps = w.shape[0] - 1

    for z in range(steps):
        table = link_planes(rims[z + start])
        lane = lax.broadcasted_iota(jnp.int32, table.shape, 1)
        count = 2 * COLORS * COLORS
        along_x = pltpu.roll(table, LY, 1)[:count]
        along_y = shift_y(table, lane)[count : 2 * count]
        along_z = table[2 * count : 3 * count]
        chosen = jnp.where(is_x, along_x, jnp.where(is_y, along_y, along_z))
        operator = jnp.concatenate(
            [
                jnp.concatenate(
                    [
                        (mask * chosen[k : k + 1]).astype(bf16)
                        for k in range(2 * COLORS * i + part, 2 * COLORS * (i + 1), 2)
                    ],
                    axis=1,
                )
                for part in range(2)
                for i in range(COLORS)
            ],
            axis=0,
        )
        source = z + ahead
        real = jnp.dot(operator, w[source, 0], preferred_element_type=f32)
        imag = jnp.dot(operator, w[source, 1], preferred_element_type=f32)
        hop_real = real[:FIELD] - imag[FIELD:]
        hop_imag = real[FIELD:] + imag[:FIELD]
        total = (hop_real + hop_imag).astype(bf16)
        rest = (hop_imag - hop_real).astype(bf16)
        vectors = 2 * half
        right[z, 0, :, pl.ds(0, vectors)] = total
        right[z, 0, :, pl.ds(vectors, vectors)] = rest
        right[z, 1, :, pl.ds(0, vectors)] = rest
        right[z, 1, :, pl.ds(vectors, vectors)] = -total
    vectors = 2 * half
    depth = steps * 2 * FIELD
    product = lax.dot_general(
        w[pl.ds(start, steps)].reshape(depth, vectors),
        right[...].reshape(depth, 2 * vectors),
        (((0,), (0,)), ((), ())),
        preferred_element_type=f32,
    )
    if scale is None:
        sums[-1][...] = product if len(sums) == 1 else product + sums[0][...]
        return
    before, out, out_low = sums
    product = product + before[...]
    packed = (product[:, :vectors] + product[:, vectors:].T) * scale
    out[...] = packed
    out_low[...] = packed.astype(bf16)


def pair_kernel(pair_scale, pairs, s00, s10, s01, s11, perambulators, elementals, out, parts, left, right):
    core, chip = position()
    index = lax.axis_index("space")
    size = s00.shape[0]
    rows = elementals.shape[3]
    own_rows = pl.ds(pl.multiple_of(index * rows, 8), rows)
    for ref, t, k in (
        (s00, chip, core),
        (s10, 1 - chip, core),
        (s01, chip, 1 - core),
        (s11, 1 - chip, 1 - core),
    ):
        packed = ref[...].astype(f32)
        turned = packed.T
        parts[t, k, 0] = 0.5 * (packed - turned)
        parts[t, k, 1] = 0.5 * (packed + turned)
    for t in range(2):
        for k in range(2):
            for part in range(2):
                elementals[t, k, part] = parts[t, k, part, own_rows]
        real, imag = parts[t, 0, 0].astype(bf16), parts[t, 0, 1].astype(bf16)
        left[t, :size, :size] = real
        left[t, :size, size:] = -imag
        left[t, size:, :size] = imag
        left[t, size:, size:] = real
        real, imag = parts[t, 1, 0].astype(bf16), parts[t, 1, 1].astype(bf16)
        right[t, :size, :size] = real
        right[t, :size, size:] = imag
        right[t, size:, :size] = -imag
        right[t, size:, size:] = real

    count = perambulators.shape[0]
    wide = []
    for p in range(count):
        propagator = perambulators[p].reshape(2 * size, size)
        first = jnp.dot(left[pairs[1, p]], propagator, preferred_element_type=f32).astype(bf16)
        wide.append(jnp.concatenate([first[:size], first[size:]], axis=1))
    both = []
    for p in range(count):
        second = jnp.dot(wide[p], right[pairs[0, p]], preferred_element_type=f32) * pair_scale
        second = second.astype(bf16)
        real, imag = second[:, :size], second[:, size:]
        both.append(jnp.concatenate([second, jnp.concatenate([imag, -real], axis=1)], axis=0))
    for p in range(count):
        turned = jnp.concatenate([perambulators[p, 0], perambulators[p, 1]], axis=1)
        third = lax.dot_general(
            both[p], turned, (((1,), (1,)), ((), ())), preferred_element_type=f32
        ).astype(bf16)
        out[p] = third.reshape(2, size, size)


def params(megabytes):
    return pltpu.CompilerParams(vmem_limit_bytes=megabytes * 1024 * 1024)


def body(eigvecs, links, directions, pairs, perambulators):
    slices = eigvecs.shape[0]
    vector_count = eigvecs.shape[5]
    n = lax.axis_size("space")
    blocks = n // 4
    vmem = whole_in_vmem()
    anywhere = pl.BlockSpec(memory_space=pl.ANY)
    hbm = pl.BlockSpec(memory_space=pltpu.HBM)
    smem = pl.BlockSpec(memory_space=pltpu.SMEM)
    table = jnp.transpose(links, (0, 1, 3, 4, 5, 2, 6))
    rows = FIELD + PACKED_LINKS

    def swap(value, bit):
        return lax.ppermute(value, "space", [(i, i ^ bit) for i in range(n)])

    package = jax.ShapeDtypeStruct((2, rows, vector_count), bf16)
    own, other, send = pl.pallas_call(
        split_kernel,
        out_shape=(package, package, package),
        in_specs=[hbm, hbm],
        out_specs=(anywhere, anywhere, anywhere),
        scratch_shapes=[
            pltpu.VMEM(table.shape, bf16),
            pltpu.VMEM((2, PACKED_LINKS, 2 * SITES), bf16),
            pltpu.SemaphoreType.DMA((29,)),
        ],
        compiler_params=params(8),
    )(eigvecs, table)
    received = swap(send, 1)
    own, other, edge = pl.pallas_call(
        join_kernel,
        out_shape=(package, package, jax.ShapeDtypeStruct((rows, vector_count), bf16)),
        in_specs=[anywhere] * 3,
        out_specs=(anywhere, anywhere, anywhere),
        scratch_shapes=[pltpu.SemaphoreType.DMA((3,))],
        input_output_aliases={1: 0, 2: 1},
        compiler_params=params(8),
    )(received, own, other)

    crossing, straight, outer = [], [], []
    for q in range(blocks):
        above, below = (q + 1) % blocks, (q + blocks - 1) % blocks
        for core in range(2):
            a, b = 4 * q + core, 4 * q + 2 + core
            crossing += [(b, 4 * above + core), (a, 4 * below + 2 + core)]
            straight += [(b, 4 * above + 2 + core), (a, 4 * below + core)]
            outer += [(a, 4 * above + core), (b, 4 * below + 2 + core)]
    across = swap(other, 2)
    second = lax.ppermute(own, "space", straight)
    first = lax.ppermute(other, "space", crossing)
    last = lax.ppermute(edge, "space", outer)

    small = pl.CostEstimate(flops=1024, bytes_accessed=1024, transcendentals=0)

    def field(count):
        return jax.ShapeDtypeStruct((count, FIELD, vector_count), bf16)

    def scratch(*shape):
        return pltpu.VMEM(shape, bf16)

    small = pl.CostEstimate(flops=1024, bytes_accessed=1024, transcendentals=0)
    site_scale = (6.0 * n * SITES) ** (-0.5)
    square = (vector_count, vector_count)
    running = jax.ShapeDtypeStruct((vector_count, 2 * vector_count), f32)

    def elemental(scale, groups, vector_pieces, packages, link_pieces, sums):
        ranks = sum(piece[2] for piece in vector_pieces)
        outputs = (running,)
        if scale is not None:
            outputs = (jax.ShapeDtypeStruct(square, f32), jax.ShapeDtypeStruct(square, bf16))
        operands = [part[0] for part in groups] + [part[1] for part in groups] + list(packages)
        return pl.pallas_call(
            functools.partial(elemental_kernel, scale, vector_pieces, link_pieces),
            out_shape=outputs,
            in_specs=[smem] + [vmem] * (len(operands) + len(sums)),
            out_specs=(vmem,) * len(outputs),
            scratch_shapes=[
                pltpu.VMEM((ranks, 2, FIELD, vector_count), bf16),
                pltpu.VMEM((ranks, PACKED_LINKS, 2 * SITES), bf16),
                pltpu.VMEM((ranks - 1, 2, FIELD, 2 * vector_count), bf16),
            ],
            compiler_params=params(16),
            cost_estimate=small,
        )(directions, *operands, *sums)

    def with_partner(part):
        return part, swap(part, 1)

    short = jax.ShapeDtypeStruct((FIELD, vector_count), f32)
    after_shape = jax.ShapeDtypeStruct((2 * FIELD, FIELD), bf16)
    within_shape = jax.ShapeDtypeStruct((2 * FIELD, 2 * FIELD), bf16)
    w_inner, u_inner, operator = pl.pallas_call(
        smear_inner,
        out_shape=(field(2), field(2), jax.ShapeDtypeStruct((2 * FIELD, 3 * FIELD), bf16)),
        in_specs=[anywhere] * 3,
        out_specs=(vmem,) * 3,
        scratch_shapes=[
            scratch(6, FIELD, vector_count),
            scratch(6, PACKED_LINKS, 2 * SITES),
            scratch(4, FIELD, vector_count),
            scratch(3, 2 * FIELD, 3 * FIELD),
            pltpu.SemaphoreType.DMA((6,)),
        ],
        compiler_params=params(24),
        cost_estimate=small,
    )(second, across, own)
    inner = with_partner(w_inner)
    prepared = pl.pallas_call(
        smear_prepare,
        out_shape=(short, short, within_shape),
        in_specs=[vmem] * 3,
        out_specs=(vmem,) * 3,
        scratch_shapes=[scratch(2, PACKED_LINKS, 2 * SITES)],
        compiler_params=params(12),
        cost_estimate=small,
    )(own, u_inner, operator)
    (sum_inner,) = elemental(None, (inner,), ((0, 0, 2),), (across,), ((0, 0, 2),), ())
    prepared, sum_inner = lax.optimization_barrier((prepared, sum_inner))
    w_middle, first_short, second_short, after = pl.pallas_call(
        smear_middle,
        out_shape=(field(2), short, short, after_shape),
        in_specs=[vmem] * 7,
        out_specs=(vmem,) * 4,
        scratch_shapes=[
            scratch(3, FIELD, vector_count),
            scratch(3, PACKED_LINKS, 2 * SITES),
            scratch(3, FIELD, vector_count),
            scratch(2 * FIELD, 3 * FIELD),
            scratch(2 * FIELD, 2 * FIELD),
            scratch(2 * FIELD, FIELD),
        ],
        compiler_params=params(20),
        cost_estimate=small,
    )(own, first, u_inner, operator, *prepared)
    middle = with_partner(w_middle)
    w_outer = pl.pallas_call(
        smear_outer,
        out_shape=jax.ShapeDtypeStruct((1, FIELD, vector_count), bf16),
        in_specs=[vmem] * 5,
        out_specs=vmem,
        scratch_shapes=[
            pltpu.VMEM((2, PACKED_LINKS, 2 * SITES), bf16),
            pltpu.VMEM((2 * FIELD, FIELD), bf16),
        ],
        compiler_params=params(8),
        cost_estimate=small,
    )(first, last, first_short, second_short, after)
    outer_part = with_partner(w_outer)
    (sum_middle,) = elemental(
        None, (inner, middle), ((0, 1, 1), (1, 0, 2)), (across, own), ((0, 1, 1), (1, 0, 2)), (sum_inner,)
    )
    partial, partial_low = elemental(
        site_scale, (middle, outer_part), ((0, 1, 1), (1, 0, 1)), (own, first), ((0, 1, 1), (1, 0, 1)), (sum_middle,)
    )

    bit = n // 2
    while bit >= 4:
        partner = bit if bit == 4 else bit + bit // 2
        partial = partial + swap(partial_low, partner).astype(f32)
        partial_low = partial.astype(bf16)
        bit //= 2
    other_slice = swap(partial_low, 2)
    other_copy = swap(partial_low, 1)
    other_both = swap(other_slice, 1)

    pair_scale = (2.0 * vector_count) ** (-0.5)
    owned_rows = vector_count // n
    big = 2 * vector_count
    return pl.pallas_call(
        functools.partial(pair_kernel, pair_scale),
        out_shape=(
            jax.ShapeDtypeStruct((slices, 2, 2, owned_rows, vector_count), f32),
            jax.ShapeDtypeStruct(perambulators.shape, bf16),
        ),
        in_specs=[smem] + [vmem] * 5,
        out_specs=(vmem, vmem),
        scratch_shapes=[
            pltpu.VMEM((slices, 2, 2, vector_count, vector_count), f32),
            pltpu.VMEM((slices, big, big), bf16),
            pltpu.VMEM((slices, big, big), bf16),
        ],
        compiler_params=params(16),
    )(pairs.T, partial_low, other_slice, other_copy, other_both, perambulators)


def solution(mesh):
    placed = (
        P("groups", None, None, "space", None, None),
        P("groups", None, None, None, None, "space", None),
        P("groups"),
        P(("groups", "space"), None),
        P(("groups", "space"), None, None, None),
    )
    return jax.shard_map(
        body,
        mesh=mesh,
        in_specs=placed,
        out_specs=(
            P("groups", None, None, "space", None),
            P(("groups", "space"), None, None, None),
        ),
        check_vma=False,
    )
```

```python
import functools

import jax
import jax.numpy as jnp
from jax import lax
from jax.experimental import pallas as pl
from jax.experimental.pallas import tpu as pltpu
from jax.sharding import PartitionSpec as P

LX = 16
LY = 8
SITES = LX * LY
COLORS = 3
FIELD = COLORS * SITES
LINK_ROWS = 54
PACKED_LINKS = 32
SMEAR = 0.12

bf16 = jnp.bfloat16
f32 = jnp.float32


def position():
    index = lax.axis_index("space")
    return lax.rem(index, 2), lax.rem(lax.div(index, 2), 2)


def whole_in_vmem():
    return pl.BlockSpec(memory_space=pltpu.VMEM)


def link_row(direction, part, row, column):
    return ((direction * COLORS + row) * COLORS + column) * 2 + part


def slot_of(core, chip, t):
    return core + (1 - 2 * core) * ((1 - chip) if t == 0 else chip)


def split_kernel(vectors, links, own, other, send):
    core, chip = position()
    half = vectors.shape[5] // 2
    for t, kept in enumerate((own, other)):
        time = chip + t * (1 - 2 * chip)
        slot = slot_of(core, chip, t)
        for part in range(2):
            for color in range(COLORS):
                rows = pl.ds(color * SITES, SITES)
                lanes = pl.ds(part * half, half)
                block = vectors[time, part, color, 0]
                low, high = block[:, :half], block[:, half:]
                kept[slot, rows, lanes] = jnp.where(core == 0, low, high)
                send[t, rows, lanes] = jnp.where(core == 0, high, low)
        gathered = [
            links[time, d, row, column, 0].astype(f32)
            for d in range(3)
            for row in range(COLORS)
            for column in range(COLORS)
        ]
        gathered.append(jnp.zeros((2 * PACKED_LINKS - LINK_ROWS, SITES), f32))
        packed = jnp.concatenate(gathered, axis=0).astype(bf16)
        rows = pl.ds(FIELD, PACKED_LINKS)
        for k in range(2):
            piece = packed[k * PACKED_LINKS : (k + 1) * PACKED_LINKS]
            kept[slot, rows, pl.ds(k * SITES, SITES)] = piece
            send[t, rows, pl.ds(k * SITES, SITES)] = piece


def join_kernel(received, own_in, other_in, own, other, edge):
    core, chip = position()
    slot = slot_of(core, chip, 0)
    own[slot] = own_in[slot]
    own[1 - slot] = received[0]
    edge[...] = jnp.where(slot == 0, own_in[0], received[0])
    slot = slot_of(core, chip, 1)
    other[slot] = other_in[slot]
    other[1 - slot] = received[1]


def shift_y(row, lane):
    return jnp.where(
        lax.rem(lane, LY) == 0,
        pltpu.roll(row, SITES - (LY - 1), 1),
        pltpu.roll(row, 1, 1),
    )


def site_masks():
    row = lax.broadcasted_iota(jnp.int32, (SITES, SITES), 0)
    column = lax.broadcasted_iota(jnp.int32, (SITES, SITES), 1)
    y = lax.rem(row, LY)
    ahead_x = column == lax.rem(row + LY, SITES)
    behind_x = column == lax.rem(row + SITES - LY, SITES)
    ahead_y = column == row - y + lax.rem(y + 1, LY)
    behind_y = column == row - y + lax.rem(y + LY - 1, LY)
    return ahead_x, ahead_y, behind_x, behind_y, column == row


def link_planes(packed):
    return jnp.concatenate([packed[:, :SITES], packed[:, SITES:]], axis=0).astype(f32)


def fetch(copies, sems):
    started = [
        pltpu.make_async_copy(source, target, sems.at[k])
        for k, (source, target) in enumerate(copies)
    ]
    for copy in started:
        copy.start()
    for copy in started:
        copy.wait()


def field_of(package):
    return package.at[:, pl.ds(0, FIELD)]


def links_of(package):
    return package.at[:, pl.ds(FIELD, PACKED_LINKS)]


BEFORE, WITHIN, AFTER = range(3)


def build(operator, rims, at, pieces=(BEFORE, WITHIN, AFTER)):
    _, chip = position()
    ascending = chip == 1
    ahead_x, ahead_y, behind_x, behind_y, same = site_masks()
    table = link_planes(rims[at])
    if AFTER not in pieces:
        below = link_planes(rims[at - 1])
    elif BEFORE not in pieces:
        below = link_planes(rims[at + 1])
    else:
        below = link_planes(jnp.where(ascending, rims[at - 1], rims[at + 1]))
    lane = lax.broadcasted_iota(jnp.int32, table.shape, 1)
    from_x = pltpu.roll(table, LY, 1)
    from_y = shift_y(table, lane)

    def row_of(values, *what):
        k = link_row(*what)
        return values[k : k + 1]

    for part in range(2):
        sign = 1.0 if part == 0 else -1.0
        for i in range(COLORS):
            rows = pl.ds((part * COLORS + i) * SITES, SITES)
            for j in range(COLORS):
                zero = jnp.zeros((SITES, SITES), f32)
                lower = sign * row_of(below, 2, part, j, i)
                upper = row_of(table, 2, part, i, j)
                for k, piece in enumerate(pieces):
                    if piece == BEFORE:
                        block = jnp.where(same, jnp.where(ascending, lower, upper), zero)
                    elif piece == AFTER:
                        block = jnp.where(same, jnp.where(ascending, upper, lower), zero)
                    else:
                        block = jnp.where(ahead_x, row_of(from_x, 0, part, i, j), zero)
                        block = jnp.where(ahead_y, row_of(from_y, 1, part, i, j), block)
                        block = jnp.where(behind_x, sign * row_of(table, 0, part, j, i), block)
                        block = jnp.where(behind_y, sign * row_of(table, 1, part, j, i), block)
                    operator[rows, pl.ds((k * COLORS + j) * SITES, SITES)] = block.astype(bf16)


def weighted_hops(operator, planes):
    half = SITES
    window = planes.reshape(-1, 2 * half)
    product = jnp.dot(operator, window, preferred_element_type=f32)
    hops = jnp.concatenate(
        [
            product[:FIELD, :half] - product[FIELD:, half:],
            product[:FIELD, half:] + product[FIELD:, :half],
        ],
        axis=1,
    )
    return SMEAR * hops


def smeared(operator, source, at):
    center = (1.0 - 6.0 * SMEAR) * source[at].astype(f32)
    return (center + weighted_hops(operator[...], source[pl.ds(at - 1, 3)])).astype(bf16)


def smeared_short(operator, planes):
    center = (1.0 - 6.0 * SMEAR) * planes[1].astype(f32)
    return center + weighted_hops(operator, planes)


def smear_inner(second, across, own, w_out, u_out, operator_out, fields, rims, grown, operators, sems):
    copies = []
    for k, package in enumerate((second, across, own)):
        copies.append((field_of(package), fields.at[pl.ds(2 * k, 2)]))
        copies.append((links_of(package), rims.at[pl.ds(2 * k, 2)]))
    fetch(copies, sems)
    for r in range(1, 5):
        operator = operators.at[r - 1] if r < 4 else operator_out
        build(operator, rims, r)
        grown[r - 1] = smeared(operator, fields, r)
    for r in range(2, 4):
        w_out[r - 2] = smeared(operators.at[r - 1], grown, r - 1)
    u_out[...] = grown[2:4]


def smear_prepare(own, u_in, operator, first_short, second_short, within_out, rims):
    for k in range(2):
        rims[k] = own[k, pl.ds(FIELD, PACKED_LINKS)]
    build(within_out, rims, 1, (BEFORE, WITHIN))
    first_short[...] = smeared_short(within_out[...], own[:, pl.ds(0, FIELD)])
    second_short[...] = smeared_short(operator[:, pl.ds(0, 2 * FIELD)], u_in[...])


def smear_middle(
    own, first, u_in, operator_in, short_in, second_in, within_in, w_out, first_short, second_short, after_out, fields, rims, grown, operator, within, after
):
    fields[0] = own[1, pl.ds(0, FIELD)]
    rims[0] = own[1, pl.ds(FIELD, PACKED_LINKS)]
    for k in range(2):
        fields[1 + k] = first[k, pl.ds(0, FIELD)]
        rims[1 + k] = first[k, pl.ds(FIELD, PACKED_LINKS)]
    grown[0] = u_in[1]
    build(after, rims, 0, (AFTER,))
    grown[1] = (short_in[...] + weighted_hops(after[...], fields[1])).astype(bf16)
    build(operator, rims, 1)
    grown[2] = smeared(operator, fields, 1)
    w_out[0] = (second_in[...] + weighted_hops(operator_in[:, pl.ds(2 * FIELD, FIELD)], grown[1])).astype(bf16)
    short = smeared_short(within_in[...], grown[pl.ds(0, 2)])
    w_out[1] = (short + weighted_hops(after[...], grown[2])).astype(bf16)
    build(within, rims, 2, (BEFORE, WITHIN))
    first_short[...] = smeared_short(within[...], fields[pl.ds(1, 2)])
    second_short[...] = smeared_short(operator[:, pl.ds(0, 2 * FIELD)], grown[pl.ds(1, 2)])
    after_out[...] = operator[:, pl.ds(2 * FIELD, FIELD)]


def smear_outer(first, last, first_short, second_short, after, w_out, rims, operator):
    rims[0] = first[1, pl.ds(FIELD, PACKED_LINKS)]
    rims[1] = last[pl.ds(FIELD, PACKED_LINKS)]
    build(operator, rims, 0, (AFTER,))
    outer = last[pl.ds(0, FIELD)]
    grown = (first_short[...] + weighted_hops(operator[...], outer)).astype(bf16)
    w_out[0] = (second_short[...] + weighted_hops(after[...], grown)).astype(bf16)


def elemental_kernel(scale, vector_pieces, link_pieces, directions, *refs):
    groups = max(piece[0] for piece in vector_pieces) + 1
    packages = max(piece[0] for piece in link_pieces) + 1
    mine, theirs, refs = refs[:groups], refs[groups : 2 * groups], refs[2 * groups :]
    packages, refs = refs[:packages], refs[packages:]
    *sums, w, rims, right = refs
    core, chip = position()
    half = SITES
    at = 0
    for k, first, count in link_pieces:
        rims[pl.ds(at, count)] = packages[k][pl.ds(first, count), pl.ds(FIELD, PACKED_LINKS)]
        at += count
    for group, side in ((mine, core), (theirs, 1 - core)):
        lanes = pl.ds(pl.multiple_of(side * half, half), half)
        at = 0
        for k, first, count in vector_pieces:
            for part in range(2):
                w[pl.ds(at, count), part, :, lanes] = group[k][
                    pl.ds(first, count), :, pl.ds(part * half, half)
                ]
            at += count
    direction = directions[core]
    ahead_x, ahead_y, _, _, same = site_masks()
    one = jnp.ones((SITES, SITES), f32)
    zero = jnp.zeros((SITES, SITES), f32)
    is_x, is_y, is_z = direction == 0, direction == 1, direction == 2
    mask_x = jnp.where(ahead_x, one, zero)
    mask_y = jnp.where(ahead_y, one, zero)
    mask_z = jnp.where(same, one, zero)
    mask = jnp.where(is_x, mask_x, jnp.where(is_y, mask_y, mask_z))
    start = jnp.where(is_z, 1 - chip, 0)
    ahead = jnp.where(is_z, chip, 0)
    steps = w.shape[0] - 1

    for z in range(steps):
        table = link_planes(rims[z + start])
        lane = lax.broadcasted_iota(jnp.int32, table.shape, 1)
        count = 2 * COLORS * COLORS
        along_x = pltpu.roll(table, LY, 1)[:count]
        along_y = shift_y(table, lane)[count : 2 * count]
        along_z = table[2 * count : 3 * count]
        chosen = jnp.where(is_x, along_x, jnp.where(is_y, along_y, along_z))
        operator = jnp.concatenate(
            [
                jnp.concatenate(
                    [
                        (mask * chosen[k : k + 1]).astype(bf16)
                        for k in range(2 * COLORS * i + part, 2 * COLORS * (i + 1), 2)
                    ],
                    axis=1,
                )
                for part in range(2)
                for i in range(COLORS)
            ],
            axis=0,
        )
        source = z + ahead
        real = jnp.dot(operator, w[source, 0], preferred_element_type=f32)
        imag = jnp.dot(operator, w[source, 1], preferred_element_type=f32)
        hop_real = real[:FIELD] - imag[FIELD:]
        hop_imag = real[FIELD:] + imag[:FIELD]
        total = (hop_real + hop_imag).astype(bf16)
        rest = (hop_imag - hop_real).astype(bf16)
        vectors = 2 * half
        right[z, 0, :, pl.ds(0, vectors)] = total
        right[z, 0, :, pl.ds(vectors, vectors)] = rest
        right[z, 1, :, pl.ds(0, vectors)] = rest
        right[z, 1, :, pl.ds(vectors, vectors)] = -total
    vectors = 2 * half
    depth = steps * 2 * FIELD
    product = lax.dot_general(
        w[pl.ds(start, steps)].reshape(depth, vectors),
        right[...].reshape(depth, 2 * vectors),
        (((0,), (0,)), ((), ())),
        preferred_element_type=f32,
    )
    if scale is None:
        sums[-1][...] = product if len(sums) == 1 else product + sums[0][...]
        return
    before, out, out_low = sums
    product = product + before[...]
    packed = (product[:, :vectors] + product[:, vectors:].T) * scale
    out[...] = packed
    out_low[...] = packed.astype(bf16)


def pair_kernel(pair_scale, pairs, s00, s10, s01, s11, perambulators, elementals, out, parts, left, right):
    core, chip = position()
    index = lax.axis_index("space")
    size = s00.shape[0]
    rows = elementals.shape[3]
    own_rows = pl.ds(pl.multiple_of(index * rows, 8), rows)
    for ref, t, k in (
        (s00, chip, core),
        (s10, 1 - chip, core),
        (s01, chip, 1 - core),
        (s11, 1 - chip, 1 - core),
    ):
        packed = ref[...].astype(f32)
        turned = packed.T
        parts[t, k, 0] = 0.5 * (packed - turned)
        parts[t, k, 1] = 0.5 * (packed + turned)
    for t in range(2):
        for k in range(2):
            for part in range(2):
                elementals[t, k, part] = parts[t, k, part, own_rows]
        real, imag = parts[t, 0, 0].astype(bf16), parts[t, 0, 1].astype(bf16)
        left[t, :size, :size] = real
        left[t, :size, size:] = -imag
        left[t, size:, :size] = imag
        left[t, size:, size:] = real
        real, imag = parts[t, 1, 0].astype(bf16), parts[t, 1, 1].astype(bf16)
        right[t, :size, :size] = real
        right[t, :size, size:] = imag
        right[t, size:, :size] = -imag
        right[t, size:, size:] = real

    count = perambulators.shape[0]
    wide = []
    for p in range(count):
        propagator = perambulators[p].reshape(2 * size, size)
        first = jnp.dot(left[pairs[1, p]], propagator, preferred_element_type=f32).astype(bf16)
        wide.append(jnp.concatenate([first[:size], first[size:]], axis=1))
    both = []
    for p in range(count):
        second = jnp.dot(wide[p], right[pairs[0, p]], preferred_element_type=f32) * pair_scale
        second = second.astype(bf16)
        real, imag = second[:, :size], second[:, size:]
        both.append(jnp.concatenate([second, jnp.concatenate([imag, -real], axis=1)], axis=0))
    for p in range(count):
        turned = jnp.concatenate([perambulators[p, 0], perambulators[p, 1]], axis=1)
        third = lax.dot_general(
            both[p], turned, (((1,), (1,)), ((), ())), preferred_element_type=f32
        ).astype(bf16)
        out[p] = third.reshape(2, size, size)


def params(megabytes):
    return pltpu.CompilerParams(vmem_limit_bytes=megabytes * 1024 * 1024)


def body(eigvecs, links, directions, pairs, perambulators):
    slices = eigvecs.shape[0]
    vector_count = eigvecs.shape[5]
    n = lax.axis_size("space")
    blocks = n // 4
    vmem = whole_in_vmem()
    anywhere = pl.BlockSpec(memory_space=pl.ANY)
    smem = pl.BlockSpec(memory_space=pltpu.SMEM)
    table = jnp.transpose(links, (0, 1, 3, 4, 5, 2, 6))
    rows = FIELD + PACKED_LINKS

    def swap(value, bit):
        return lax.ppermute(value, "space", [(i, i ^ bit) for i in range(n)])

    package = jax.ShapeDtypeStruct((2, rows, vector_count), bf16)
    own, other, send = pl.pallas_call(
        split_kernel,
        out_shape=(package, package, package),
        in_specs=[vmem] * 2,
        out_specs=(vmem,) * 3,
        compiler_params=params(8),
    )(eigvecs, table)
    received = swap(send, 1)
    own, other, edge = pl.pallas_call(
        join_kernel,
        out_shape=(package, package, jax.ShapeDtypeStruct((rows, vector_count), bf16)),
        in_specs=[vmem] * 3,
        out_specs=(vmem,) * 3,
        compiler_params=params(8),
    )(received, own, other)

    crossing, straight, outer = [], [], []
    for q in range(blocks):
        above, below = (q + 1) % blocks, (q + blocks - 1) % blocks
        for core in range(2):
            a, b = 4 * q + core, 4 * q + 2 + core
            crossing += [(b, 4 * above + core), (a, 4 * below + 2 + core)]
            straight += [(b, 4 * above + 2 + core), (a, 4 * below + core)]
            outer += [(a, 4 * above + core), (b, 4 * below + 2 + core)]
    across = swap(other, 2)
    second = lax.ppermute(own, "space", straight)
    first = lax.ppermute(other, "space", crossing)
    last = lax.ppermute(edge, "space", outer)

    small = pl.CostEstimate(flops=1024, bytes_accessed=1024, transcendentals=0)

    def field(count):
        return jax.ShapeDtypeStruct((count, FIELD, vector_count), bf16)

    def scratch(*shape):
        return pltpu.VMEM(shape, bf16)

    small = pl.CostEstimate(flops=1024, bytes_accessed=1024, transcendentals=0)
    site_scale = (6.0 * n * SITES) ** (-0.5)
    square = (vector_count, vector_count)
    running = jax.ShapeDtypeStruct((vector_count, 2 * vector_count), f32)

    def elemental(scale, groups, vector_pieces, packages, link_pieces, sums):
        ranks = sum(piece[2] for piece in vector_pieces)
        outputs = (running,)
        if scale is not None:
            outputs = (jax.ShapeDtypeStruct(square, f32), jax.ShapeDtypeStruct(square, bf16))
        operands = [part[0] for part in groups] + [part[1] for part in groups] + list(packages)
        return pl.pallas_call(
            functools.partial(elemental_kernel, scale, vector_pieces, link_pieces),
            out_shape=outputs,
            in_specs=[smem] + [vmem] * (len(operands) + len(sums)),
            out_specs=(vmem,) * len(outputs),
            scratch_shapes=[
                pltpu.VMEM((ranks, 2, FIELD, vector_count), bf16),
                pltpu.VMEM((ranks, PACKED_LINKS, 2 * SITES), bf16),
                pltpu.VMEM((ranks - 1, 2, FIELD, 2 * vector_count), bf16),
            ],
            compiler_params=params(16),
            cost_estimate=small,
        )(directions, *operands, *sums)

    def with_partner(part):
        return part, swap(part, 1)

    short = jax.ShapeDtypeStruct((FIELD, vector_count), f32)
    after_shape = jax.ShapeDtypeStruct((2 * FIELD, FIELD), bf16)
    within_shape = jax.ShapeDtypeStruct((2 * FIELD, 2 * FIELD), bf16)
    w_inner, u_inner, operator = pl.pallas_call(
        smear_inner,
        out_shape=(field(2), field(2), jax.ShapeDtypeStruct((2 * FIELD, 3 * FIELD), bf16)),
        in_specs=[anywhere] * 3,
        out_specs=(vmem,) * 3,
        scratch_shapes=[
            scratch(6, FIELD, vector_count),
            scratch(6, PACKED_LINKS, 2 * SITES),
            scratch(4, FIELD, vector_count),
            scratch(3, 2 * FIELD, 3 * FIELD),
            pltpu.SemaphoreType.DMA((6,)),
        ],
        compiler_params=params(24),
        cost_estimate=small,
    )(second, across, own)
    inner = with_partner(w_inner)
    prepared = pl.pallas_call(
        smear_prepare,
        out_shape=(short, short, within_shape),
        in_specs=[vmem] * 3,
        out_specs=(vmem,) * 3,
        scratch_shapes=[scratch(2, PACKED_LINKS, 2 * SITES)],
        compiler_params=params(12),
        cost_estimate=small,
    )(own, u_inner, operator)
    (sum_inner,) = elemental(None, (inner,), ((0, 0, 2),), (across,), ((0, 0, 2),), ())
    prepared, sum_inner = lax.optimization_barrier((prepared, sum_inner))
    w_middle, first_short, second_short, after = pl.pallas_call(
        smear_middle,
        out_shape=(field(2), short, short, after_shape),
        in_specs=[vmem] * 7,
        out_specs=(vmem,) * 4,
        scratch_shapes=[
            scratch(3, FIELD, vector_count),
            scratch(3, PACKED_LINKS, 2 * SITES),
            scratch(3, FIELD, vector_count),
            scratch(2 * FIELD, 3 * FIELD),
            scratch(2 * FIELD, 2 * FIELD),
            scratch(2 * FIELD, FIELD),
        ],
        compiler_params=params(20),
        cost_estimate=small,
    )(own, first, u_inner, operator, *prepared)
    middle = with_partner(w_middle)
    w_outer = pl.pallas_call(
        smear_outer,
        out_shape=jax.ShapeDtypeStruct((1, FIELD, vector_count), bf16),
        in_specs=[vmem] * 5,
        out_specs=vmem,
        scratch_shapes=[
            pltpu.VMEM((2, PACKED_LINKS, 2 * SITES), bf16),
            pltpu.VMEM((2 * FIELD, FIELD), bf16),
        ],
        compiler_params=params(8),
        cost_estimate=small,
    )(first, last, first_short, second_short, after)
    outer_part = with_partner(w_outer)
    (sum_middle,) = elemental(
        None, (inner, middle), ((0, 1, 1), (1, 0, 2)), (across, own), ((0, 1, 1), (1, 0, 2)), (sum_inner,)
    )
    partial, partial_low = elemental(
        site_scale, (middle, outer_part), ((0, 1, 1), (1, 0, 1)), (own, first), ((0, 1, 1), (1, 0, 1)), (sum_middle,)
    )

    bit = n // 2
    while bit >= 4:
        partner = bit if bit == 4 else bit + bit // 2
        partial = partial + swap(partial_low, partner).astype(f32)
        partial_low = partial.astype(bf16)
        bit //= 2
    other_slice = swap(partial_low, 2)
    other_copy = swap(partial_low, 1)
    other_both = swap(other_slice, 1)

    pair_scale = (2.0 * vector_count) ** (-0.5)
    owned_rows = vector_count // n
    big = 2 * vector_count
    return pl.pallas_call(
        functools.partial(pair_kernel, pair_scale),
        out_shape=(
            jax.ShapeDtypeStruct((slices, 2, 2, owned_rows, vector_count), f32),
            jax.ShapeDtypeStruct(perambulators.shape, bf16),
        ),
        in_specs=[smem] + [vmem] * 5,
        out_specs=(vmem, vmem),
        scratch_shapes=[
            pltpu.VMEM((slices, 2, 2, vector_count, vector_count), f32),
            pltpu.VMEM((slices, big, big), bf16),
            pltpu.VMEM((slices, big, big), bf16),
        ],
        compiler_params=params(16),
    )(pairs.T, partial_low, other_slice, other_copy, other_both, perambulators)


def solution(mesh):
    placed = (
        P("groups", None, None, "space", None, None),
        P("groups", None, None, None, None, "space", None),
        P("groups"),
        P(("groups", "space"), None),
        P(("groups", "space"), None, None, None),
    )
    return jax.shard_map(
        body,
        mesh=mesh,
        in_specs=placed,
        out_specs=(
            P("groups", None, None, "space", None),
            P(("groups", "space"), None, None, None),
        ),
        check_vma=False,
    )
```

```python
import functools

import jax
import jax.numpy as jnp
from jax import lax
from jax.experimental import pallas as pl
from jax.experimental.pallas import tpu as pltpu
from jax.sharding import PartitionSpec as P

LX = 16
LY = 8
SITES = LX * LY
COLORS = 3
FIELD = COLORS * SITES
LINK_ROWS = 54
PACKED_LINKS = 32
SMEAR = 0.12

bf16 = jnp.bfloat16
f32 = jnp.float32


def position():
    index = lax.axis_index("space")
    return lax.rem(index, 2), lax.rem(lax.div(index, 2), 2)


def whole_in_vmem():
    return pl.BlockSpec(memory_space=pltpu.VMEM)


def link_row(direction, part, row, column):
    return ((direction * COLORS + row) * COLORS + column) * 2 + part


def slot_of(core, chip, t):
    return core + (1 - 2 * core) * ((1 - chip) if t == 0 else chip)


def split_kernel(vectors, links, own, other, send):
    core, chip = position()
    half = vectors.shape[5] // 2
    for t, kept in enumerate((own, other)):
        time = chip + t * (1 - 2 * chip)
        slot = slot_of(core, chip, t)
        for part in range(2):
            for color in range(COLORS):
                rows = pl.ds(color * SITES, SITES)
                lanes = pl.ds(part * half, half)
                block = vectors[time, part, color, 0]
                low, high = block[:, :half], block[:, half:]
                kept[slot, rows, lanes] = jnp.where(core == 0, low, high)
                send[t, rows, lanes] = jnp.where(core == 0, high, low)
        gathered = [
            links[time, d, row, column, 0].astype(f32)
            for d in range(3)
            for row in range(COLORS)
            for column in range(COLORS)
        ]
        gathered.append(jnp.zeros((2 * PACKED_LINKS - LINK_ROWS, SITES), f32))
        packed = jnp.concatenate(gathered, axis=0).astype(bf16)
        rows = pl.ds(FIELD, PACKED_LINKS)
        for k in range(2):
            piece = packed[k * PACKED_LINKS : (k + 1) * PACKED_LINKS]
            kept[slot, rows, pl.ds(k * SITES, SITES)] = piece
            send[t, rows, pl.ds(k * SITES, SITES)] = piece


def join_kernel(received, own_in, other_in, own, other, edge):
    core, chip = position()
    slot = slot_of(core, chip, 0)
    own[slot] = own_in[slot]
    own[1 - slot] = received[0]
    edge[...] = jnp.where(slot == 0, own_in[0], received[0])
    slot = slot_of(core, chip, 1)
    other[slot] = other_in[slot]
    other[1 - slot] = received[1]


def shift_y(row, lane):
    return jnp.where(
        lax.rem(lane, LY) == 0,
        pltpu.roll(row, SITES - (LY - 1), 1),
        pltpu.roll(row, 1, 1),
    )


def site_masks():
    row = lax.broadcasted_iota(jnp.int32, (SITES, SITES), 0)
    column = lax.broadcasted_iota(jnp.int32, (SITES, SITES), 1)
    y = lax.rem(row, LY)
    ahead_x = column == lax.rem(row + LY, SITES)
    behind_x = column == lax.rem(row + SITES - LY, SITES)
    ahead_y = column == row - y + lax.rem(y + 1, LY)
    behind_y = column == row - y + lax.rem(y + LY - 1, LY)
    return ahead_x, ahead_y, behind_x, behind_y, column == row


def link_planes(packed):
    return jnp.concatenate([packed[:, :SITES], packed[:, SITES:]], axis=0).astype(f32)


def fetch(copies, sems):
    started = [
        pltpu.make_async_copy(source, target, sems.at[k])
        for k, (source, target) in enumerate(copies)
    ]
    for copy in started:
        copy.start()
    for copy in started:
        copy.wait()


def field_of(package):
    return package.at[:, pl.ds(0, FIELD)]


def links_of(package):
    return package.at[:, pl.ds(FIELD, PACKED_LINKS)]


BEFORE, WITHIN, AFTER = range(3)


def build(operator, rims, at, pieces=(BEFORE, WITHIN, AFTER)):
    _, chip = position()
    ascending = chip == 1
    ahead_x, ahead_y, behind_x, behind_y, same = site_masks()
    table = link_planes(rims[at])
    if AFTER not in pieces:
        below = link_planes(rims[at - 1])
    elif BEFORE not in pieces:
        below = link_planes(rims[at + 1])
    else:
        below = link_planes(jnp.where(ascending, rims[at - 1], rims[at + 1]))
    lane = lax.broadcasted_iota(jnp.int32, table.shape, 1)
    from_x = pltpu.roll(table, LY, 1)
    from_y = shift_y(table, lane)

    def row_of(values, *what):
        k = link_row(*what)
        return values[k : k + 1]

    for part in range(2):
        sign = 1.0 if part == 0 else -1.0
        for i in range(COLORS):
            rows = pl.ds((part * COLORS + i) * SITES, SITES)
            for j in range(COLORS):
                zero = jnp.zeros((SITES, SITES), f32)
                lower = sign * row_of(below, 2, part, j, i)
                upper = row_of(table, 2, part, i, j)
                for k, piece in enumerate(pieces):
                    if piece == BEFORE:
                        block = jnp.where(same, jnp.where(ascending, lower, upper), zero)
                    elif piece == AFTER:
                        block = jnp.where(same, jnp.where(ascending, upper, lower), zero)
                    else:
                        block = jnp.where(ahead_x, row_of(from_x, 0, part, i, j), zero)
                        block = jnp.where(ahead_y, row_of(from_y, 1, part, i, j), block)
                        block = jnp.where(behind_x, sign * row_of(table, 0, part, j, i), block)
                        block = jnp.where(behind_y, sign * row_of(table, 1, part, j, i), block)
                    operator[rows, pl.ds((k * COLORS + j) * SITES, SITES)] = block.astype(bf16)


def weighted_hops(operator, planes):
    half = SITES
    window = planes.reshape(-1, 2 * half)
    product = jnp.dot(operator, window, preferred_element_type=f32)
    hops = jnp.concatenate(
        [
            product[:FIELD, :half] - product[FIELD:, half:],
            product[:FIELD, half:] + product[FIELD:, :half],
        ],
        axis=1,
    )
    return SMEAR * hops


def smeared(operator, source, at):
    center = (1.0 - 6.0 * SMEAR) * source[at].astype(f32)
    return (center + weighted_hops(operator[...], source[pl.ds(at - 1, 3)])).astype(bf16)


def smeared_short(operator, planes):
    center = (1.0 - 6.0 * SMEAR) * planes[1].astype(f32)
    return center + weighted_hops(operator, planes)


def smear_inner(second, across, own, w_out, u_out, operator_out, fields, rims, grown, operators):
    for k, package in enumerate((second, across, own)):
        fields[pl.ds(2 * k, 2)] = package[:, pl.ds(0, FIELD)]
        rims[pl.ds(2 * k, 2)] = package[:, pl.ds(FIELD, PACKED_LINKS)]
    for r in range(1, 5):
        operator = operators.at[r - 1] if r < 4 else operator_out
        build(operator, rims, r)
        grown[r - 1] = smeared(operator, fields, r)
    for r in range(2, 4):
        w_out[r - 2] = smeared(operators.at[r - 1], grown, r - 1)
    u_out[...] = grown[2:4]


def smear_prepare(own, u_in, operator, first_short, second_short, within_out, rims):
    for k in range(2):
        rims[k] = own[k, pl.ds(FIELD, PACKED_LINKS)]
    build(within_out, rims, 1, (BEFORE, WITHIN))
    first_short[...] = smeared_short(within_out[...], own[:, pl.ds(0, FIELD)])
    second_short[...] = smeared_short(operator[:, pl.ds(0, 2 * FIELD)], u_in[...])


def smear_middle(
    own, first, u_in, operator_in, short_in, second_in, within_in, w_out, first_short, second_short, after_out, fields, rims, grown, operator, within, after
):
    fields[0] = own[1, pl.ds(0, FIELD)]
    rims[0] = own[1, pl.ds(FIELD, PACKED_LINKS)]
    for k in range(2):
        fields[1 + k] = first[k, pl.ds(0, FIELD)]
        rims[1 + k] = first[k, pl.ds(FIELD, PACKED_LINKS)]
    grown[0] = u_in[1]
    build(after, rims, 0, (AFTER,))
    grown[1] = (short_in[...] + weighted_hops(after[...], fields[1])).astype(bf16)
    build(operator, rims, 1)
    grown[2] = smeared(operator, fields, 1)
    w_out[0] = (second_in[...] + weighted_hops(operator_in[:, pl.ds(2 * FIELD, FIELD)], grown[1])).astype(bf16)
    short = smeared_short(within_in[...], grown[pl.ds(0, 2)])
    w_out[1] = (short + weighted_hops(after[...], grown[2])).astype(bf16)
    build(within, rims, 2, (BEFORE, WITHIN))
    first_short[...] = smeared_short(within[...], fields[pl.ds(1, 2)])
    second_short[...] = smeared_short(operator[:, pl.ds(0, 2 * FIELD)], grown[pl.ds(1, 2)])
    after_out[...] = operator[:, pl.ds(2 * FIELD, FIELD)]


def smear_outer(first, last, first_short, second_short, after, w_out, rims, operator):
    rims[0] = first[1, pl.ds(FIELD, PACKED_LINKS)]
    rims[1] = last[pl.ds(FIELD, PACKED_LINKS)]
    build(operator, rims, 0, (AFTER,))
    outer = last[pl.ds(0, FIELD)]
    grown = (first_short[...] + weighted_hops(operator[...], outer)).astype(bf16)
    w_out[0] = (second_short[...] + weighted_hops(after[...], grown)).astype(bf16)


def elemental_kernel(scale, vector_pieces, link_pieces, directions, *refs):
    groups = max(piece[0] for piece in vector_pieces) + 1
    packages = max(piece[0] for piece in link_pieces) + 1
    mine, theirs, refs = refs[:groups], refs[groups : 2 * groups], refs[2 * groups :]
    packages, refs = refs[:packages], refs[packages:]
    *sums, w, rims, right = refs
    core, chip = position()
    half = SITES
    at = 0
    for k, first, count in link_pieces:
        rims[pl.ds(at, count)] = packages[k][pl.ds(first, count), pl.ds(FIELD, PACKED_LINKS)]
        at += count
    for group, side in ((mine, core), (theirs, 1 - core)):
        lanes = pl.ds(pl.multiple_of(side * half, half), half)
        at = 0
        for k, first, count in vector_pieces:
            for part in range(2):
                w[pl.ds(at, count), part, :, lanes] = group[k][
                    pl.ds(first, count), :, pl.ds(part * half, half)
                ]
            at += count
    direction = directions[core]
    ahead_x, ahead_y, _, _, same = site_masks()
    one = jnp.ones((SITES, SITES), f32)
    zero = jnp.zeros((SITES, SITES), f32)
    is_x, is_y, is_z = direction == 0, direction == 1, direction == 2
    mask_x = jnp.where(ahead_x, one, zero)
    mask_y = jnp.where(ahead_y, one, zero)
    mask_z = jnp.where(same, one, zero)
    mask = jnp.where(is_x, mask_x, jnp.where(is_y, mask_y, mask_z))
    start = jnp.where(is_z, 1 - chip, 0)
    ahead = jnp.where(is_z, chip, 0)
    steps = w.shape[0] - 1

    for z in range(steps):
        table = link_planes(rims[z + start])
        lane = lax.broadcasted_iota(jnp.int32, table.shape, 1)
        count = 2 * COLORS * COLORS
        along_x = pltpu.roll(table, LY, 1)[:count]
        along_y = shift_y(table, lane)[count : 2 * count]
        along_z = table[2 * count : 3 * count]
        chosen = jnp.where(is_x, along_x, jnp.where(is_y, along_y, along_z))
        operator = jnp.concatenate(
            [
                jnp.concatenate(
                    [
                        (mask * chosen[k : k + 1]).astype(bf16)
                        for k in range(2 * COLORS * i + part, 2 * COLORS * (i + 1), 2)
                    ],
                    axis=1,
                )
                for part in range(2)
                for i in range(COLORS)
            ],
            axis=0,
        )
        source = z + ahead
        real = jnp.dot(operator, w[source, 0], preferred_element_type=f32)
        imag = jnp.dot(operator, w[source, 1], preferred_element_type=f32)
        hop_real = real[:FIELD] - imag[FIELD:]
        hop_imag = real[FIELD:] + imag[:FIELD]
        total = (hop_real + hop_imag).astype(bf16)
        rest = (hop_imag - hop_real).astype(bf16)
        vectors = 2 * half
        right[z, 0, :, pl.ds(0, vectors)] = total
        right[z, 0, :, pl.ds(vectors, vectors)] = rest
        right[z, 1, :, pl.ds(0, vectors)] = rest
        right[z, 1, :, pl.ds(vectors, vectors)] = -total
    vectors = 2 * half
    depth = steps * 2 * FIELD
    product = lax.dot_general(
        w[pl.ds(start, steps)].reshape(depth, vectors),
        right[...].reshape(depth, 2 * vectors),
        (((0,), (0,)), ((), ())),
        preferred_element_type=f32,
    )
    if scale is None:
        sums[-1][...] = product if len(sums) == 1 else product + sums[0][...]
        return
    before, out, out_low = sums
    product = product + before[...]
    packed = (product[:, :vectors] + product[:, vectors:].T) * scale
    out[...] = packed
    out_low[...] = packed.astype(bf16)


def pair_kernel(pair_scale, pairs, s00, s10, s01, s11, perambulators, elementals, out, parts, left, right):
    core, chip = position()
    index = lax.axis_index("space")
    size = s00.shape[0]
    rows = elementals.shape[3]
    own_rows = pl.ds(pl.multiple_of(index * rows, 8), rows)
    for ref, t, k in (
        (s00, chip, core),
        (s10, 1 - chip, core),
        (s01, chip, 1 - core),
        (s11, 1 - chip, 1 - core),
    ):
        packed = ref[...].astype(f32)
        turned = packed.T
        parts[t, k, 0] = 0.5 * (packed - turned)
        parts[t, k, 1] = 0.5 * (packed + turned)
    for t in range(2):
        for k in range(2):
            for part in range(2):
                elementals[t, k, part] = parts[t, k, part, own_rows]
        real, imag = parts[t, 0, 0].astype(bf16), parts[t, 0, 1].astype(bf16)
        left[t, :size, :size] = real
        left[t, :size, size:] = -imag
        left[t, size:, :size] = imag
        left[t, size:, size:] = real
        real, imag = parts[t, 1, 0].astype(bf16), parts[t, 1, 1].astype(bf16)
        right[t, :size, :size] = real
        right[t, :size, size:] = imag
        right[t, size:, :size] = -imag
        right[t, size:, size:] = real

    count = perambulators.shape[0]
    wide = []
    for p in range(count):
        propagator = perambulators[p].reshape(2 * size, size)
        first = jnp.dot(left[pairs[1, p]], propagator, preferred_element_type=f32).astype(bf16)
        wide.append(jnp.concatenate([first[:size], first[size:]], axis=1))
    both = []
    for p in range(count):
        second = jnp.dot(wide[p], right[pairs[0, p]], preferred_element_type=f32) * pair_scale
        second = second.astype(bf16)
        real, imag = second[:, :size], second[:, size:]
        both.append(jnp.concatenate([second, jnp.concatenate([imag, -real], axis=1)], axis=0))
    for p in range(count):
        turned = jnp.concatenate([perambulators[p, 0], perambulators[p, 1]], axis=1)
        third = lax.dot_general(
            both[p], turned, (((1,), (1,)), ((), ())), preferred_element_type=f32
        ).astype(bf16)
        out[p] = third.reshape(2, size, size)


def params(megabytes):
    return pltpu.CompilerParams(vmem_limit_bytes=megabytes * 1024 * 1024)


def body(eigvecs, links, directions, pairs, perambulators):
    slices = eigvecs.shape[0]
    vector_count = eigvecs.shape[5]
    n = lax.axis_size("space")
    blocks = n // 4
    vmem = whole_in_vmem()
    anywhere = pl.BlockSpec(memory_space=pl.ANY)
    smem = pl.BlockSpec(memory_space=pltpu.SMEM)
    table = jnp.transpose(links, (0, 1, 3, 4, 5, 2, 6))
    rows = FIELD + PACKED_LINKS

    def swap(value, bit):
        return lax.ppermute(value, "space", [(i, i ^ bit) for i in range(n)])

    package = jax.ShapeDtypeStruct((2, rows, vector_count), bf16)
    own, other, send = pl.pallas_call(
        split_kernel,
        out_shape=(package, package, package),
        in_specs=[vmem] * 2,
        out_specs=(vmem,) * 3,
        compiler_params=params(8),
    )(eigvecs, table)
    received = swap(send, 1)
    own, other, edge = pl.pallas_call(
        join_kernel,
        out_shape=(package, package, jax.ShapeDtypeStruct((rows, vector_count), bf16)),
        in_specs=[vmem] * 3,
        out_specs=(vmem,) * 3,
        compiler_params=params(8),
    )(received, own, other)

    crossing, straight, outer = [], [], []
    for q in range(blocks):
        above, below = (q + 1) % blocks, (q + blocks - 1) % blocks
        for core in range(2):
            a, b = 4 * q + core, 4 * q + 2 + core
            crossing += [(b, 4 * above + core), (a, 4 * below + 2 + core)]
            straight += [(b, 4 * above + 2 + core), (a, 4 * below + core)]
            outer += [(a, 4 * above + core), (b, 4 * below + 2 + core)]
    across = swap(other, 2)
    second = lax.ppermute(own, "space", straight)
    first = lax.ppermute(other, "space", crossing)
    last = lax.ppermute(edge, "space", outer)

    small = pl.CostEstimate(flops=1024, bytes_accessed=1024, transcendentals=0)

    def field(count):
        return jax.ShapeDtypeStruct((count, FIELD, vector_count), bf16)

    def scratch(*shape):
        return pltpu.VMEM(shape, bf16)

    small = pl.CostEstimate(flops=1024, bytes_accessed=1024, transcendentals=0)
    site_scale = (6.0 * n * SITES) ** (-0.5)
    square = (vector_count, vector_count)
    running = jax.ShapeDtypeStruct((vector_count, 2 * vector_count), f32)

    def elemental(scale, groups, vector_pieces, packages, link_pieces, sums):
        ranks = sum(piece[2] for piece in vector_pieces)
        outputs = (running,)
        if scale is not None:
            outputs = (jax.ShapeDtypeStruct(square, f32), jax.ShapeDtypeStruct(square, bf16))
        operands = [part[0] for part in groups] + [part[1] for part in groups] + list(packages)
        return pl.pallas_call(
            functools.partial(elemental_kernel, scale, vector_pieces, link_pieces),
            out_shape=outputs,
            in_specs=[smem] + [vmem] * (len(operands) + len(sums)),
            out_specs=(vmem,) * len(outputs),
            scratch_shapes=[
                pltpu.VMEM((ranks, 2, FIELD, vector_count), bf16),
                pltpu.VMEM((ranks, PACKED_LINKS, 2 * SITES), bf16),
                pltpu.VMEM((ranks - 1, 2, FIELD, 2 * vector_count), bf16),
            ],
            compiler_params=params(16),
            cost_estimate=small,
        )(directions, *operands, *sums)

    def with_partner(part):
        return part, swap(part, 1)

    short = jax.ShapeDtypeStruct((FIELD, vector_count), f32)
    after_shape = jax.ShapeDtypeStruct((2 * FIELD, FIELD), bf16)
    within_shape = jax.ShapeDtypeStruct((2 * FIELD, 2 * FIELD), bf16)
    w_inner, u_inner, operator = pl.pallas_call(
        smear_inner,
        out_shape=(field(2), field(2), jax.ShapeDtypeStruct((2 * FIELD, 3 * FIELD), bf16)),
        in_specs=[vmem] * 3,
        out_specs=(vmem,) * 3,
        scratch_shapes=[
            scratch(6, FIELD, vector_count),
            scratch(6, PACKED_LINKS, 2 * SITES),
            scratch(4, FIELD, vector_count),
            scratch(3, 2 * FIELD, 3 * FIELD),
        ],
        compiler_params=params(24),
        cost_estimate=small,
    )(second, across, own)
    inner = with_partner(w_inner)
    prepared = pl.pallas_call(
        smear_prepare,
        out_shape=(short, short, within_shape),
        in_specs=[vmem] * 3,
        out_specs=(vmem,) * 3,
        scratch_shapes=[scratch(2, PACKED_LINKS, 2 * SITES)],
        compiler_params=params(12),
        cost_estimate=small,
    )(own, u_inner, operator)
    (sum_inner,) = elemental(None, (inner,), ((0, 0, 2),), (across,), ((0, 0, 2),), ())
    prepared, sum_inner = lax.optimization_barrier((prepared, sum_inner))
    w_middle, first_short, second_short, after = pl.pallas_call(
        smear_middle,
        out_shape=(field(2), short, short, after_shape),
        in_specs=[vmem] * 7,
        out_specs=(vmem,) * 4,
        scratch_shapes=[
            scratch(3, FIELD, vector_count),
            scratch(3, PACKED_LINKS, 2 * SITES),
            scratch(3, FIELD, vector_count),
            scratch(2 * FIELD, 3 * FIELD),
            scratch(2 * FIELD, 2 * FIELD),
            scratch(2 * FIELD, FIELD),
        ],
        compiler_params=params(20),
        cost_estimate=small,
    )(own, first, u_inner, operator, *prepared)
    middle = with_partner(w_middle)
    w_outer = pl.pallas_call(
        smear_outer,
        out_shape=jax.ShapeDtypeStruct((1, FIELD, vector_count), bf16),
        in_specs=[vmem] * 5,
        out_specs=vmem,
        scratch_shapes=[
            pltpu.VMEM((2, PACKED_LINKS, 2 * SITES), bf16),
            pltpu.VMEM((2 * FIELD, FIELD), bf16),
        ],
        compiler_params=params(8),
        cost_estimate=small,
    )(first, last, first_short, second_short, after)
    outer_part = with_partner(w_outer)
    (sum_middle,) = elemental(
        None, (inner, middle), ((0, 1, 1), (1, 0, 2)), (across, own), ((0, 1, 1), (1, 0, 2)), (sum_inner,)
    )
    partial, partial_low = elemental(
        site_scale, (middle, outer_part), ((0, 1, 1), (1, 0, 1)), (own, first), ((0, 1, 1), (1, 0, 1)), (sum_middle,)
    )

    bit = n // 2
    while bit >= 4:
        partner = bit if bit == 4 else bit + bit // 2
        partial = partial + swap(partial_low, partner).astype(f32)
        partial_low = partial.astype(bf16)
        bit //= 2
    other_slice = swap(partial_low, 2)
    other_copy = swap(partial_low, 1)
    other_both = swap(other_slice, 1)

    pair_scale = (2.0 * vector_count) ** (-0.5)
    owned_rows = vector_count // n
    big = 2 * vector_count
    return pl.pallas_call(
        functools.partial(pair_kernel, pair_scale),
        out_shape=(
            jax.ShapeDtypeStruct((slices, 2, 2, owned_rows, vector_count), f32),
            jax.ShapeDtypeStruct(perambulators.shape, bf16),
        ),
        in_specs=[smem] + [vmem] * 5,
        out_specs=(vmem, vmem),
        scratch_shapes=[
            pltpu.VMEM((slices, 2, 2, vector_count, vector_count), f32),
            pltpu.VMEM((slices, big, big), bf16),
            pltpu.VMEM((slices, big, big), bf16),
        ],
        compiler_params=params(16),
    )(pairs.T, partial_low, other_slice, other_copy, other_both, perambulators)


def solution(mesh):
    placed = (
        P("groups", None, None, "space", None, None),
        P("groups", None, None, None, None, "space", None),
        P("groups"),
        P(("groups", "space"), None),
        P(("groups", "space"), None, None, None),
    )
    return jax.shard_map(
        body,
        mesh=mesh,
        in_specs=placed,
        out_specs=(
            P("groups", None, None, "space", None),
            P(("groups", "space"), None, None, None),
        ),
        check_vma=False,
    )
```
